32 devices in a mesh: role: 2 (over x), dp: 16 (over z, y, core).
Axes of the slice: x: 2, y: 2, z: 4, core: 2. Of those that a mesh axis runs over, the one named last changes fastest.
Arguments:
- stream: bfloat16 [32768, 767], P(('role', 'dp')), may hold values from -6 to 6
- cotangent: bfloat16 [32768, 767], P(('role', 'dp')), may hold values from -6 to 6
- w_qkv: bfloat16 [768, 2304], replicated, may hold values from -0.21875 to 0.21875
- w_out: bfloat16 [768, 768], replicated, may hold values from -0.875 to 0.875
- w_up: bfloat16 [768, 3072], replicated, may hold values from -0.21875 to 0.21875
- w_down: bfloat16 [3072, 768], replicated, may hold values from -0.15625 to 0.15625
- gain_attn: float32 [768], replicated, may hold values from 0.5 to 1.5
- gain_mlp: float32 [768], replicated, may hold values from 0.5 to 1.5
- doc_lengths: int32 [32, 4], replicated, may hold values from 0 to 1024, as said below
Outputs:
- output: bfloat16 [32768, 767], P(('role', 'dp'))
- stream_grad: bfloat16 [32768, 767], P(('role', 'dp'))
- grad_qkv: float32 [768, 2304], replicated
- grad_out: float32 [768, 768], replicated
- grad_up: float32 [768, 3072], replicated
- grad_down: float32 [3072, 768], replicated
- grad_gain_attn: float32 [768], replicated
- grad_gain_mlp: float32 [768], replicated
- rms_log: float32 [3], replicated
The draws below stay inside these ranges and needn't reach their ends.
Inputs may be any that keep to these rules, and one draw needn't show every extreme that they name: `doc_lengths`: each row sums to 512 or 1024. Its first 1, 2 or 4 entries are positive and the rest zero; with r positive entries summing to L, each is at least L // (2 * r). Some row holds a single entry equal to 1024.
All inputs are finite; a program needn't handle non-finite values.
Results may differ from the reference program's by a relative error of at most 0.025.
Values may be sent and summed in bfloat16 or wider, within the bound.
No kernel may reach another device: no remote copies, remote signals or barrier semaphores. Data moves between devices by JAX's collectives and lax.ppermute only.
A program may use at most 320 MiB of HBM per device.

```python
import jax
import jax.numpy as jnp
from jax import lax

D = 768
HEADS = 12
HEAD_DIM = 64
FF = 3072
SLOTS = 1024
ROWMAX = 4
BUCKETS = 32
TOKENS = 32768


def draw_doc_lengths(key, part):
    key = jax.random.fold_in(key, 11)
    pick_key, length_key, force_key, fill_key = jax.random.split(key, 4)
    row_level = jax.random.randint(pick_key, (BUCKETS,), 0, 3)
    forced = jax.random.randint(force_key, (), 0, BUCKETS)
    is_forced = jnp.arange(BUCKETS) == forced
    row_level = jnp.where(is_forced, 0, row_level)
    half_fill = jax.random.randint(fill_key, (BUCKETS,), 0, 2)
    live_total = jnp.where(is_forced | (half_fill == 0), SLOTS, SLOTS // 2)
    row_count = jnp.where(row_level == 0, 1, jnp.where(row_level == 1, 2, 4))
    bucket = live_total // row_count
    drawn = jax.random.randint(length_key, (BUCKETS, ROWMAX), (bucket // 2)[:, None], (bucket + 1)[:, None])
    column = jnp.arange(ROWMAX)[None, :]
    before_last = jnp.where(column < row_count[:, None] - 1, drawn, 0)
    last_value = live_total - jnp.sum(before_last, axis=1)
    result = jnp.where(column == row_count[:, None] - 1, last_value[:, None], before_last)
    return result.astype(jnp.int32)


def steps_of(key, extent, shards, smallest, high):
    gain, own = 1.0, jax.random.fold_in(key, 6)
    for axis_at, parts in shards:
        heights = jnp.exp(jax.random.uniform(jax.random.fold_in(own, axis_at), (parts,), jnp.float32, smallest / len(shards), high / len(shards)))
        gain = gain * jnp.repeat(heights, extent[axis_at] // parts).reshape([-1 if axis == axis_at else 1 for axis in range(len(extent))])
    return gain


def noise(rng, extent, width, bound, cuts=(), held_as=jnp.bfloat16):
    values = jax.random.normal(rng, extent, jnp.float32) * width
    if len(cuts) > 0:
        values = steps_of(rng, extent, cuts, -0.22, 0.18) * values
    return jnp.clip(values, min=-bound, max=bound).astype(held_as)


def setup_inputs(seed: int = 0) -> dict:
    arg_keys = jax.random.split(jax.random.key(seed), 10)
    return {
        "stream": noise(arg_keys[0], (TOKENS, D - 1), 1.0, 6.0, ((0, 32),)),
        "cotangent": noise(arg_keys[1], (TOKENS, D - 1), 1.0, 6.0, ((0, 32),)),
        "w_qkv": noise(arg_keys[2], (D, 3 * D), D ** -0.5, 0.21875),
        "w_out": noise(arg_keys[3], (D, D), (D // 16) ** -0.5, 0.875),
        "w_up": noise(arg_keys[4], (D, FF), D ** -0.5, 0.21875),
        "w_down": noise(arg_keys[5], (FF, D), (FF // 2) ** -0.5, 0.15625),
        "gain_attn": jnp.clip(1.0 + 0.1 * jax.random.normal(arg_keys[6], (D,), jnp.float32), 0.5, 1.5),
        "gain_mlp": jnp.clip(1.0 + 0.1 * jax.random.normal(arg_keys[7], (D,), jnp.float32), 0.5, 1.5),
        "doc_lengths": draw_doc_lengths(jax.random.fold_in(arg_keys[9], 71), 0),
    }


@jax.custom_vjp
def low(v):
    return lax.optimization_barrier(v.astype(jnp.bfloat16)).astype(jnp.float32)

@jax.custom_vjp
def low_back(v):
    return v

def low_keep(v):
    return (low(v), None)

def low_pass(kept, grad):
    return (grad,)

def back_keep(v):
    return (v, None)

def back_low(kept, grad):
    return (low(grad),)
low.defvjp(low_keep, low_pass)
low_back.defvjp(back_keep, back_low)
EPS = 1e-05
NEG = -1e+30

def decompress(values):
    return jnp.concatenate([values, -lax.optimization_barrier(jnp.sum(values, axis=1, keepdims=True))], axis=1)

def compress(values):
    return (values - lax.optimization_barrier(jnp.mean(values, axis=1, keepdims=True)))[:, :-1]

def normalize(values, gain_vector):
    return values * lax.rsqrt(lax.optimization_barrier(jnp.mean(values * values, axis=1, keepdims=True)) + EPS) * gain_vector

def matmul(left_side, right_side):
    return jnp.dot(left_side, right_side, precision=lax.Precision.HIGHEST, preferred_element_type=jnp.float32)

def layer(inputs, segment, w_qkv, w_out, w_up, w_down, gain_attn, gain_mlp):
    length = inputs.shape[0]
    model_width = w_out.shape[0]
    normed = low(normalize(decompress(inputs), gain_attn))
    project = low(low_back(matmul(normed, w_qkv)))
    queries = project[:, :model_width].reshape(length, HEADS, HEAD_DIM)
    key_rows = project[:, model_width:2 * model_width].reshape(length, HEADS, HEAD_DIM)
    value_rows = project[:, 2 * model_width:].reshape(length, HEADS, HEAD_DIM)
    positions = jnp.arange(length)
    allowed = (segment[:, None] == segment[None, :]) & (positions[None, :] <= positions[:, None])
    scores = jnp.einsum('qhd,khd->hqk', queries, key_rows, precision=lax.Precision.HIGHEST) * 0.125
    scores = low_back(jnp.where(allowed[None], scores, NEG))
    shifted = jnp.exp(scores - lax.optimization_barrier(jnp.max(scores, axis=2, keepdims=True)))
    weights = shifted / lax.optimization_barrier(jnp.sum(shifted, axis=2, keepdims=True))
    attended = jnp.einsum('hqk,khd->qhd', low(weights), value_rows, precision=lax.Precision.HIGHEST)
    attended = low(low_back(attended.reshape(length, model_width)))
    branch = low_back(matmul(attended, w_out))
    middle = low(low_back(inputs + compress(branch)))
    normed_mlp = low(normalize(decompress(middle), gain_mlp))
    hidden = low_back(matmul(normed_mlp, w_up))
    active = low(jax.nn.gelu(hidden, approximate=True))
    branch_mlp = low_back(matmul(active, w_down))
    return (middle + compress(branch_mlp), middle)

def energy(values, living):
    full = decompress(values)
    return jnp.sum(living * lax.optimization_barrier(jnp.sum(full * full, axis=1)))

def reference(stream, cotangent, w_qkv, w_out, w_up, w_down, gain_attn, gain_mlp, doc_lengths):
    inputs = stream.astype(jnp.float32).reshape(BUCKETS, SLOTS, D - 1)
    positions = jnp.arange(SLOTS, dtype=jnp.int32)
    cumulative = jnp.cumsum(doc_lengths, axis=1).astype(jnp.int32)
    segments = lax.optimization_barrier(jnp.sum((positions[None, :, None] >= cumulative[:, None, :]).astype(jnp.int32), axis=2))
    living = (positions[None, :] < cumulative[:, -1:]).astype(jnp.float32)

    def whole(values, wq_full, wo_full, wu_full, wd_full, ga_full, gm_full):

        def per_bucket(item):
            return jax.checkpoint(layer)(item[0], item[1], wq_full, wo_full, wu_full, wd_full, ga_full, gm_full)
        return lax.map(per_bucket, (values, segments))
    (output, middle), pullback = jax.vjp(whole, inputs, w_qkv.astype(jnp.float32), w_out.astype(jnp.float32), w_up.astype(jnp.float32), w_down.astype(jnp.float32), gain_attn.astype(jnp.float32), gain_mlp.astype(jnp.float32))
    masked_cot = living[:, :, None] * cotangent.astype(jnp.float32).reshape(BUCKETS, SLOTS, D - 1)
    grads = pullback((masked_cot, jnp.zeros_like(middle)))
    out_low = output.astype(jnp.bfloat16).reshape(TOKENS, D - 1)
    flat_live = living.reshape(TOKENS)
    count = jnp.sum(flat_live)
    sums = jnp.stack([energy(inputs.reshape(TOKENS, D - 1), flat_live), energy(middle.reshape(TOKENS, D - 1), flat_live), energy(out_low.astype(jnp.float32), flat_live)])
    rms_log = jnp.sqrt(sums / (D * count))
    return (out_low, grads[0].reshape(TOKENS, D - 1).astype(jnp.bfloat16), grads[1], grads[2], grads[3], grads[4], grads[5], grads[6], rms_log)
```

```python
import jax
import jax.numpy as jnp
from jax import lax
from jax.experimental import pallas as pl
from jax.experimental.pallas import tpu as pltpu
from jax.sharding import PartitionSpec as P

HEAD_DIM = 64
PAIR = 2 * HEAD_DIM
EPS = 1e-05
NEG = -1e30
BLOCK = 256
KINDS = 5
bf16 = jnp.bfloat16
f32 = jnp.float32
NT = (((1,), (1,)), ((), ()))
NN = (((1,), (0,)), ((), ()))
TN = (((0,), (0,)), ((), ()))


def product(left, right, dims):
    return lax.dot_general(left, right, dims, preferred_element_type=f32)


def decompress(values):
    return jnp.concatenate([values, -jnp.sum(values, axis=1, keepdims=True)], axis=1)


def compress(values):
    return (values - jnp.mean(values, axis=1, keepdims=True))[:, :-1]


def normalize(values, gain_vector):
    return values * lax.rsqrt(jnp.mean(values * values, axis=1, keepdims=True) + EPS) * gain_vector


def spread_back(grad_rows):
    full = jnp.concatenate([grad_rows, jnp.zeros_like(grad_rows[:, :1])], axis=1)
    return full - jnp.mean(full, axis=1, keepdims=True)


def squeeze_back(full_grad):
    return full_grad[:, :-1] - full_grad[:, -1:]


def energy(values, living):
    full = decompress(values)
    return jnp.sum(living * jnp.sum(full * full, axis=1))


def segments_of(lengths_row, count):
    positions = jnp.arange(count, dtype=jnp.int32)
    cumulative = jnp.cumsum(lengths_row)
    segment = jnp.sum((positions[:, None] >= cumulative[None, :]).astype(jnp.int32), axis=1)
    living = (positions < cumulative[-1]).astype(f32)
    return (segment, living)


def mask_features(segment):
    lane = jnp.arange(PAIR)[None, :]
    hot = lane == segment[:, None]
    query_side = jnp.where(hot, 1.0, 0.0).astype(bf16)
    key_side = jnp.where(
        lane < KINDS, jnp.where(hot, 0.0, NEG), jnp.where(lane < KINDS + 3, 1.0, 0.0)
    ).astype(bf16)
    return query_side, key_side


def forward_kernel(q_ref, k_ref, v_ref, fq_ref, fk_ref, o_ref, lse_ref):
    count = q_ref.shape[0]
    lane = lax.broadcasted_iota(jnp.int32, (BLOCK, PAIR), 1)
    row = lax.broadcasted_iota(jnp.int32, (BLOCK, BLOCK), 0)
    col = lax.broadcasted_iota(jnp.int32, (BLOCK, BLOCK), 1)
    causal = col <= row
    for i in range(count // BLOCK):
        here = slice(i * BLOCK, (i + 1) * BLOCK)
        past = slice(0, i * BLOCK)
        q = q_ref[here, :]
        outs, lses = [], []
        for head in range(2):
            inside = (lane < HEAD_DIM) if head == 0 else (lane >= HEAD_DIM)
            masked = jnp.where(inside, q * jnp.asarray(0.125, bf16), jnp.zeros_like(q))
            query = jnp.concatenate([masked, fq_ref[here, :]], 1)
            near = product(query, jnp.concatenate([k_ref[here, :], fk_ref[here, :]], 1), NT)
            near = jnp.where(causal, near, NEG)
            top = jnp.max(near, 1, keepdims=True)
            if i:
                far = product(query, jnp.concatenate([k_ref[past, :], fk_ref[past, :]], 1), NT)
                top = jnp.maximum(top, jnp.max(far, 1, keepdims=True))
            weights = jnp.exp(near - top)
            total = jnp.sum(weights, 1, keepdims=True)
            out = product(weights.astype(bf16), v_ref[here, :], NN)
            if i:
                weights = jnp.exp(far - top)
                total = total + jnp.sum(weights, 1, keepdims=True)
                out = out + product(weights.astype(bf16), v_ref[past, :], NN)
            outs.append(out / total)
            lses.append(top + jnp.log(total))
        o_ref[here, :] = jnp.where(lane < HEAD_DIM, outs[0], outs[1]).astype(bf16)
        lse_ref[0, here, :] = jnp.concatenate(lses, 1)


def attention_forward(project, fq, fk):
    count, width = project.shape[0], project.shape[1] // 3
    pairs = width // PAIR

    def part(at):
        return pl.BlockSpec((count, PAIR), lambda h: (0, h + at))

    same = pl.BlockSpec((count, PAIR), lambda h: (0, 0))
    return pl.pallas_call(
        forward_kernel,
        grid=(pairs,),
        in_specs=[part(0), part(pairs), part(2 * pairs), same, same],
        out_specs=[part(0), pl.BlockSpec((1, count, 2), lambda h: (h, 0, 0))],
        out_shape=[
            jax.ShapeDtypeStruct((count, width), bf16),
            jax.ShapeDtypeStruct((pairs, count, 2), f32),
        ],
        compiler_params=pltpu.CompilerParams(vmem_limit_bytes=48 * 2**20),
        name="attention_forward",
    )(project, project, project, fq, fk)


def three_parts(values):
    high = values.astype(bf16)
    rest = values - high.astype(f32)
    middle = rest.astype(bf16)
    return high, middle, (rest - middle.astype(f32)).astype(bf16)


def backward_kernel(
    q_ref, k_ref, v_ref, fq_ref, fk_ref, o_ref, do_ref, lse_ref, dq_ref, dk_ref, dv_ref, qa, da, dq
):
    count = q_ref.shape[0]
    lane = lax.broadcasted_iota(jnp.int32, (count, PAIR), 1)
    row = lax.broadcasted_iota(jnp.int32, (BLOCK, BLOCK), 0)
    col = lax.broadcasted_iota(jnp.int32, (BLOCK, BLOCK), 1)
    causal = row <= col
    q, do = q_ref[...], do_ref[...]
    both = do.astype(f32) * o_ref[...].astype(f32)
    zero = jnp.zeros_like(q)
    fq = fq_ref[...]
    for head in range(2):
        inside = (lane < HEAD_DIM) if head == 0 else (lane >= HEAD_DIM)
        qa[head, :, :PAIR] = jnp.where(inside, q * jnp.asarray(0.125, bf16), zero)
        a, b, c = three_parts(-lse_ref[0][:, head : head + 1])
        qa[head, :, PAIR:] = jnp.where(
            lane == KINDS, a, jnp.where(lane == KINDS + 1, b, jnp.where(lane == KINDS + 2, c, fq))
        )
        da[head, :, :PAIR] = jnp.where(inside, do, zero)
        a, b, c = three_parts(-jnp.sum(jnp.where(inside, both, 0.0), 1, keepdims=True))
        da[head, :, PAIR:] = jnp.where(lane == KINDS, a, jnp.where(lane == KINDS + 1, b, zero))
    dq[...] = jnp.zeros_like(dq)
    narrow = lax.broadcasted_iota(jnp.int32, (BLOCK, PAIR), 1)
    ones = jnp.where((narrow == KINDS) | (narrow == KINDS + 1), 1.0, 0.0).astype(bf16)
    for j in range(count // BLOCK):
        here = slice(j * BLOCK, (j + 1) * BLOCK)
        k = k_ref[here, :]
        ka = jnp.concatenate([k, fk_ref[here, :]], 1)
        va = jnp.concatenate([v_ref[here, :], ones], 1)
        dk = jnp.zeros((BLOCK, PAIR), f32)
        dv = jnp.zeros((BLOCK, PAIR), f32)
        for head in range(2):
            inside = (narrow < HEAD_DIM) if head == 0 else (narrow >= HEAD_DIM)
            km = jnp.where(inside, k * jnp.asarray(0.125, bf16), jnp.zeros_like(k))
            for i in range(j, count // BLOCK):
                rows = slice(i * BLOCK, (i + 1) * BLOCK)
                scores = product(ka, qa[head, rows, :], NT)
                if i == j:
                    scores = jnp.where(causal, scores, NEG)
                weights = jnp.exp(scores)
                slope = product(va, da[head, rows, :], NT)
                ds = (weights * slope).astype(bf16)
                dv += product(weights.astype(bf16), da[head, rows, :PAIR], NN)
                dk += product(ds, qa[head, rows, :PAIR], NN)
                dq[rows, :] += product(ds, km, TN)
        dk_ref[here, :] = dk.astype(bf16)
        dv_ref[here, :] = dv.astype(bf16)
    dq_ref[...] = dq[...].astype(bf16)


def attention_backward(project, fq, fk, attended, attended_grad, lse):
    count, width = attended.shape
    pairs = width // PAIR

    def part(at):
        return pl.BlockSpec((count, PAIR), lambda h: (0, h + at))

    same = pl.BlockSpec((count, PAIR), lambda h: (0, 0))
    return pl.pallas_call(
        backward_kernel,
        grid=(pairs,),
        in_specs=[
            part(0),
            part(pairs),
            part(2 * pairs),
            same,
            same,
            part(0),
            part(0),
            pl.BlockSpec((1, count, 2), lambda h: (h, 0, 0)),
        ],
        out_specs=[part(0)] * 3,
        out_shape=[jax.ShapeDtypeStruct((count, width), bf16)] * 3,
        scratch_shapes=[
            pltpu.VMEM((2, count, 2 * PAIR), bf16),
            pltpu.VMEM((2, count, 2 * PAIR), bf16),
            pltpu.VMEM((count, PAIR), f32),
        ],
        compiler_params=pltpu.CompilerParams(vmem_limit_bytes=48 * 2**20),
        name="attention_backward",
    )(project, project, project, fq, fk, attended, attended_grad, lse)


def body(stream, cotangent, w_qkv, w_out, w_up, w_down, gain_attn, gain_mlp, doc_lengths):
    slots = stream.shape[0]
    width = w_out.shape[0]
    axes = ("role", "dp")
    place = lax.axis_index("role") * lax.axis_size("dp") + lax.axis_index("dp")
    lengths = lax.dynamic_slice_in_dim(doc_lengths, place, 1, 0)[0]
    segment, living = segments_of(lengths, slots)
    fq, fk = mask_features(segment)

    inputs = stream.astype(f32)
    normed, pull_attn = jax.vjp(normalize, decompress(inputs), gain_attn)
    normed = normed.astype(bf16)
    project = product(normed, w_qkv, NN).astype(bf16)
    attended, lse = attention_forward(project, fq, fk)
    branch = product(attended, w_out, NN)
    middle = (inputs + compress(branch)).astype(bf16)

    values = middle.astype(f32)
    normed_mlp, pull_mlp = jax.vjp(normalize, decompress(values), gain_mlp)
    normed_mlp = normed_mlp.astype(bf16)
    hidden = product(normed_mlp, w_up, NN)
    active, pull_gelu = jax.vjp(lambda t: jax.nn.gelu(t, approximate=True), hidden)
    active = active.astype(bf16)
    masked_cot = living[:, None] * cotangent.astype(f32)
    branch_grad = spread_back(masked_cot).astype(bf16)
    grad_down = lax.psum(product(active, branch_grad, TN).astype(bf16), axes)
    hidden_grad = pull_gelu(product(branch_grad, w_down, NT))[0].astype(bf16)
    grad_up = lax.psum(product(normed_mlp, hidden_grad, TN).astype(bf16), axes)
    output = (values + compress(product(active, w_down, NN))).astype(bf16)
    full_grad, grad_gain_mlp = pull_mlp(product(hidden_grad, w_up, NT))
    grad_in = (masked_cot + squeeze_back(full_grad)).astype(bf16).astype(f32)

    attn_grad = spread_back(grad_in).astype(bf16)
    grad_out = product(attended, attn_grad, TN)
    attended_grad = product(attn_grad, w_out, NT).astype(bf16)
    project_grad = jnp.concatenate(
        attention_backward(project, fq, fk, attended, attended_grad, lse), axis=1
    )
    grad_qkv = product(normed, project_grad, TN)
    full_grad, grad_gain_attn = pull_attn(product(project_grad, w_qkv, NT))
    stream_grad = (grad_in + squeeze_back(full_grad)).astype(bf16)
    joined = jnp.concatenate([grad_qkv, grad_out], axis=1).astype(bf16)
    joined = lax.psum(joined, axes)
    statistics = jnp.stack(
        [
            energy(inputs, living),
            energy(values, living),
            energy(output.astype(f32), living),
            jnp.sum(living),
        ]
    )
    small = lax.psum(jnp.concatenate([grad_gain_attn, grad_gain_mlp, statistics]), axes)
    totals = small[2 * width :]
    return (
        output,
        stream_grad,
        joined[:, : 3 * width].astype(f32),
        joined[:, 3 * width :].astype(f32),
        grad_up.astype(f32),
        grad_down.astype(f32),
        small[:width],
        small[width : 2 * width],
        jnp.sqrt(totals[:3] / (width * totals[3])),
    )


def solution(mesh):
    rows = P(("role", "dp"), None)
    return jax.shard_map(
        body,
        mesh=mesh,
        in_specs=(rows, rows) + (P(),) * 7,
        out_specs=(rows, rows) + (P(),) * 7,
        check_vma=False,
    )
```

```python
import jax
import jax.numpy as jnp
from jax import lax
from jax.experimental import pallas as pl
from jax.experimental.pallas import tpu as pltpu
from jax.sharding import PartitionSpec as P

HEAD_DIM = 64
PAIR = 2 * HEAD_DIM
EPS = 1e-05
NEG = -1e30
BLOCK = 256
KINDS = 5
SHARDS = 32
STAGES = 5
SUB = 8
AXES = ("role", "dp")
bf16 = jnp.bfloat16
f32 = jnp.float32
NT = (((1,), (1,)), ((), ()))
NN = (((1,), (0,)), ((), ()))
TN = (((0,), (0,)), ((), ()))


def product(left, right, dims):
    return lax.dot_general(left, right, dims, preferred_element_type=f32)


def decompress(values):
    return jnp.concatenate([values, -jnp.sum(values, axis=1, keepdims=True)], axis=1)


def compress(values):
    return (values - jnp.mean(values, axis=1, keepdims=True))[:, :-1]


def normalize(values, gain_vector):
    return values * lax.rsqrt(jnp.mean(values * values, axis=1, keepdims=True) + EPS) * gain_vector


def spread_back(grad_rows):
    full = jnp.concatenate([grad_rows, jnp.zeros_like(grad_rows[:, :1])], axis=1)
    return full - jnp.mean(full, axis=1, keepdims=True)


def squeeze_back(full_grad):
    return full_grad[:, :-1] - full_grad[:, -1:]


def energy(values, living):
    full = decompress(values)
    return jnp.sum(living * jnp.sum(full * full, axis=1))


def segments_of(lengths_row, count):
    positions = jnp.arange(count, dtype=jnp.int32)
    cumulative = jnp.cumsum(lengths_row)
    segment = jnp.sum((positions[:, None] >= cumulative[None, :]).astype(jnp.int32), axis=1)
    living = (positions < cumulative[-1]).astype(f32)
    return (segment, living)


def mask_features(segment):
    lane = jnp.arange(PAIR)[None, :]
    hot = lane == segment[:, None]
    query_side = jnp.where(hot, 1.0, 0.0).astype(bf16)
    key_side = jnp.where(
        lane < KINDS, jnp.where(hot, 0.0, NEG), jnp.where(lane < KINDS + 3, 1.0, 0.0)
    ).astype(bf16)
    return query_side, key_side


def forward_kernel(q_ref, k_ref, v_ref, fq_ref, fk_ref, o_ref, lse_ref):
    count = q_ref.shape[0]
    lane = lax.broadcasted_iota(jnp.int32, (BLOCK, PAIR), 1)
    row = lax.broadcasted_iota(jnp.int32, (BLOCK, BLOCK), 0)
    col = lax.broadcasted_iota(jnp.int32, (BLOCK, BLOCK), 1)
    causal = col <= row
    for i in range(count // BLOCK):
        here = slice(i * BLOCK, (i + 1) * BLOCK)
        past = slice(0, i * BLOCK)
        q = q_ref[here, :]
        outs, lses = [], []
        for head in range(2):
            inside = (lane < HEAD_DIM) if head == 0 else (lane >= HEAD_DIM)
            masked = jnp.where(inside, q * jnp.asarray(0.125, bf16), jnp.zeros_like(q))
            query = jnp.concatenate([masked, fq_ref[here, :]], 1)
            near = product(query, jnp.concatenate([k_ref[here, :], fk_ref[here, :]], 1), NT)
            near = jnp.where(causal, near, NEG)
            top = jnp.max(near, 1, keepdims=True)
            if i:
                far = product(query, jnp.concatenate([k_ref[past, :], fk_ref[past, :]], 1), NT)
                top = jnp.maximum(top, jnp.max(far, 1, keepdims=True))
            weights = jnp.exp(near - top)
            total = jnp.sum(weights, 1, keepdims=True)
            out = product(weights.astype(bf16), v_ref[here, :], NN)
            if i:
                weights = jnp.exp(far - top)
                total = total + jnp.sum(weights, 1, keepdims=True)
                out = out + product(weights.astype(bf16), v_ref[past, :], NN)
            outs.append(out / total)
            lses.append(top + jnp.log(total))
        o_ref[here, :] = jnp.where(lane < HEAD_DIM, outs[0], outs[1]).astype(bf16)
        lse_ref[0, here, :] = jnp.concatenate(lses, 1)


def attention_forward(project, fq, fk):
    count, width = project.shape[0], project.shape[1] // 3
    pairs = width // PAIR

    def part(at):
        return pl.BlockSpec((count, PAIR), lambda h: (0, h + at))

    same = pl.BlockSpec((count, PAIR), lambda h: (0, 0))
    return pl.pallas_call(
        forward_kernel,
        grid=(pairs,),
        in_specs=[part(0), part(pairs), part(2 * pairs), same, same],
        out_specs=[part(0), pl.BlockSpec((1, count, 2), lambda h: (h, 0, 0))],
        out_shape=[
            jax.ShapeDtypeStruct((count, width), bf16),
            jax.ShapeDtypeStruct((pairs, count, 2), f32),
        ],
        compiler_params=pltpu.CompilerParams(vmem_limit_bytes=48 * 2**20),
        name="attention_forward",
    )(project, project, project, fq, fk)


def three_parts(values):
    high = values.astype(bf16)
    rest = values - high.astype(f32)
    middle = rest.astype(bf16)
    return high, middle, (rest - middle.astype(f32)).astype(bf16)


def backward_kernel(
    q_ref, k_ref, v_ref, fq_ref, fk_ref, o_ref, do_ref, lse_ref, dq_ref, dk_ref, dv_ref, qa, da, dq
):
    count = q_ref.shape[0]
    lane = lax.broadcasted_iota(jnp.int32, (count, PAIR), 1)
    row = lax.broadcasted_iota(jnp.int32, (BLOCK, BLOCK), 0)
    col = lax.broadcasted_iota(jnp.int32, (BLOCK, BLOCK), 1)
    causal = row <= col
    q, do = q_ref[...], do_ref[...]
    both = do.astype(f32) * o_ref[...].astype(f32)
    zero = jnp.zeros_like(q)
    fq = fq_ref[...]
    for head in range(2):
        inside = (lane < HEAD_DIM) if head == 0 else (lane >= HEAD_DIM)
        qa[head, :, :PAIR] = jnp.where(inside, q * jnp.asarray(0.125, bf16), zero)
        a, b, c = three_parts(-lse_ref[0][:, head : head + 1])
        qa[head, :, PAIR:] = jnp.where(
            lane == KINDS, a, jnp.where(lane == KINDS + 1, b, jnp.where(lane == KINDS + 2, c, fq))
        )
        da[head, :, :PAIR] = jnp.where(inside, do, zero)
        a, b, c = three_parts(-jnp.sum(jnp.where(inside, both, 0.0), 1, keepdims=True))
        da[head, :, PAIR:] = jnp.where(lane == KINDS, a, jnp.where(lane == KINDS + 1, b, zero))
    dq[...] = jnp.zeros_like(dq)
    narrow = lax.broadcasted_iota(jnp.int32, (BLOCK, PAIR), 1)
    ones = jnp.where((narrow == KINDS) | (narrow == KINDS + 1), 1.0, 0.0).astype(bf16)
    for j in range(count // BLOCK):
        here = slice(j * BLOCK, (j + 1) * BLOCK)
        k = k_ref[here, :]
        ka = jnp.concatenate([k, fk_ref[here, :]], 1)
        va = jnp.concatenate([v_ref[here, :], ones], 1)
        dk = jnp.zeros((BLOCK, PAIR), f32)
        dv = jnp.zeros((BLOCK, PAIR), f32)
        for head in range(2):
            inside = (narrow < HEAD_DIM) if head == 0 else (narrow >= HEAD_DIM)
            km = jnp.where(inside, k * jnp.asarray(0.125, bf16), jnp.zeros_like(k))
            for i in range(j, count // BLOCK):
                rows = slice(i * BLOCK, (i + 1) * BLOCK)
                scores = product(ka, qa[head, rows, :], NT)
                if i == j:
                    scores = jnp.where(causal, scores, NEG)
                weights = jnp.exp(scores)
                slope = product(va, da[head, rows, :], NT)
                ds = (weights * slope).astype(bf16)
                dv += product(weights.astype(bf16), da[head, rows, :PAIR], NN)
                dk += product(ds, qa[head, rows, :PAIR], NN)
                dq[rows, :] += product(ds, km, TN)
        dk_ref[here, :] = dk.astype(bf16)
        dv_ref[here, :] = dv.astype(bf16)
    dq_ref[...] = dq[...].astype(bf16)


def attention_backward(project, fq, fk, attended, attended_grad, lse):
    count, width = attended.shape
    pairs = width // PAIR

    def part(at):
        return pl.BlockSpec((count, PAIR), lambda h: (0, h + at))

    same = pl.BlockSpec((count, PAIR), lambda h: (0, 0))
    return pl.pallas_call(
        backward_kernel,
        grid=(pairs,),
        in_specs=[
            part(0),
            part(pairs),
            part(2 * pairs),
            same,
            same,
            part(0),
            part(0),
            pl.BlockSpec((1, count, 2), lambda h: (h, 0, 0)),
        ],
        out_specs=[part(0)] * 3,
        out_shape=[jax.ShapeDtypeStruct((count, width), bf16)] * 3,
        scratch_shapes=[
            pltpu.VMEM((2, count, 2 * PAIR), bf16),
            pltpu.VMEM((2, count, 2 * PAIR), bf16),
            pltpu.VMEM((count, PAIR), f32),
        ],
        compiler_params=pltpu.CompilerParams(vmem_limit_bytes=48 * 2**20),
        name="attention_backward",
    )(project, project, project, fq, fk, attended, attended_grad, lse)


def halving_stages(group):
    stages = [(("dp", 0), ("dp", 0)), (("role", 0), ("dp", 1)), (("dp", 1), ("role", 0))]
    return stages + [(("dp", bit), ("dp", bit)) for bit in range(2, group.bit_length() - 1)]


def route_of(stage, roles, group):
    pairs = []
    for role in range(roles):
        for place in range(group):
            axis, bit = stage[place & 1]
            other = (role ^ (1 << bit), place) if axis == "role" else (role, place ^ (1 << bit))
            pairs.append((role * group + place, other[0] * group + other[1]))
    return pairs


def codes_of(stages):
    codes = []
    for other in (0, 1):
        place = {"role": lax.axis_index("role"), "dp": lax.axis_index("dp") ^ other}
        odd = place["dp"] & 1
        code = jnp.int32(0)
        for even_way, odd_way in stages[:STAGES]:
            bits = [(place[axis] >> bit) & 1 for axis, bit in (even_way, odd_way)]
            code = code * 2 + jnp.where(odd == 0, bits[0], bits[1])
        codes.append(code)
    return jnp.stack(codes)


def panel_of(step, first, second):
    return (step & 1) ^ (jnp.where(step < 2, first, second) >> 3)


def place_rows(acc, low, out_ref):
    rows = acc.shape[0] // SUB
    for j in range(SUB):
        at = pl.multiple_of((jnp.int32(j) ^ low) * rows, rows)
        out_ref[pl.ds(at, rows), :] = acc[j * rows : (j + 1) * rows]


def weight_grad_kernel(code_ref, left_ref, right_ref, send_ref, keep_ref):
    step = pl.program_id(0)
    low = jnp.where(step < 2, code_ref[1], code_ref[0]) & (SUB - 1)
    acc = product(left_ref[...], right_ref[...], TN).astype(bf16)

    @pl.when(step < 2)
    def _():
        place_rows(acc, low, send_ref)

    @pl.when(step >= 2)
    def _():
        place_rows(acc, low, keep_ref)


def attn_weight_grad_kernel(
    code_ref, normed_ref, attended_ref, q_ref, k_ref, v_ref, o_ref, send_ref, keep_ref, acc_ref
):
    step = pl.program_id(0)
    low = jnp.where(step < 2, code_ref[1], code_ref[0]) & (SUB - 1)
    panel = panel_of(step, code_ref[1], code_ref[0])
    rights = (q_ref, k_ref, v_ref, o_ref)
    for k in range(4):

        @pl.when(panel == k)
        def _():
            left = attended_ref if k == 3 else normed_ref
            acc_ref[...] = product(left[...], rights[k][...], TN).astype(bf16)

    @pl.when(step < 2)
    def _():
        place_rows(acc_ref[...], low, send_ref)

    @pl.when(step >= 2)
    def _():
        place_rows(acc_ref[...], low, keep_ref)


def weight_grad(codes, left, right, name):
    several = isinstance(right, tuple)
    count = left.shape[0]
    width = right[0].shape[1] if several else min(left.shape[1], right.shape[1])

    def spec(array):
        if array.shape[1] > width:
            return pl.BlockSpec((count, width), lambda i, c: (0, panel_of(i, c[1], c[0])))
        return pl.BlockSpec((count, width), lambda i, c: (0, 0))

    operands = (left, *right) if several else (left, right)
    return pl.pallas_call(
        attn_weight_grad_kernel if several else weight_grad_kernel,
        grid_spec=pltpu.PrefetchScalarGridSpec(
            num_scalar_prefetch=1,
            grid=(4,),
            in_specs=[spec(array) for array in operands],
            out_specs=[
                pl.BlockSpec((width, width), lambda i, c: (jnp.minimum(i, 1), 0)),
                pl.BlockSpec((width, width), lambda i, c: (jnp.maximum(i - 2, 0), 0)),
            ],
            scratch_shapes=[pltpu.VMEM((width, width), bf16)] if several else [],
        ),
        out_shape=[jax.ShapeDtypeStruct((2 * width, width), bf16)] * 2,
        compiler_params=pltpu.CompilerParams(vmem_limit_bytes=40 * 2**20),
        cost_estimate=pl.CostEstimate(
            flops=8 * count * width * width,
            bytes_accessed=10 * count * width + 8 * width * width,
            transcendentals=0,
        ),
        name=name,
    )(codes, *operands)


def finish_kernel(code_ref, *refs):
    pieces, outs = refs[:4], refs[4:]
    step = pl.program_id(0)
    low = jnp.where(step < 2, code_ref[0], code_ref[1]) & (SUB - 1)
    panel = panel_of(step, code_ref[0], code_ref[1])
    rows = pieces[0].shape[0] // SUB

    def fill(out_ref, piece):
        for j in range(SUB):
            at = pl.multiple_of((jnp.int32(j) ^ low) * rows, rows)
            out_ref[j * rows : (j + 1) * rows, :] = piece[pl.ds(at, rows), :].astype(f32)

    for k, piece in enumerate(pieces):
        if len(outs) == 1:

            @pl.when(step == k)
            def _():
                fill(outs[0], piece)

        else:

            @pl.when((step == k) & (panel < 3))
            def _():
                fill(outs[0], piece)

            @pl.when((step == k) & (panel == 3))
            def _():
                fill(outs[1], piece)


def finish(codes, pieces, layout, name):
    width = pieces[0].shape[1]
    block = (width, width)

    def panel(i, c):
        return panel_of(i, c[0], c[1])

    if layout == "tall":
        shapes = [(4 * width, width)]
        places = [lambda i, c: (panel(i, c), 0)]
    elif layout == "wide":
        shapes = [(width, 4 * width)]
        places = [lambda i, c: (0, panel(i, c))]
    else:
        shapes = [(width, 3 * width), (width, width)]
        places = [lambda i, c: (0, jnp.minimum(panel(i, c), 2)), lambda i, c: (0, 0)]
    return pl.pallas_call(
        finish_kernel,
        grid_spec=pltpu.PrefetchScalarGridSpec(
            num_scalar_prefetch=1,
            grid=(4,),
            in_specs=[pl.BlockSpec(block, lambda i, c: (0, 0))] * 4,
            out_specs=[pl.BlockSpec(block, place) for place in places],
        ),
        out_shape=[jax.ShapeDtypeStruct(shape, f32) for shape in shapes],
        compiler_params=pltpu.CompilerParams(vmem_limit_bytes=40 * 2**20),
        cost_estimate=pl.CostEstimate(
            flops=0, bytes_accessed=24 * width * width, transcendentals=0
        ),
        name=name,
    )(codes, *pieces)


def reduce_rows(send, keep, routes):
    for route in routes[: STAGES - 1]:
        got = lax.ppermute(send, AXES, route)
        half = keep.shape[0] // 2
        keep, send = keep[:half] + got[:half], keep[half:] + got[half:]
    keep = keep + lax.ppermute(send, AXES, routes[STAGES - 1])
    for route in routes[STAGES:]:
        keep = keep + lax.ppermute(keep, AXES, route)
    return keep


def gather_rows(own, routes):
    for route in routes[STAGES - 1 : 1 : -1]:
        own = jnp.concatenate([own, lax.ppermute(own, AXES, route)], axis=0)
    far = lax.ppermute(own, AXES, routes[1])
    return own, far, lax.ppermute(own, AXES, routes[0]), lax.ppermute(far, AXES, routes[0])


def body(stream, cotangent, w_qkv, w_out, w_up, w_down, gain_attn, gain_mlp, doc_lengths):
    slots = stream.shape[0]
    width = w_out.shape[0]
    roles, group = lax.axis_size("role"), lax.axis_size("dp")
    stages = halving_stages(group)
    routes = [route_of(stage, roles, group) for stage in stages]
    codes = codes_of(stages)

    def summed(halves, layout, name):
        with jax.named_scope(name + "_sum"):
            pieces = gather_rows(reduce_rows(*halves, routes), routes)
        return finish(codes, pieces, layout, name + "_rows")

    place = lax.axis_index("role") * lax.axis_size("dp") + lax.axis_index("dp")
    lengths = lax.dynamic_slice_in_dim(doc_lengths, place, 1, 0)[0]
    segment, living = segments_of(lengths, slots)
    fq, fk = mask_features(segment)

    inputs = stream.astype(f32)
    normed, pull_attn = jax.vjp(normalize, decompress(inputs), gain_attn)
    normed = normed.astype(bf16)
    project = product(normed, w_qkv, NN).astype(bf16)
    attended, lse = attention_forward(project, fq, fk)
    branch = product(attended, w_out, NN)
    middle = (inputs + compress(branch)).astype(bf16)

    values = middle.astype(f32)
    normed_mlp, pull_mlp = jax.vjp(normalize, decompress(values), gain_mlp)
    normed_mlp = normed_mlp.astype(bf16)
    hidden = product(normed_mlp, w_up, NN)
    active, pull_gelu = jax.vjp(lambda t: jax.nn.gelu(t, approximate=True), hidden)
    active = active.astype(bf16)
    masked_cot = living[:, None] * cotangent.astype(f32)
    branch_grad = spread_back(masked_cot).astype(bf16)
    (grad_down,) = summed(weight_grad(codes, active, branch_grad, "grad_down"), "tall", "down")
    hidden_grad = pull_gelu(product(branch_grad, w_down, NT))[0].astype(bf16)
    (grad_up,) = summed(weight_grad(codes, normed_mlp, hidden_grad, "grad_up"), "wide", "up")
    output = (values + compress(product(active, w_down, NN))).astype(bf16)
    full_grad, grad_gain_mlp = pull_mlp(product(hidden_grad, w_up, NT))
    grad_in = (masked_cot + squeeze_back(full_grad)).astype(bf16).astype(f32)

    attn_grad = spread_back(grad_in).astype(bf16)
    attended_grad = product(attn_grad, w_out, NT).astype(bf16)
    parts = attention_backward(project, fq, fk, attended, attended_grad, lse)
    grad_qkv, grad_out = summed(
        weight_grad(codes, normed, (attended, *parts, attn_grad), "grad_attn"), "attn", "attn"
    )
    project_grad = jnp.concatenate(parts, axis=1)
    full_grad, grad_gain_attn = pull_attn(product(project_grad, w_qkv, NT))
    stream_grad = (grad_in + squeeze_back(full_grad)).astype(bf16)
    statistics = jnp.stack(
        [
            energy(inputs, living),
            energy(values, living),
            energy(output.astype(f32), living),
            jnp.sum(living),
        ]
    )
    small = jnp.concatenate([grad_gain_attn, grad_gain_mlp, statistics])
    small = jnp.pad(small, (0, -small.shape[0] % 1024)).reshape(-1, 128)
    for route in routes:
        small = small + lax.ppermute(small, AXES, route)
    small = small.reshape(-1)
    totals = small[2 * width : 2 * width + 4]
    return (
        output,
        stream_grad,
        grad_qkv,
        grad_out,
        grad_up,
        grad_down,
        small[:width],
        small[width : 2 * width],
        jnp.sqrt(totals[:3] / (width * totals[3])),
    )


def solution(mesh):
    rows = P(("role", "dp"), None)
    return jax.shard_map(
        body,
        mesh=mesh,
        in_specs=(rows, rows) + (P(),) * 7,
        out_specs=(rows, rows) + (P(),) * 7,
        check_vma=False,
    )
```

```python
from functools import partial

import jax
import jax.numpy as jnp
from jax import lax
from jax.experimental import pallas as pl
from jax.experimental.pallas import tpu as pltpu
from jax.sharding import PartitionSpec as P

HEAD_DIM = 64
PAIR = 2 * HEAD_DIM
EPS = 1e-05
NEG = -1e30
BLOCK = 256
KINDS = 5
ROWMAX = 4
ENDS = 2
TOTAL = ENDS + ROWMAX - 1
MIB = 2**20
SQRT_2_PI = 0.7978845608028654
SHARDS = 32
STAGES = 5
SUB = 8
AXES = ("role", "dp")
bf16 = jnp.bfloat16
f32 = jnp.float32
NT = (((1,), (1,)), ((), ()))
NN = (((1,), (0,)), ((), ()))
TN = (((0,), (0,)), ((), ()))


def far(*arrays):
    return [pltpu.with_memory_space_constraint(array, pltpu.HBM) for array in arrays]


def product(left, right, dims):
    return lax.dot_general(left, right, dims, preferred_element_type=f32)


def forward_kernel(q_ref, k_ref, v_ref, fq_ref, fk_ref, o_ref, lse_ref):
    count = q_ref.shape[0]
    lane = lax.broadcasted_iota(jnp.int32, (BLOCK, PAIR), 1)
    row = lax.broadcasted_iota(jnp.int32, (BLOCK, BLOCK), 0)
    col = lax.broadcasted_iota(jnp.int32, (BLOCK, BLOCK), 1)
    causal = col <= row
    for i in range(count // BLOCK):
        here, seen = slice(i * BLOCK, (i + 1) * BLOCK), slice(0, (i + 1) * BLOCK)
        q, feature = q_ref[here, :] * jnp.asarray(0.125, bf16), fq_ref[here, :]
        first = jnp.where(lane < HEAD_DIM, q, jnp.zeros_like(q))
        second = jnp.where(lane < HEAD_DIM, jnp.zeros_like(q), q)
        queries = jnp.concatenate(
            [jnp.concatenate([part, feature], 1) for part in (first, second)], 0
        )
        scores = product(queries, jnp.concatenate([k_ref[seen, :], fk_ref[seen, :]], 1), NT)
        tops, weights = [], []
        for head in range(2):
            part = scores[head * BLOCK : (head + 1) * BLOCK]
            near = jnp.where(causal, part[:, i * BLOCK :], NEG)
            part = jnp.concatenate([part[:, : i * BLOCK], near], 1) if i else near
            tops.append(jnp.max(part, 1, keepdims=True))
            weights.append(jnp.exp(part - tops[-1]).astype(bf16))
        ones = jnp.ones(((i + 1) * BLOCK, PAIR), bf16)
        values = jnp.concatenate([v_ref[seen, :], ones], 1)
        out = product(jnp.concatenate(weights, 0), values, NN)
        total = out[:, PAIR:]
        out = out[:, :PAIR] / total
        o_ref[here, :] = jnp.where(lane < HEAD_DIM, out[:BLOCK], out[BLOCK:]).astype(bf16)
        sums = [total[:BLOCK, :1], total[BLOCK:, :1]]
        lse_ref[0, here, :] = jnp.concatenate([t + jnp.log(l) for t, l in zip(tops, sums)], 1)


def attention_forward(project, fq, fk):
    count, width = project.shape[0], project.shape[1] // 3
    pairs = width // PAIR

    def part(at):
        return pl.BlockSpec((count, PAIR), lambda h: (0, h + at))

    same = pl.BlockSpec((count, PAIR), lambda h: (0, 0))
    return pl.pallas_call(
        forward_kernel,
        grid=(pairs,),
        in_specs=[part(0), part(pairs), part(2 * pairs), same, same],
        out_specs=[part(0), pl.BlockSpec((1, count, 2), lambda h: (h, 0, 0))],
        out_shape=[
            jax.ShapeDtypeStruct((count, width), bf16),
            jax.ShapeDtypeStruct((pairs, count, 2), f32),
        ],
        compiler_params=pltpu.CompilerParams(vmem_limit_bytes=24 * MIB),
        name="attention_forward",
    )(project, project, project, fq, fk)


def three_parts(values):
    high = values.astype(bf16)
    rest = values - high.astype(f32)
    middle = rest.astype(bf16)
    return high, middle, (rest - middle.astype(f32)).astype(bf16)


def backward_kernel(
    q_ref, k_ref, v_ref, fq_ref, fk_ref, o_ref, do_ref, lse_ref, dq_ref, dk_ref, dv_ref, qa, da, qt, dt, dq
):
    count = q_ref.shape[0]
    lane = lax.broadcasted_iota(jnp.int32, (count, PAIR), 1)
    narrow = lax.broadcasted_iota(jnp.int32, (BLOCK, PAIR), 1)
    row = lax.broadcasted_iota(jnp.int32, (BLOCK, BLOCK), 0)
    col = lax.broadcasted_iota(jnp.int32, (BLOCK, BLOCK), 1)
    causal = col <= row
    q, do, fq = q_ref[...] * jnp.asarray(0.125, bf16), do_ref[...], fq_ref[...]
    both = do.astype(f32) * o_ref[...].astype(f32)
    zero = jnp.zeros_like(q)
    qt[...] = q.T
    dt[...] = do.T
    for head in range(2):
        inside = (lane < HEAD_DIM) if head == 0 else (lane >= HEAD_DIM)
        rows = slice(head * count, (head + 1) * count)
        qa[rows, :PAIR] = jnp.where(inside, q, zero)
        a, b, c = three_parts(-lse_ref[0][:, head : head + 1])
        qa[rows, PAIR:] = jnp.where(
            lane == KINDS, a, jnp.where(lane == KINDS + 1, b, jnp.where(lane == KINDS + 2, c, fq))
        )
        da[rows, :PAIR] = jnp.where(inside, do, zero)
        a, b, c = three_parts(-jnp.sum(jnp.where(inside, both, 0.0), 1, keepdims=True))
        da[rows, PAIR:] = jnp.where(lane == KINDS, a, jnp.where(lane == KINDS + 1, b, zero))
    ones = jnp.where((narrow == KINDS) | (narrow == KINDS + 1), 1.0, 0.0).astype(bf16)
    for j in range(count // BLOCK):
        start = j * BLOCK
        here, rest = slice(start, start + BLOCK), count - start
        k = k_ref[here, :]
        keys = jnp.concatenate([k, fk_ref[here, :]], 1)
        values = jnp.concatenate([v_ref[here, :], ones], 1)
        weights, slopes = [], []
        for head in range(2):
            rows = slice(head * count + start, (head + 1) * count)
            part = jnp.exp(product(qa[rows, :], keys, NT))
            near = jnp.where(causal, part[:BLOCK], 0.0)
            part = jnp.concatenate([near, part[BLOCK:]], 0) if rest > BLOCK else near
            slopes.append((part * product(da[rows, :], values, NT)).astype(bf16))
            weights.append(part.astype(bf16))
        queries = product(jnp.concatenate(slopes, 0), k * jnp.asarray(0.125, bf16), NN)
        queries = jnp.where(lane[:rest] < HEAD_DIM, queries[:rest], queries[rest:])
        if j == 0:
            dq[...] = queries
        else:
            dq[start:, :] += queries
        heads = [slice(0, HEAD_DIM), slice(HEAD_DIM, PAIR)]
        dv = [product(dt[head, start:], part, NN) for head, part in zip(heads, weights)]
        dk = [product(qt[head, start:], part, NN) for head, part in zip(heads, slopes)]
        dv_ref[here, :] = jnp.concatenate(dv, 0).T.astype(bf16)
        dk_ref[here, :] = jnp.concatenate(dk, 0).T.astype(bf16)
    dq_ref[...] = dq[...].astype(bf16)


def attention_backward(project, fq, fk, attended, attended_grad, lse, first, pairs, earlier):
    count, width = attended.shape
    total = width // PAIR

    def part(at):
        return pl.BlockSpec((count, PAIR), lambda h: (0, h + at + first))

    same = pl.BlockSpec((count, PAIR), lambda h: (0, 0))
    operands = (project, project, project, fq, fk, attended, attended_grad, lse)
    specs = [part(0), part(total), part(2 * total), same, same, part(0), part(0)]
    specs.append(pl.BlockSpec((1, count, 2), lambda h: (h + first, 0, 0)))
    kernel, aliases = backward_kernel, {}
    if earlier is not None:
        aliases = {len(operands) + k: k for k in range(3)}
        specs += [pl.BlockSpec(memory_space=pl.ANY)] * 3
        kernel = lambda *refs: backward_kernel(*refs[: len(operands)], *refs[len(operands) + 3 :])
    return pl.pallas_call(
        kernel,
        grid=(pairs,),
        in_specs=specs,
        out_specs=[part(0)] * 3,
        out_shape=[jax.ShapeDtypeStruct((count, width), bf16)] * 3,
        scratch_shapes=[
            pltpu.VMEM((2 * count, 2 * PAIR), bf16),
            pltpu.VMEM((2 * count, 2 * PAIR), bf16),
            pltpu.VMEM((PAIR, count), bf16),
            pltpu.VMEM((PAIR, count), bf16),
            pltpu.VMEM((count, PAIR), f32),
        ],
        input_output_aliases=aliases,
        compiler_params=pltpu.CompilerParams(vmem_limit_bytes=24 * MIB),
        cost_estimate=pl.CostEstimate(
            flops=pairs * 20 * count * count * PAIR,
            bytes_accessed=pairs * 24 * count * PAIR,
            transcendentals=0,
        ),
        name="attention_backward",
    )(*operands, *(earlier or ()))


def halving_stages(group):
    stages = [(("dp", 0), ("dp", 0)), (("role", 0), ("dp", 1)), (("dp", 1), ("role", 0))]
    return stages + [(("dp", bit), ("dp", bit)) for bit in range(2, group.bit_length() - 1)]


def route_of(stage, roles, group):
    pairs = []
    for role in range(roles):
        for place in range(group):
            axis, bit = stage[place & 1]
            other = (role ^ (1 << bit), place) if axis == "role" else (role, place ^ (1 << bit))
            pairs.append((role * group + place, other[0] * group + other[1]))
    return pairs


def codes_of(stages):
    codes = []
    for other in (0, 1):
        place = {"role": lax.axis_index("role"), "dp": lax.axis_index("dp") ^ other}
        odd = place["dp"] & 1
        code = jnp.int32(0)
        for even_way, odd_way in stages[:STAGES]:
            bits = [(place[axis] >> bit) & 1 for axis, bit in (even_way, odd_way)]
            code = code * 2 + jnp.where(odd == 0, bits[0], bits[1])
        codes.append(code)
    return jnp.stack(codes)


def place_rows(acc, low, out_ref):
    rows = acc.shape[0] // SUB
    for j in range(SUB):
        at = pl.multiple_of((jnp.int32(j) ^ low) * rows, rows)
        out_ref[pl.ds(at, rows), :] = acc[j * rows : (j + 1) * rows]


def attn_weight_grad_kernel(
    half, info_ref, normed_ref, attended_ref, q_ref, k_ref, v_ref, o_ref, grad_ref, acc_ref
):
    panel = panel_in(half)(pl.program_id(0), info_ref)
    rights = (q_ref, k_ref, v_ref, o_ref)
    for k in range(4):

        @pl.when(panel == k)
        def _():
            left = attended_ref if k == 3 else normed_ref
            acc_ref[...] = product(left[...], rights[k][...], TN).astype(bf16)

    place_rows(acc_ref[...], info_ref[1 - half] & (SUB - 1), grad_ref)


def attn_weight_grad(info, half, normed, attended, rights):
    count, width = normed.shape
    whole = pl.BlockSpec((count, width), lambda i, c: (0, 0), pipeline_mode=pl.Buffered(1))
    return pl.pallas_call(
        partial(attn_weight_grad_kernel, half),
        grid_spec=pltpu.PrefetchScalarGridSpec(
            num_scalar_prefetch=1,
            grid=(2,),
            in_specs=[whole] * 6,
            out_specs=pl.BlockSpec((width, width), lambda i, c: (i, 0)),
            scratch_shapes=[pltpu.VMEM((width, width), bf16)],
        ),
        out_shape=jax.ShapeDtypeStruct((2 * width, width), bf16),
        compiler_params=pltpu.CompilerParams(vmem_limit_bytes=22 * MIB),
        cost_estimate=pl.CostEstimate(
            flops=4 * count * width * width, bytes_accessed=10 * count * width, transcendentals=0
        ),
        name="attn_weight_grad",
    )(info, normed, attended, *rights)


def finish_kernel(info_ref, *refs):
    pieces, outs = refs[:4], refs[4:]
    step = pl.program_id(0)
    code = jnp.where(step < 2, info_ref[0], info_ref[1])
    panel = (step & 1) ^ (code >> 3)
    rows = pieces[0].shape[0] // SUB

    def fill(out_ref, piece):
        for j in range(SUB):
            at = pl.multiple_of((jnp.int32(j) ^ (code & (SUB - 1))) * rows, rows)
            out_ref[j * rows : (j + 1) * rows, :] = piece[pl.ds(at, rows), :].astype(f32)

    for k, piece in enumerate(pieces):
        if len(outs) == 1:

            @pl.when(step == k)
            def _():
                fill(outs[0], piece)

        else:

            @pl.when((step == k) & (panel < 3))
            def _():
                fill(outs[0], piece)

            @pl.when((step == k) & (panel == 3))
            def _():
                fill(outs[1], piece)


def finish(info, pieces, layout, name):
    width = pieces[0].shape[1]
    block = (width, width)

    def panel(i, c):
        return (i & 1) ^ (jnp.where(i < 2, c[0], c[1]) >> 3)

    if layout == "tall":
        shapes = [(4 * width, width)]
        places = [lambda i, c: (panel(i, c), 0)]
    elif layout == "wide":
        shapes = [(width, 4 * width)]
        places = [lambda i, c: (0, panel(i, c))]
    else:
        shapes = [(width, 3 * width), (width, width)]
        places = [lambda i, c: (0, jnp.minimum(panel(i, c), 2)), lambda i, c: (0, 0)]
    return pl.pallas_call(
        finish_kernel,
        grid_spec=pltpu.PrefetchScalarGridSpec(
            num_scalar_prefetch=1,
            grid=(4,),
            in_specs=[
                pl.BlockSpec(block, lambda i, c: (0, 0), pipeline_mode=pl.Buffered(1))
            ]
            * 4,
            out_specs=[pl.BlockSpec(block, place) for place in places],
        ),
        out_shape=[jax.ShapeDtypeStruct(shape, f32) for shape in shapes],
        compiler_params=pltpu.CompilerParams(vmem_limit_bytes=24 * MIB),
        cost_estimate=pl.CostEstimate(
            flops=0, bytes_accessed=24 * width * width, transcendentals=0
        ),
        name=name,
    )(info, *far(*pieces))


class RowSum:
    def __init__(self, send, routes):
        self.send, self.keep = [send], None
        self.pieces = []
        self.steps = [("halve", route) for route in routes[: STAGES - 1]]
        self.steps += [("last", routes[STAGES - 1])]
        self.steps += [("whole", route) for route in routes[STAGES:]]
        self.steps += [("join", route) for route in routes[STAGES - 1 : 1 : -1]]
        self.steps += [("far", routes[1]), ("core", routes[0])]
        self.got = None

    def launch(self):
        self.got = [lax.ppermute(part, AXES, self.steps[0][1]) for part in self.send]

    def take(self, got):
        kind = self.steps.pop(0)[0]
        if kind == "halve":
            half = self.keep.shape[0] // 2
            self.send = [self.keep[half:] + got[0][half:]]
            self.keep = self.keep[:half] + got[0][:half]
            if self.steps[0][0] == "last":
                return
        elif kind in ("last", "whole"):
            self.keep = self.keep + got[0]
            self.send = [self.keep]
        elif kind == "join":
            self.keep = jnp.concatenate([self.keep, got[0]], axis=0)
            self.send = [self.keep]
        elif kind == "far":
            self.pieces = [self.keep, got[0]]
            self.send = list(self.pieces)
        else:
            self.pieces += got
            self.send = []


class SmallSum:
    def __init__(self, values, routes):
        self.send, self.steps = [values], list(routes)

    def launch(self):
        self.got = [lax.ppermute(part, AXES, self.steps[0]) for part in self.send]

    def take(self, got):
        self.steps.pop(0)
        self.send = [self.send[0] + got[0]]


def start(sums, after):
    after, sends = lax.optimization_barrier((after, [each.send for each in sums]))
    for each, send in zip(sums, sends):
        each.send = send
        each.launch()
    return after


def advance(taken, before, after, started=None):
    taken = [each for each in taken if each.steps]
    before, gots = lax.optimization_barrier((before, [each.got for each in taken]))
    for each, got in zip(taken, gots):
        each.take(got)
    started = taken if started is None else started
    return before, start([each for each in started if each.steps], after)


def drain(sums, token):
    while any(each.steps for each in sums):
        _, token = advance(sums, token, token)
    return token


def lanes_of(rows, width):
    return lax.broadcasted_iota(jnp.int32, (rows, width), 1)


def live_rows(info_ref, start, rows):
    place = start + lax.broadcasted_iota(jnp.int32, (rows, 1), 0)
    return place, place < info_ref[TOTAL]


def decompressed(values, lane, last):
    return jnp.where(lane == last, -jnp.sum(values, axis=1, keepdims=True), values)


def enter_kernel(
    info_ref, x_ref, cot_ref, gain_ref, w_ref, normed_ref, project_ref, bg_ref, fq_ref, fk_ref, energy_ref
):
    step = pl.program_id(0)
    rows, width = x_ref.shape
    last = width - 1
    lane = lanes_of(rows, width)
    place, live = live_rows(info_ref, step * rows, rows)
    x = jnp.where(lane < last, x_ref[...].astype(f32), 0.0)
    full = decompressed(x, lane, last)
    square = jnp.sum(full * full, axis=1, keepdims=True)
    normed = (full * lax.rsqrt(square * (1.0 / width) + EPS) * gain_ref[...]).astype(bf16)
    normed_ref[...] = normed
    project_ref[...] = product(normed, w_ref[...], NN).astype(bf16)
    cot = jnp.where((lane < last) & live, cot_ref[...].astype(f32), 0.0)
    bg_ref[...] = (cot - jnp.sum(cot, axis=1, keepdims=True) * (1.0 / width)).astype(bf16)
    segment = jnp.zeros_like(place)
    for k in range(ROWMAX):
        segment += (place >= info_ref[ENDS + k]).astype(jnp.int32)
    narrow = lanes_of(rows, PAIR)
    hot = narrow == segment
    fq_ref[...] = jnp.where(hot, 1.0, 0.0).astype(bf16)
    ones = jnp.where(narrow < KINDS + 3, 1.0, 0.0)
    fk_ref[...] = jnp.where(narrow < KINDS, jnp.where(hot, 0.0, NEG), ones).astype(bf16)

    @pl.when(step == 0)
    def _():
        energy_ref[...] = jnp.zeros_like(energy_ref)

    energy_ref[...] += jnp.sum(jnp.where(live, square, 0.0), keepdims=True)


def enter(info, stream, cotangent, gain, w_qkv):
    count, width = stream.shape[0], w_qkv.shape[0]
    rows = min(BLOCK, count)

    def some(columns):
        return pl.BlockSpec((rows, columns), lambda i, c: (i, 0))

    def whole(shape):
        return pl.BlockSpec(shape, lambda i, c: (0, 0), pipeline_mode=pl.Buffered(1))

    return pl.pallas_call(
        enter_kernel,
        grid_spec=pltpu.PrefetchScalarGridSpec(
            num_scalar_prefetch=1,
            grid=(count // rows,),
            in_specs=[some(width), some(width), whole((1, width)), whole(w_qkv.shape)],
            out_specs=[some(width), some(3 * width), some(width), some(PAIR), some(PAIR), whole((8, PAIR))],
        ),
        out_shape=[
            jax.ShapeDtypeStruct((count, width), bf16),
            jax.ShapeDtypeStruct((count, 3 * width), bf16),
            jax.ShapeDtypeStruct((count, width), bf16),
            jax.ShapeDtypeStruct((count, PAIR), bf16),
            jax.ShapeDtypeStruct((count, PAIR), bf16),
            jax.ShapeDtypeStruct((8, PAIR), f32),
        ],
        compiler_params=pltpu.CompilerParams(vmem_limit_bytes=18 * MIB),
        cost_estimate=pl.CostEstimate(
            flops=6 * count * width * width, bytes_accessed=16 * count * width, transcendentals=0
        ),
        name="enter",
    )(info, *far(stream, cotangent), gain, *far(w_qkv))


def middle_rows(info_ref, attended_ref, w_out_ref, x_ref, gain_ref, middle_ref, normed_ref, energy_ref):
    count, width = attended_ref.shape
    last = width - 1
    rows = min(BLOCK, count)
    lane = lanes_of(rows, width)
    energy_ref[...] = jnp.zeros_like(energy_ref)

    @pl.loop(0, count // rows)
    def _(block):
        start = pl.multiple_of(block * rows, rows)
        here = pl.ds(start, rows)
        branch = product(attended_ref[here, :], w_out_ref[...], NN)
        mean = jnp.sum(branch, axis=1, keepdims=True) * (1.0 / width)
        middle = (x_ref[here, :].astype(f32) + branch - mean).astype(bf16)
        middle = jnp.where(lane < last, middle, jnp.zeros_like(middle))
        middle_ref[here, :] = middle
        full = decompressed(middle.astype(f32), lane, last)
        square = jnp.sum(full * full, axis=1, keepdims=True)
        scaled = full * lax.rsqrt(square * (1.0 / width) + EPS) * gain_ref[...]
        normed_ref[here, :] = scaled.astype(bf16)
        _, live = live_rows(info_ref, start, rows)
        energy_ref[...] += jnp.sum(jnp.where(live, square, 0.0), keepdims=True)


def up_rows(normed_ref, w_up_ref, bg_ref, active_ref, slope_ref, grad_ref, low):
    count = normed_ref.shape[0]
    rows = min(BLOCK, count)
    for block in range(count // rows):
        here = slice(block * rows, (block + 1) * rows)
        hidden = product(normed_ref[here, :], w_up_ref[...], NN)
        square = hidden * hidden
        gate = 0.5 + 0.5 * jnp.tanh(hidden * (SQRT_2_PI + (SQRT_2_PI * 0.044715) * square))
        active = hidden * gate
        active_ref[here, :] = active.astype(bf16)
        inner = (1.0 - gate) * (2.0 * SQRT_2_PI + (6.0 * SQRT_2_PI * 0.044715) * square)
        slope_ref[here, :] = (gate + active * inner).astype(bf16)
    place_rows(product(active_ref[...], bg_ref[...], TN).astype(bf16), low, grad_ref)


def first_up_kernel(
    info_ref,
    attended_ref,
    w_out_ref,
    x_ref,
    gain_ref,
    w_up_ref,
    bg_ref,
    middle_ref,
    normed_ref,
    energy_ref,
    active_ref,
    slope_ref,
    grad_ref,
):
    @pl.when(pl.program_id(0) == 0)
    def _():
        middle_rows(
            info_ref, attended_ref, w_out_ref, x_ref, gain_ref, middle_ref, normed_ref, energy_ref
        )

    up_rows(normed_ref, w_up_ref, bg_ref, active_ref, slope_ref, grad_ref, info_ref[1] & (SUB - 1))


def second_up_kernel(
    info_ref, normed_ref, w_up_ref, bg_ref, _, __, active_ref, slope_ref, grad_ref
):
    up_rows(normed_ref, w_up_ref, bg_ref, active_ref, slope_ref, grad_ref, info_ref[0] & (SUB - 1))


def panel_in(half):
    return lambda i, c: i ^ (c[1 - half] >> 3)


def up_and_grad_down(info, half, attended, w_out, stream, gain, w_up, bg, first=None):
    count, width = bg.shape
    panel = panel_in(half)
    whole = pl.BlockSpec((count, width), lambda i, c: (0, 0), pipeline_mode=pl.Buffered(1))
    stays = pl.BlockSpec((count, width), lambda i, c: (0, 0))
    wide = pl.BlockSpec((count, width), lambda i, c: (0, panel(i, c)))
    w_up_spec = pl.BlockSpec((width, width), lambda i, c: (0, panel(i, c)))
    out_specs = [wide, wide, pl.BlockSpec((width, width), lambda i, c: (i, 0))]
    out_shape = [pltpu.HBM((count, 4 * width), bf16)] * 2
    out_shape += [jax.ShapeDtypeStruct((2 * width, width), bf16)]
    if half == 0:
        kernel, aliases = first_up_kernel, {}
        in_specs = [
            whole,
            pl.BlockSpec((width, width), lambda i, c: (0, 0), pipeline_mode=pl.Buffered(1)),
            whole,
            pl.BlockSpec((1, width), lambda i, c: (0, 0)),
            w_up_spec,
            whole,
        ]
        operands = (attended, *far(w_out, stream), gain, *far(w_up), bg)
        out_specs = [stays, stays, pl.BlockSpec((8, PAIR), lambda i, c: (0, 0))] + out_specs
        out_shape = [
            jax.ShapeDtypeStruct((count, width), bf16),
            jax.ShapeDtypeStruct((count, width), bf16),
            jax.ShapeDtypeStruct((8, PAIR), f32),
        ] + out_shape
    else:
        kernel, aliases = second_up_kernel, {4: 0, 5: 1}
        in_specs = [whole, w_up_spec, whole] + [pl.BlockSpec(memory_space=pl.ANY)] * 2
        operands = (attended, *far(w_up), bg, *far(*first))
    return pl.pallas_call(
        kernel,
        grid_spec=pltpu.PrefetchScalarGridSpec(
            num_scalar_prefetch=1, grid=(2,), in_specs=in_specs, out_specs=out_specs
        ),
        out_shape=out_shape,
        input_output_aliases=aliases,
        compiler_params=pltpu.CompilerParams(vmem_limit_bytes=34 * MIB),
        cost_estimate=pl.CostEstimate(
            flops=9 * count * width * width, bytes_accessed=20 * count * width, transcendentals=0
        ),
        name="up_and_grad_down",
    )(info, *operands)


def hidden_grad_kernel(half, info_ref, bg_ref, w_down_ref, slope_ref, normed_ref, *refs):
    hg_ref, grad_ref = refs[-2:]
    count = bg_ref.shape[0]
    rows = min(BLOCK, count)
    for block in range(count // rows):
        here = slice(block * rows, (block + 1) * rows)
        grad = product(bg_ref[here, :], w_down_ref[...], NT)
        hg_ref[here, :] = (grad * slope_ref[here, :].astype(f32)).astype(bf16)
    acc = product(normed_ref[...], hg_ref[...], TN).astype(bf16)
    place_rows(acc, info_ref[1 - half] & (SUB - 1), grad_ref)


def hidden_grad_and_grad_up(info, half, bg, w_down, slope, normed, first=None):
    count, width = bg.shape
    panel = panel_in(half)
    whole = pl.BlockSpec((count, width), lambda i, c: (0, 0), pipeline_mode=pl.Buffered(1))
    wide = pl.BlockSpec((count, width), lambda i, c: (0, panel(i, c)))
    in_specs = [whole, pl.BlockSpec((width, width), lambda i, c: (panel(i, c), 0)), wide, whole]
    operands = [bg, *far(w_down, slope), normed]
    if half:
        in_specs += [pl.BlockSpec(memory_space=pl.ANY)]
        operands += far(first)
    return pl.pallas_call(
        partial(hidden_grad_kernel, half),
        grid_spec=pltpu.PrefetchScalarGridSpec(
            num_scalar_prefetch=1,
            grid=(2,),
            in_specs=in_specs,
            out_specs=[wide, pl.BlockSpec((width, width), lambda i, c: (i, 0))],
        ),
        out_shape=[
            pltpu.HBM((count, 4 * width), bf16),
            jax.ShapeDtypeStruct((2 * width, width), bf16),
        ],
        input_output_aliases={5: 0} if half else {},
        compiler_params=pltpu.CompilerParams(vmem_limit_bytes=24 * MIB),
        cost_estimate=pl.CostEstimate(
            flops=8 * count * width * width, bytes_accessed=15 * count * width, transcendentals=0
        ),
        name="hidden_grad_and_grad_up",
    )(info, *operands)


def norm_back(dz, values, gain, lane, last):
    width = last + 1
    full = decompressed(values, lane, last)
    scale = lax.rsqrt(jnp.sum(full * full, axis=1, keepdims=True) * (1.0 / width) + EPS)
    normal = full * scale
    gain_rows = jnp.sum((dz * normal).reshape(dz.shape[0] // 8, 8, width), axis=0)
    pulled = gain * dz
    inner = jnp.sum(normal * pulled, axis=1, keepdims=True) * (1.0 / width)
    grad = scale * (pulled - normal * inner)
    return grad - jnp.sum(jnp.where(lane == last, grad, 0.0), axis=1, keepdims=True), gain_rows


def middle_grad_kernel(
    info_ref, hg_ref, w_up_ref, middle_ref, gain_ref, cot_ref, w_out_ref, grad_ref, bag_ref, ag_ref, gains_ref
):
    step = pl.program_id(0)
    rows, width = middle_ref.shape
    last = width - 1
    lane = lanes_of(rows, width)
    _, live = live_rows(info_ref, step * rows, rows)
    dz = product(hg_ref[...], w_up_ref[...], NT)
    pulled, gain_rows = norm_back(dz, middle_ref[...].astype(f32), gain_ref[...], lane, last)
    cot = jnp.where(live, cot_ref[...].astype(f32), 0.0)
    grad = jnp.where(lane < last, cot + pulled, 0.0).astype(bf16)
    grad_ref[...] = grad
    grad = grad.astype(f32)
    bag = (grad - jnp.sum(grad, axis=1, keepdims=True) * (1.0 / width)).astype(bf16)
    bag_ref[...] = bag
    ag_ref[...] = product(bag, w_out_ref[...], NT).astype(bf16)

    @pl.when(step == 0)
    def _():
        gains_ref[...] = jnp.zeros_like(gains_ref)

    gains_ref[...] += gain_rows


def middle_grad(info, hg, w_up, middle, gain, cotangent, w_out):
    count, width = middle.shape
    rows = min(BLOCK, count)

    def some(columns):
        return pl.BlockSpec((rows, columns), lambda i, c: (i, 0))

    def whole(shape):
        return pl.BlockSpec(shape, lambda i, c: (0, 0), pipeline_mode=pl.Buffered(1))

    return pl.pallas_call(
        middle_grad_kernel,
        grid_spec=pltpu.PrefetchScalarGridSpec(
            num_scalar_prefetch=1,
            grid=(count // rows,),
            in_specs=[
                some(hg.shape[1]),
                whole(w_up.shape),
                some(width),
                whole((1, width)),
                some(width),
                whole(w_out.shape),
            ],
            out_specs=[some(width)] * 3 + [whole((8, width))],
        ),
        out_shape=[jax.ShapeDtypeStruct((count, width), bf16)] * 3
        + [jax.ShapeDtypeStruct((8, width), f32)],
        compiler_params=pltpu.CompilerParams(vmem_limit_bytes=24 * MIB),
        cost_estimate=pl.CostEstimate(
            flops=10 * count * width * width, bytes_accessed=24 * count * width, transcendentals=0
        ),
        name="middle_grad",
    )(info, *far(hg, w_up), middle, gain, *far(cotangent, w_out))


def leave_kernel(info_ref, active_ref, w_down_ref, middle_ref, out_ref, energy_ref):
    step = pl.program_id(0)
    rows, width = middle_ref.shape
    last = width - 1
    lane = lanes_of(rows, width)
    _, live = live_rows(info_ref, step * rows, rows)
    branch = product(active_ref[...], w_down_ref[...], NN)
    mean = jnp.sum(branch, axis=1, keepdims=True) * (1.0 / width)
    out = (middle_ref[...].astype(f32) + branch - mean).astype(bf16)
    out_ref[...] = out
    values = jnp.where(lane < last, out.astype(f32), 0.0)
    full = decompressed(values, lane, last)
    square = jnp.sum(full * full, axis=1, keepdims=True)

    @pl.when(step == 0)
    def _():
        energy_ref[...] = jnp.zeros_like(energy_ref)

    energy_ref[...] += jnp.sum(jnp.where(live, square, 0.0), keepdims=True)


def leave(info, active, w_down, middle):
    count, width = middle.shape
    rows = min(BLOCK, count)

    def some(columns):
        return pl.BlockSpec((rows, columns), lambda i, c: (i, 0))

    def whole(shape):
        return pl.BlockSpec(shape, lambda i, c: (0, 0), pipeline_mode=pl.Buffered(1))

    return pl.pallas_call(
        leave_kernel,
        grid_spec=pltpu.PrefetchScalarGridSpec(
            num_scalar_prefetch=1,
            grid=(count // rows,),
            in_specs=[some(active.shape[1]), whole(w_down.shape), some(width)],
            out_specs=[some(width), whole((8, PAIR))],
        ),
        out_shape=[
            jax.ShapeDtypeStruct((count, width - 1), bf16),
            jax.ShapeDtypeStruct((8, PAIR), f32),
        ],
        compiler_params=pltpu.CompilerParams(vmem_limit_bytes=20 * MIB),
        cost_estimate=pl.CostEstimate(
            flops=8 * count * width * width, bytes_accessed=16 * count * width, transcendentals=0
        ),
        name="leave",
    )(info, *far(active, w_down), middle)


def stream_grad_kernel(
    info_ref, dq_ref, dk_ref, dv_ref, w_ref, x_ref, gain_ref, middle_grad_ref, out_ref, gains_ref
):
    step = pl.program_id(0)
    rows, width = x_ref.shape
    last = width - 1
    lane = lanes_of(rows, width)
    dz = product(dq_ref[...], w_ref[:, :width], NT)
    dz += product(dk_ref[...], w_ref[:, width : 2 * width], NT)
    dz += product(dv_ref[...], w_ref[:, 2 * width :], NT)
    x = jnp.where(lane < last, x_ref[...].astype(f32), 0.0)
    pulled, gain_rows = norm_back(dz, x, gain_ref[...], lane, last)
    out_ref[...] = (middle_grad_ref[...].astype(f32) + pulled).astype(bf16)

    @pl.when(step == 0)
    def _():
        gains_ref[...] = jnp.zeros_like(gains_ref)

    gains_ref[...] += gain_rows


def stream_gradient(info, parts, w_qkv, stream, gain, middle_grads):
    count, width = middle_grads.shape
    rows = min(BLOCK, count)

    def some(columns):
        return pl.BlockSpec((rows, columns), lambda i, c: (i, 0))

    def whole(shape):
        return pl.BlockSpec(shape, lambda i, c: (0, 0), pipeline_mode=pl.Buffered(1))

    return pl.pallas_call(
        stream_grad_kernel,
        grid_spec=pltpu.PrefetchScalarGridSpec(
            num_scalar_prefetch=1,
            grid=(count // rows,),
            in_specs=[some(width)] * 3
            + [whole(w_qkv.shape), some(width), whole((1, width)), some(width)],
            out_specs=[some(width), whole((8, width))],
        ),
        out_shape=[
            jax.ShapeDtypeStruct((count, width - 1), bf16),
            jax.ShapeDtypeStruct((8, width), f32),
        ],
        compiler_params=pltpu.CompilerParams(vmem_limit_bytes=20 * MIB),
        cost_estimate=pl.CostEstimate(
            flops=6 * count * width * width, bytes_accessed=18 * count * width, transcendentals=0
        ),
        name="stream_grad",
    )(info, *parts, *far(w_qkv, stream), gain, middle_grads)


def body(stream, cotangent, w_qkv, w_out, w_up, w_down, gain_attn, gain_mlp, doc_lengths):
    width = w_out.shape[0]
    roles, group = lax.axis_size("role"), lax.axis_size("dp")
    stages = halving_stages(group)
    routes = [route_of(stage, roles, group) for stage in stages]
    place = lax.axis_index("role") * group + lax.axis_index("dp")
    lengths = lax.dynamic_slice_in_dim(doc_lengths, place, 1, 0)[0]
    ends = jnp.cumsum(lengths)
    info = jnp.concatenate([codes_of(stages), ends]).astype(jnp.int32)
    gain_attn, gain_mlp = gain_attn[None, :], gain_mlp[None, :]

    normed, project, branch_grad, fq, fk, energy_in = enter(info, stream, cotangent, gain_attn, w_qkv)
    attended, lse = attention_forward(project, fq, fk)
    middle, normed_mlp, energy_middle, *wide, half = up_and_grad_down(
        info, 0, attended, w_out, stream, gain_mlp, w_up, branch_grad
    )
    down = RowSum(half, routes)
    normed_mlp = start([down], normed_mlp)
    active, slope, down.keep = up_and_grad_down(
        info, 1, normed_mlp, None, None, None, w_up, branch_grad, wide
    )
    slope, branch_grad = advance([down], slope, branch_grad)
    hidden_grad, half = hidden_grad_and_grad_up(info, 0, branch_grad, w_down, slope, normed_mlp)
    up = RowSum(half, routes)
    branch_grad = start([up], branch_grad)
    hidden_grad, up.keep = hidden_grad_and_grad_up(
        info, 1, branch_grad, w_down, slope, normed_mlp, hidden_grad
    )
    hidden_grad, middle = advance([down, up], hidden_grad, middle)
    middle_grads, attn_grad, attended_grad, gains_mlp = middle_grad(
        info, hidden_grad, w_up, middle, gain_mlp, cotangent, w_out
    )
    parts = None
    pairs = width // PAIR
    plan = [[], [down, up], [], [down, up], [], [down, up]]
    middle_grads, attended_grad = advance([down, up], middle_grads, attended_grad)
    for call in range(pairs):
        parts = attention_backward(
            project, fq, fk, attended, attended_grad, lse, call, 1, parts
        )
        parts, attended_grad = advance(plan[call], parts, attended_grad)
    rights = (*parts, attn_grad)
    half = attn_weight_grad(info, 0, normed, attended, rights)
    attn = RowSum(half, routes)
    normed = start([attn], normed)
    attn.keep = attn_weight_grad(info, 1, normed, attended, rights)
    _, middle_grads = advance([attn, down, up], (), middle_grads)
    stream_grad, gains_attn = stream_gradient(info, parts, w_qkv, stream, gain_attn, middle_grads)
    stream_grad, middle = advance([down, up], stream_grad, middle, [up])
    output, energy_out = leave(info, active, w_down, middle)

    energies = jnp.stack([energy_in[0, 0], energy_middle[0, 0], energy_out[0, 0]])
    small = jnp.concatenate([jnp.sum(gains_attn, 0), jnp.sum(gains_mlp, 0), energies])
    small = jnp.pad(small, (0, -small.shape[0] % 1024)).reshape(-1, PAIR)
    small = SmallSum(small, routes)
    output, token = advance([attn], output, info)
    _, token = advance([up], token, token, [small])
    rounds = [
        ([attn, small], [attn, small, down]),
        ([attn, small], [attn, small, up]),
        ([attn, small, down], [attn, small, down]),
        ([attn, up], [attn, up]),
        ([attn, small, down], [attn, small]),
        ([attn, up], [attn, up]),
    ]
    for taken, started in rounds:
        _, token = advance(taken, token, token, started)
    token = drain([down], token)
    (grad_down,) = finish(token, down.pieces, "tall", "down_rows")
    grad_down, token = advance([attn, small], grad_down, token)
    token = drain([up], token)
    (grad_up,) = finish(token, up.pieces, "wide", "up_rows")
    grad_up, token = advance([attn], grad_up, token)
    token = drain([attn, small], token)
    grad_qkv, grad_out = finish(info, attn.pieces, "attn", "attn_rows")
    small = small.send[0].reshape(-1)
    live = jnp.sum(doc_lengths).astype(f32)
    return (
        output,
        stream_grad,
        grad_qkv,
        grad_out,
        grad_up,
        grad_down,
        small[:width],
        small[width : 2 * width],
        jnp.sqrt(small[2 * width : 2 * width + 3] / (width * live)),
    )


def solution(mesh):
    rows = P(("role", "dp"), None)
    return jax.shard_map(
        body,
        mesh=mesh,
        in_specs=(rows, rows) + (P(),) * 7,
        out_specs=(rows, rows) + (P(),) * 7,
        check_vma=False,
    )
```

```python
from functools import partial

import jax
import jax.numpy as jnp
from jax import lax
from jax.experimental import pallas as pl
from jax.experimental.pallas import tpu as pltpu
from jax.sharding import PartitionSpec as P

HEAD_DIM = 64
PAIR = 2 * HEAD_DIM
EPS = 1e-05
NEG = -1e30
BLOCK = 256
KINDS = 5
ROWMAX = 4
ENDS = 2
TOTAL = ENDS + ROWMAX - 1
MIB = 2**20
SQRT_2_PI = 0.7978845608028654
SHARDS = 32
STAGES = 5
SUB = 8
AXES = ("role", "dp")
bf16 = jnp.bfloat16
f32 = jnp.float32
NT = (((1,), (1,)), ((), ()))
NN = (((1,), (0,)), ((), ()))
TN = (((0,), (0,)), ((), ()))


def far(*arrays):
    return [pltpu.with_memory_space_constraint(array, pltpu.HBM) for array in arrays]


def product(left, right, dims):
    return lax.dot_general(left, right, dims, preferred_element_type=f32)


def forward_kernel(q_ref, k_ref, v_ref, fq_ref, fk_ref, o_ref, lse_ref):
    count = q_ref.shape[0]
    lane = lax.broadcasted_iota(jnp.int32, (BLOCK, PAIR), 1)
    row = lax.broadcasted_iota(jnp.int32, (BLOCK, BLOCK), 0)
    col = lax.broadcasted_iota(jnp.int32, (BLOCK, BLOCK), 1)
    causal = col <= row
    for i in range(count // BLOCK):
        here, seen = slice(i * BLOCK, (i + 1) * BLOCK), slice(0, (i + 1) * BLOCK)
        q, feature = q_ref[here, :] * jnp.asarray(0.125, bf16), fq_ref[here, :]
        first = jnp.where(lane < HEAD_DIM, q, jnp.zeros_like(q))
        second = jnp.where(lane < HEAD_DIM, jnp.zeros_like(q), q)
        queries = jnp.concatenate(
            [jnp.concatenate([part, feature], 1) for part in (first, second)], 0
        )
        scores = product(queries, jnp.concatenate([k_ref[seen, :], fk_ref[seen, :]], 1), NT)
        tops, weights = [], []
        for head in range(2):
            part = scores[head * BLOCK : (head + 1) * BLOCK]
            near = jnp.where(causal, part[:, i * BLOCK :], NEG)
            part = jnp.concatenate([part[:, : i * BLOCK], near], 1) if i else near
            tops.append(jnp.max(part, 1, keepdims=True))
            weights.append(jnp.exp(part - tops[-1]).astype(bf16))
        ones = jnp.ones(((i + 1) * BLOCK, PAIR), bf16)
        values = jnp.concatenate([v_ref[seen, :], ones], 1)
        out = product(jnp.concatenate(weights, 0), values, NN)
        total = out[:, PAIR:]
        out = out[:, :PAIR] / total
        o_ref[here, :] = jnp.where(lane < HEAD_DIM, out[:BLOCK], out[BLOCK:]).astype(bf16)
        sums = [total[:BLOCK, :1], total[BLOCK:, :1]]
        lse_ref[0, here, :] = jnp.concatenate([t + jnp.log(l) for t, l in zip(tops, sums)], 1)


def attention_forward(project, fq, fk):
    count, width = project.shape[0], project.shape[1] // 3
    pairs = width // PAIR

    def part(at):
        return pl.BlockSpec((count, PAIR), lambda h: (0, h + at))

    same = pl.BlockSpec((count, PAIR), lambda h: (0, 0))
    return pl.pallas_call(
        forward_kernel,
        grid=(pairs,),
        in_specs=[part(0), part(pairs), part(2 * pairs), same, same],
        out_specs=[part(0), pl.BlockSpec((1, count, 2), lambda h: (h, 0, 0))],
        out_shape=[
            jax.ShapeDtypeStruct((count, width), bf16),
            jax.ShapeDtypeStruct((pairs, count, 2), f32),
        ],
        compiler_params=pltpu.CompilerParams(vmem_limit_bytes=24 * MIB),
        name="attention_forward",
    )(project, project, project, fq, fk)


def three_parts(values):
    high = values.astype(bf16)
    rest = values - high.astype(f32)
    middle = rest.astype(bf16)
    return high, middle, (rest - middle.astype(f32)).astype(bf16)


def backward_kernel(
    q_ref, k_ref, v_ref, fq_ref, fk_ref, o_ref, do_ref, lse_ref, dq_ref, dk_ref, dv_ref, qa, da, qt, dt, dq
):
    count = q_ref.shape[0]
    lane = lax.broadcasted_iota(jnp.int32, (count, PAIR), 1)
    narrow = lax.broadcasted_iota(jnp.int32, (BLOCK, PAIR), 1)
    row = lax.broadcasted_iota(jnp.int32, (BLOCK, BLOCK), 0)
    col = lax.broadcasted_iota(jnp.int32, (BLOCK, BLOCK), 1)
    causal = col <= row
    q, do, fq = q_ref[...] * jnp.asarray(0.125, bf16), do_ref[...], fq_ref[...]
    both = do.astype(f32) * o_ref[...].astype(f32)
    zero = jnp.zeros_like(q)
    qt[...] = q.T
    dt[...] = do.T
    for head in range(2):
        inside = (lane < HEAD_DIM) if head == 0 else (lane >= HEAD_DIM)
        rows = slice(head * count, (head + 1) * count)
        qa[rows, :PAIR] = jnp.where(inside, q, zero)
        a, b, c = three_parts(-lse_ref[0][:, head : head + 1])
        qa[rows, PAIR:] = jnp.where(
            lane == KINDS, a, jnp.where(lane == KINDS + 1, b, jnp.where(lane == KINDS + 2, c, fq))
        )
        da[rows, :PAIR] = jnp.where(inside, do, zero)
        a, b, c = three_parts(-jnp.sum(jnp.where(inside, both, 0.0), 1, keepdims=True))
        da[rows, PAIR:] = jnp.where(lane == KINDS, a, jnp.where(lane == KINDS + 1, b, zero))
    ones = jnp.where((narrow == KINDS) | (narrow == KINDS + 1), 1.0, 0.0).astype(bf16)
    for j in range(count // BLOCK):
        start = j * BLOCK
        here, rest = slice(start, start + BLOCK), count - start
        k = k_ref[here, :]
        keys = jnp.concatenate([k, fk_ref[here, :]], 1)
        values = jnp.concatenate([v_ref[here, :], ones], 1)
        weights, slopes = [], []
        for head in range(2):
            rows = slice(head * count + start, (head + 1) * count)
            part = jnp.exp(product(qa[rows, :], keys, NT))
            near = jnp.where(causal, part[:BLOCK], 0.0)
            part = jnp.concatenate([near, part[BLOCK:]], 0) if rest > BLOCK else near
            slopes.append((part * product(da[rows, :], values, NT)).astype(bf16))
            weights.append(part.astype(bf16))
        queries = product(jnp.concatenate(slopes, 0), k * jnp.asarray(0.125, bf16), NN)
        queries = jnp.where(lane[:rest] < HEAD_DIM, queries[:rest], queries[rest:])
        if j == 0:
            dq[...] = queries
        else:
            dq[start:, :] += queries
        heads = [slice(0, HEAD_DIM), slice(HEAD_DIM, PAIR)]
        dv = [product(dt[head, start:], part, NN) for head, part in zip(heads, weights)]
        dk = [product(qt[head, start:], part, NN) for head, part in zip(heads, slopes)]
        dv_ref[here, :] = jnp.concatenate(dv, 0).T.astype(bf16)
        dk_ref[here, :] = jnp.concatenate(dk, 0).T.astype(bf16)
    dq_ref[...] = dq[...].astype(bf16)


def attention_backward(project, fq, fk, attended, attended_grad, lse, first, pairs, earlier):
    count, width = attended.shape
    total = width // PAIR

    def part(at):
        return pl.BlockSpec((count, PAIR), lambda h: (0, h + at + first))

    same = pl.BlockSpec((count, PAIR), lambda h: (0, 0))
    operands = (project, project, project, fq, fk, attended, attended_grad, lse)
    specs = [part(0), part(total), part(2 * total), same, same, part(0), part(0)]
    specs.append(pl.BlockSpec((1, count, 2), lambda h: (h + first, 0, 0)))
    kernel, aliases = backward_kernel, {}
    if earlier is not None:
        aliases = {len(operands) + k: k for k in range(3)}
        specs += [pl.BlockSpec(memory_space=pl.ANY)] * 3
        kernel = lambda *refs: backward_kernel(*refs[: len(operands)], *refs[len(operands) + 3 :])
    return pl.pallas_call(
        kernel,
        grid=(pairs,),
        in_specs=specs,
        out_specs=[part(0)] * 3,
        out_shape=[jax.ShapeDtypeStruct((count, width), bf16)] * 3,
        scratch_shapes=[
            pltpu.VMEM((2 * count, 2 * PAIR), bf16),
            pltpu.VMEM((2 * count, 2 * PAIR), bf16),
            pltpu.VMEM((PAIR, count), bf16),
            pltpu.VMEM((PAIR, count), bf16),
            pltpu.VMEM((count, PAIR), f32),
        ],
        input_output_aliases=aliases,
        compiler_params=pltpu.CompilerParams(vmem_limit_bytes=24 * MIB),
        cost_estimate=pl.CostEstimate(
            flops=pairs * 20 * count * count * PAIR,
            bytes_accessed=pairs * 24 * count * PAIR,
            transcendentals=0,
        ),
        name="attention_backward",
    )(*operands, *(earlier or ()))


def halving_stages(group):
    stages = [(("dp", 0), ("dp", 0)), (("role", 0), ("dp", 1)), (("dp", 1), ("role", 0))]
    return stages + [(("dp", bit), ("dp", bit)) for bit in range(2, group.bit_length() - 1)]


def route_of(stage, roles, group):
    pairs = []
    for role in range(roles):
        for place in range(group):
            axis, bit = stage[place & 1]
            other = (role ^ (1 << bit), place) if axis == "role" else (role, place ^ (1 << bit))
            pairs.append((role * group + place, other[0] * group + other[1]))
    return pairs


def codes_of(stages):
    codes = []
    for other in (0, 1):
        place = {"role": lax.axis_index("role"), "dp": lax.axis_index("dp") ^ other}
        odd = place["dp"] & 1
        code = jnp.int32(0)
        for even_way, odd_way in stages[:STAGES]:
            bits = [(place[axis] >> bit) & 1 for axis, bit in (even_way, odd_way)]
            code = code * 2 + jnp.where(odd == 0, bits[0], bits[1])
        codes.append(code)
    return jnp.stack(codes)


def place_rows(acc, low, out_ref):
    rows = acc.shape[0] // SUB
    for j in range(SUB):
        at = pl.multiple_of((jnp.int32(j) ^ low) * rows, rows)
        out_ref[pl.ds(at, rows), :] = acc[j * rows : (j + 1) * rows]


def attn_weight_grad_kernel(
    half, info_ref, normed_ref, attended_ref, q_ref, k_ref, v_ref, o_ref, grad_ref, acc_ref
):
    panel = panel_in(half)(pl.program_id(0), info_ref)
    rights = (q_ref, k_ref, v_ref, o_ref)
    for k in range(4):

        @pl.when(panel == k)
        def _():
            left = attended_ref if k == 3 else normed_ref
            acc_ref[...] = product(left[...], rights[k][...], TN).astype(bf16)

    place_rows(acc_ref[...], info_ref[1 - half] & (SUB - 1), grad_ref)


def attn_weight_grad(info, half, normed, attended, rights):
    count, width = normed.shape
    whole = pl.BlockSpec((count, width), lambda i, c: (0, 0), pipeline_mode=pl.Buffered(1))
    return pl.pallas_call(
        partial(attn_weight_grad_kernel, half),
        grid_spec=pltpu.PrefetchScalarGridSpec(
            num_scalar_prefetch=1,
            grid=(2,),
            in_specs=[whole] * 6,
            out_specs=pl.BlockSpec((width, width), lambda i, c: (i, 0)),
            scratch_shapes=[pltpu.VMEM((width, width), bf16)],
        ),
        out_shape=jax.ShapeDtypeStruct((2 * width, width), bf16),
        compiler_params=pltpu.CompilerParams(vmem_limit_bytes=22 * MIB),
        cost_estimate=pl.CostEstimate(
            flops=4 * count * width * width, bytes_accessed=10 * count * width, transcendentals=0
        ),
        name="attn_weight_grad",
    )(info, normed, attended, *rights)


def finish_kernel(halves, split, info_ref, *refs):
    pieces = refs[: 2 * len(halves)]
    outs = refs[-2:] if split else refs[-1:]
    step = pl.program_id(0)
    half = halves[0] + step // 2
    code = jnp.where(half == 0, info_ref[0], info_ref[1])
    panel = (step & 1) ^ (code >> 3)
    rows = pieces[0].shape[0] // SUB

    def fill(out_ref, piece):
        for j in range(SUB):
            at = pl.multiple_of((jnp.int32(j) ^ (code & (SUB - 1))) * rows, rows)
            out_ref[j * rows : (j + 1) * rows, :] = piece[pl.ds(at, rows), :].astype(f32)

    if split and halves == (1,):

        @pl.when((step == 0) & (code >> 4 == 0))
        def _():
            outs[1][...] = refs[3][...]

    for k, piece in enumerate(pieces):
        if split:

            @pl.when((step == k) & (panel < 3))
            def _():
                fill(outs[0], piece)

            @pl.when((step == k) & (panel == 3))
            def _():
                fill(outs[1], piece)

        else:

            @pl.when(step == k)
            def _():
                fill(outs[0], piece)


def finish(info, pieces, layout, name, halves=(0, 1), earlier=()):
    width = pieces[0].shape[1]
    block = (width, width)
    split = layout == "attn"

    def panel(i, c):
        return (i & 1) ^ (jnp.where(halves[0] + i // 2 == 0, c[0], c[1]) >> 3)

    if layout == "tall":
        shapes = [(4 * width, width)]
        places = [lambda i, c: (panel(i, c), 0)]
    elif layout == "wide":
        shapes = [(width, 4 * width)]
        places = [lambda i, c: (0, panel(i, c))]
    else:
        shapes = [(width, 3 * width), (width, width)]
        places = [lambda i, c: (0, jnp.minimum(panel(i, c), 2)), lambda i, c: (0, 0)]
    whole = pl.BlockSpec(block, lambda i, c: (0, 0), pipeline_mode=pl.Buffered(1))
    in_specs = [whole] * len(pieces)
    if earlier:
        in_specs += [pl.BlockSpec(memory_space=pl.ANY), whole]
    return pl.pallas_call(
        partial(finish_kernel, halves, split),
        grid_spec=pltpu.PrefetchScalarGridSpec(
            num_scalar_prefetch=1,
            grid=(len(pieces),),
            in_specs=in_specs,
            out_specs=[pl.BlockSpec(block, place) for place in places],
        ),
        out_shape=[jax.ShapeDtypeStruct(shape, f32) for shape in shapes],
        input_output_aliases={3: 0, 4: 1} if earlier else {},
        compiler_params=pltpu.CompilerParams(vmem_limit_bytes=24 * MIB),
        cost_estimate=pl.CostEstimate(
            flops=0, bytes_accessed=6 * len(pieces) * width * width, transcendentals=0
        ),
        name=name,
    )(info, *far(*pieces), *earlier)


class RowSum:
    def __init__(self, send, routes):
        self.send, self.keep = [send], None
        self.pieces = []
        self.steps = [("halve", route) for route in routes[: STAGES - 1]]
        self.steps += [("last", routes[STAGES - 1])]
        self.steps += [("whole", route) for route in routes[STAGES:]]
        self.steps += [("join", route) for route in routes[STAGES - 1 : 1 : -1]]
        self.steps += [("far", routes[1]), ("core", routes[0])]
        self.got = None

    def launch(self):
        self.got = [lax.ppermute(part, AXES, self.steps[0][1]) for part in self.send]

    def take(self, got):
        kind = self.steps.pop(0)[0]
        if kind == "halve":
            half = self.keep.shape[0] // 2
            self.send = [self.keep[half:] + got[0][half:]]
            self.keep = self.keep[:half] + got[0][:half]
            if self.steps[0][0] == "last":
                return
        elif kind in ("last", "whole"):
            self.keep = self.keep + got[0]
            self.send = [self.keep]
        elif kind == "join":
            self.keep = jnp.concatenate([self.keep, got[0]], axis=0)
            self.send = [self.keep]
        elif kind == "far":
            self.pieces = [self.keep, got[0]]
            self.send = list(self.pieces)
        else:
            self.pieces += got
            self.send = []


class SmallSum:
    def __init__(self, values, routes):
        self.send, self.steps = [values], list(routes)

    def launch(self):
        self.got = [lax.ppermute(part, AXES, self.steps[0]) for part in self.send]

    def take(self, got):
        self.steps.pop(0)
        self.send = [self.send[0] + got[0]]


def start(sums, after):
    after, sends = lax.optimization_barrier((after, [each.send for each in sums]))
    for each, send in zip(sums, sends):
        each.send = send
        each.launch()
    return after


def advance(taken, before, after, started=None):
    taken = [each for each in taken if each.steps]
    before, gots = lax.optimization_barrier((before, [each.got for each in taken]))
    for each, got in zip(taken, gots):
        each.take(got)
    started = taken if started is None else started
    return before, start([each for each in started if each.steps], after)


def drain(sums, token):
    while any(each.steps for each in sums):
        _, token = advance(sums, token, token)
    return token


def lanes_of(rows, width):
    return lax.broadcasted_iota(jnp.int32, (rows, width), 1)


def live_rows(info_ref, start, rows):
    place = start + lax.broadcasted_iota(jnp.int32, (rows, 1), 0)
    return place, place < info_ref[TOTAL]


def decompressed(values, lane, last):
    return jnp.where(lane == last, -jnp.sum(values, axis=1, keepdims=True), values)


def enter_kernel(
    info_ref, x_ref, cot_ref, gain_ref, w_ref, normed_ref, project_ref, bg_ref, fq_ref, fk_ref, energy_ref
):
    step = pl.program_id(0)
    rows, width = x_ref.shape
    last = width - 1
    lane = lanes_of(rows, width)
    place, live = live_rows(info_ref, step * rows, rows)
    x = jnp.where(lane < last, x_ref[...].astype(f32), 0.0)
    full = decompressed(x, lane, last)
    square = jnp.sum(full * full, axis=1, keepdims=True)
    normed = (full * lax.rsqrt(square * (1.0 / width) + EPS) * gain_ref[...]).astype(bf16)
    normed_ref[...] = normed
    project_ref[...] = product(normed, w_ref[...], NN).astype(bf16)
    cot = jnp.where((lane < last) & live, cot_ref[...].astype(f32), 0.0)
    bg_ref[...] = (cot - jnp.sum(cot, axis=1, keepdims=True) * (1.0 / width)).astype(bf16)
    segment = jnp.zeros_like(place)
    for k in range(ROWMAX):
        segment += (place >= info_ref[ENDS + k]).astype(jnp.int32)
    narrow = lanes_of(rows, PAIR)
    hot = narrow == segment
    fq_ref[...] = jnp.where(hot, 1.0, 0.0).astype(bf16)
    ones = jnp.where(narrow < KINDS + 3, 1.0, 0.0)
    fk_ref[...] = jnp.where(narrow < KINDS, jnp.where(hot, 0.0, NEG), ones).astype(bf16)

    @pl.when(step == 0)
    def _():
        energy_ref[...] = jnp.zeros_like(energy_ref)

    energy_ref[...] += jnp.sum(jnp.where(live, square, 0.0), keepdims=True)


def enter(info, stream, cotangent, gain, w_qkv):
    count, width = stream.shape[0], w_qkv.shape[0]
    rows = min(BLOCK, count)

    def some(columns):
        return pl.BlockSpec((rows, columns), lambda i, c: (i, 0))

    def whole(shape):
        return pl.BlockSpec(shape, lambda i, c: (0, 0), pipeline_mode=pl.Buffered(1))

    return pl.pallas_call(
        enter_kernel,
        grid_spec=pltpu.PrefetchScalarGridSpec(
            num_scalar_prefetch=1,
            grid=(count // rows,),
            in_specs=[some(width), some(width), whole((1, width)), whole(w_qkv.shape)],
            out_specs=[some(width), some(3 * width), some(width), some(PAIR), some(PAIR), whole((8, PAIR))],
        ),
        out_shape=[
            jax.ShapeDtypeStruct((count, width), bf16),
            jax.ShapeDtypeStruct((count, 3 * width), bf16),
            jax.ShapeDtypeStruct((count, width), bf16),
            jax.ShapeDtypeStruct((count, PAIR), bf16),
            jax.ShapeDtypeStruct((count, PAIR), bf16),
            jax.ShapeDtypeStruct((8, PAIR), f32),
        ],
        compiler_params=pltpu.CompilerParams(vmem_limit_bytes=18 * MIB),
        cost_estimate=pl.CostEstimate(
            flops=6 * count * width * width, bytes_accessed=16 * count * width, transcendentals=0
        ),
        name="enter",
    )(info, *far(stream, cotangent), gain, *far(w_qkv))


def middle_rows(info_ref, attended_ref, w_out_ref, x_ref, gain_ref, middle_ref, normed_ref, energy_ref):
    count, width = attended_ref.shape
    last = width - 1
    rows = min(BLOCK, count)
    lane = lanes_of(rows, width)
    energy_ref[...] = jnp.zeros_like(energy_ref)

    @pl.loop(0, count // rows)
    def _(block):
        start = pl.multiple_of(block * rows, rows)
        here = pl.ds(start, rows)
        branch = product(attended_ref[here, :], w_out_ref[...], NN)
        mean = jnp.sum(branch, axis=1, keepdims=True) * (1.0 / width)
        middle = (x_ref[here, :].astype(f32) + branch - mean).astype(bf16)
        middle = jnp.where(lane < last, middle, jnp.zeros_like(middle))
        middle_ref[here, :] = middle
        full = decompressed(middle.astype(f32), lane, last)
        square = jnp.sum(full * full, axis=1, keepdims=True)
        scaled = full * lax.rsqrt(square * (1.0 / width) + EPS) * gain_ref[...]
        normed_ref[here, :] = scaled.astype(bf16)
        _, live = live_rows(info_ref, start, rows)
        energy_ref[...] += jnp.sum(jnp.where(live, square, 0.0), keepdims=True)


def up_rows(normed_ref, w_up_ref, bg_ref, active_ref, slope_ref, grad_ref, low):
    count = normed_ref.shape[0]
    rows = min(BLOCK, count)
    for block in range(count // rows):
        here = slice(block * rows, (block + 1) * rows)
        hidden = product(normed_ref[here, :], w_up_ref[...], NN)
        square = hidden * hidden
        gate = 0.5 + 0.5 * jnp.tanh(hidden * (SQRT_2_PI + (SQRT_2_PI * 0.044715) * square))
        active = hidden * gate
        active_ref[here, :] = active.astype(bf16)
        inner = (1.0 - gate) * (2.0 * SQRT_2_PI + (6.0 * SQRT_2_PI * 0.044715) * square)
        slope_ref[here, :] = (gate + active * inner).astype(bf16)
    place_rows(product(active_ref[...], bg_ref[...], TN).astype(bf16), low, grad_ref)


def first_up_kernel(
    info_ref,
    attended_ref,
    w_out_ref,
    x_ref,
    gain_ref,
    w_up_ref,
    bg_ref,
    middle_ref,
    normed_ref,
    energy_ref,
    active_ref,
    slope_ref,
    grad_ref,
):
    @pl.when(pl.program_id(0) == 0)
    def _():
        middle_rows(
            info_ref, attended_ref, w_out_ref, x_ref, gain_ref, middle_ref, normed_ref, energy_ref
        )

    up_rows(normed_ref, w_up_ref, bg_ref, active_ref, slope_ref, grad_ref, info_ref[1] & (SUB - 1))


def second_up_kernel(
    info_ref, normed_ref, w_up_ref, bg_ref, _, __, active_ref, slope_ref, grad_ref
):
    up_rows(normed_ref, w_up_ref, bg_ref, active_ref, slope_ref, grad_ref, info_ref[0] & (SUB - 1))


def panel_in(half):
    return lambda i, c: i ^ (c[1 - half] >> 3)


def up_and_grad_down(info, half, attended, w_out, stream, gain, w_up, bg, first=None):
    count, width = bg.shape
    panel = panel_in(half)
    whole = pl.BlockSpec((count, width), lambda i, c: (0, 0), pipeline_mode=pl.Buffered(1))
    stays = pl.BlockSpec((count, width), lambda i, c: (0, 0))
    wide = pl.BlockSpec((count, width), lambda i, c: (0, panel(i, c)))
    w_up_spec = pl.BlockSpec((width, width), lambda i, c: (0, panel(i, c)))
    out_specs = [wide, wide, pl.BlockSpec((width, width), lambda i, c: (i, 0))]
    out_shape = [pltpu.HBM((count, 4 * width), bf16)] * 2
    out_shape += [jax.ShapeDtypeStruct((2 * width, width), bf16)]
    if half == 0:
        kernel, aliases = first_up_kernel, {}
        in_specs = [
            whole,
            pl.BlockSpec((width, width), lambda i, c: (0, 0), pipeline_mode=pl.Buffered(1)),
            whole,
            pl.BlockSpec((1, width), lambda i, c: (0, 0)),
            w_up_spec,
            whole,
        ]
        operands = (attended, *far(w_out, stream), gain, *far(w_up), bg)
        out_specs = [stays, stays, pl.BlockSpec((8, PAIR), lambda i, c: (0, 0))] + out_specs
        out_shape = [
            jax.ShapeDtypeStruct((count, width), bf16),
            jax.ShapeDtypeStruct((count, width), bf16),
            jax.ShapeDtypeStruct((8, PAIR), f32),
        ] + out_shape
    else:
        kernel, aliases = second_up_kernel, {4: 0, 5: 1}
        in_specs = [whole, w_up_spec, whole] + [pl.BlockSpec(memory_space=pl.ANY)] * 2
        operands = (attended, *far(w_up), bg, *far(*first))
    return pl.pallas_call(
        kernel,
        grid_spec=pltpu.PrefetchScalarGridSpec(
            num_scalar_prefetch=1, grid=(2,), in_specs=in_specs, out_specs=out_specs
        ),
        out_shape=out_shape,
        input_output_aliases=aliases,
        compiler_params=pltpu.CompilerParams(vmem_limit_bytes=34 * MIB),
        cost_estimate=pl.CostEstimate(
            flops=9 * count * width * width, bytes_accessed=20 * count * width, transcendentals=0
        ),
        name="up_and_grad_down",
    )(info, *operands)


def hidden_grad_kernel(half, info_ref, bg_ref, w_down_ref, slope_ref, normed_ref, *refs):
    hg_ref, grad_ref = refs[-2:]
    count = bg_ref.shape[0]
    rows = min(BLOCK, count)
    for block in range(count // rows):
        here = slice(block * rows, (block + 1) * rows)
        grad = product(bg_ref[here, :], w_down_ref[...], NT)
        hg_ref[here, :] = (grad * slope_ref[here, :].astype(f32)).astype(bf16)
    acc = product(normed_ref[...], hg_ref[...], TN).astype(bf16)
    place_rows(acc, info_ref[1 - half] & (SUB - 1), grad_ref)


def hidden_grad_and_grad_up(info, half, bg, w_down, slope, normed, first=None):
    count, width = bg.shape
    panel = panel_in(half)
    whole = pl.BlockSpec((count, width), lambda i, c: (0, 0), pipeline_mode=pl.Buffered(1))
    wide = pl.BlockSpec((count, width), lambda i, c: (0, panel(i, c)))
    in_specs = [whole, pl.BlockSpec((width, width), lambda i, c: (panel(i, c), 0)), wide, whole]
    operands = [bg, *far(w_down, slope), normed]
    if half:
        in_specs += [pl.BlockSpec(memory_space=pl.ANY)]
        operands += far(first)
    return pl.pallas_call(
        partial(hidden_grad_kernel, half),
        grid_spec=pltpu.PrefetchScalarGridSpec(
            num_scalar_prefetch=1,
            grid=(2,),
            in_specs=in_specs,
            out_specs=[wide, pl.BlockSpec((width, width), lambda i, c: (i, 0))],
        ),
        out_shape=[
            pltpu.HBM((count, 4 * width), bf16),
            jax.ShapeDtypeStruct((2 * width, width), bf16),
        ],
        input_output_aliases={5: 0} if half else {},
        compiler_params=pltpu.CompilerParams(vmem_limit_bytes=24 * MIB),
        cost_estimate=pl.CostEstimate(
            flops=8 * count * width * width, bytes_accessed=15 * count * width, transcendentals=0
        ),
        name="hidden_grad_and_grad_up",
    )(info, *operands)


def norm_back(dz, values, gain, lane, last):
    width = last + 1
    full = decompressed(values, lane, last)
    scale = lax.rsqrt(jnp.sum(full * full, axis=1, keepdims=True) * (1.0 / width) + EPS)
    normal = full * scale
    gain_rows = jnp.sum((dz * normal).reshape(dz.shape[0] // 8, 8, width), axis=0)
    pulled = gain * dz
    inner = jnp.sum(normal * pulled, axis=1, keepdims=True) * (1.0 / width)
    grad = scale * (pulled - normal * inner)
    return grad - jnp.sum(jnp.where(lane == last, grad, 0.0), axis=1, keepdims=True), gain_rows


def middle_grad_kernel(
    info_ref, hg_ref, w_up_ref, middle_ref, gain_ref, cot_ref, w_out_ref, grad_ref, bag_ref, ag_ref, gains_ref
):
    step = pl.program_id(0)
    rows, width = middle_ref.shape
    last = width - 1
    lane = lanes_of(rows, width)
    _, live = live_rows(info_ref, step * rows, rows)
    dz = product(hg_ref[...], w_up_ref[...], NT)
    pulled, gain_rows = norm_back(dz, middle_ref[...].astype(f32), gain_ref[...], lane, last)
    cot = jnp.where(live, cot_ref[...].astype(f32), 0.0)
    grad = jnp.where(lane < last, cot + pulled, 0.0).astype(bf16)
    grad_ref[...] = grad
    grad = grad.astype(f32)
    bag = (grad - jnp.sum(grad, axis=1, keepdims=True) * (1.0 / width)).astype(bf16)
    bag_ref[...] = bag
    ag_ref[...] = product(bag, w_out_ref[...], NT).astype(bf16)

    @pl.when(step == 0)
    def _():
        gains_ref[...] = jnp.zeros_like(gains_ref)

    gains_ref[...] += gain_rows


def middle_grad(info, hg, w_up, middle, gain, cotangent, w_out):
    count, width = middle.shape
    rows = min(BLOCK, count)

    def some(columns):
        return pl.BlockSpec((rows, columns), lambda i, c: (i, 0))

    def whole(shape):
        return pl.BlockSpec(shape, lambda i, c: (0, 0), pipeline_mode=pl.Buffered(1))

    return pl.pallas_call(
        middle_grad_kernel,
        grid_spec=pltpu.PrefetchScalarGridSpec(
            num_scalar_prefetch=1,
            grid=(count // rows,),
            in_specs=[
                some(hg.shape[1]),
                whole(w_up.shape),
                some(width),
                whole((1, width)),
                some(width),
                whole(w_out.shape),
            ],
            out_specs=[some(width)] * 3 + [whole((8, width))],
        ),
        out_shape=[jax.ShapeDtypeStruct((count, width), bf16)] * 3
        + [jax.ShapeDtypeStruct((8, width), f32)],
        compiler_params=pltpu.CompilerParams(vmem_limit_bytes=24 * MIB),
        cost_estimate=pl.CostEstimate(
            flops=10 * count * width * width, bytes_accessed=24 * count * width, transcendentals=0
        ),
        name="middle_grad",
    )(info, *far(hg, w_up), middle, gain, *far(cotangent, w_out))


def leave_kernel(first, info_ref, active_ref, w_down_ref, middle_ref, *refs):
    out_ref, energy_ref = refs[-2:]
    step = pl.program_id(0)
    rows, width = middle_ref.shape
    last = width - 1
    lane = lanes_of(rows, width)
    _, live = live_rows(info_ref, (first + step) * rows, rows)
    branch = product(active_ref[...], w_down_ref[...], NN)
    mean = jnp.sum(branch, axis=1, keepdims=True) * (1.0 / width)
    out = (middle_ref[...].astype(f32) + branch - mean).astype(bf16)
    out_ref[...] = out
    values = jnp.where(lane < last, out.astype(f32), 0.0)
    full = decompressed(values, lane, last)
    square = jnp.sum(full * full, axis=1, keepdims=True)

    @pl.when(step == 0)
    def _():
        energy_ref[...] = jnp.zeros_like(energy_ref)

    energy_ref[...] += jnp.sum(jnp.where(live, square, 0.0), keepdims=True)


def leave(info, active, w_down, middle, part, parts, earlier=None):
    count, width = middle.shape
    rows = min(BLOCK, count // parts)
    steps = count // parts // rows
    first = part * steps

    def some(columns):
        return pl.BlockSpec((rows, columns), lambda i, c: (i + first, 0))

    def whole(shape):
        return pl.BlockSpec(shape, lambda i, c: (0, 0), pipeline_mode=pl.Buffered(1))

    in_specs = [some(active.shape[1]), whole(w_down.shape), some(width)]
    operands = [*far(active, w_down), middle]
    if part:
        in_specs += [pl.BlockSpec(memory_space=pl.ANY)]
        operands += [earlier]
    return pl.pallas_call(
        partial(leave_kernel, first),
        grid_spec=pltpu.PrefetchScalarGridSpec(
            num_scalar_prefetch=1,
            grid=(steps,),
            in_specs=in_specs,
            out_specs=[some(width), pl.BlockSpec((8, PAIR), lambda i, c: (0, 0))],
        ),
        out_shape=[
            jax.ShapeDtypeStruct((count, width - 1), bf16),
            jax.ShapeDtypeStruct((8, PAIR), f32),
        ],
        input_output_aliases={4: 0} if part else {},
        compiler_params=pltpu.CompilerParams(vmem_limit_bytes=20 * MIB),
        cost_estimate=pl.CostEstimate(
            flops=8 * count * width * width // parts,
            bytes_accessed=16 * count * width // parts,
            transcendentals=0,
        ),
        name="leave",
    )(info, *operands)


def stream_grad_kernel(
    info_ref, dq_ref, dk_ref, dv_ref, w_ref, x_ref, gain_ref, middle_grad_ref, out_ref, gains_ref
):
    step = pl.program_id(0)
    rows, width = x_ref.shape
    last = width - 1
    lane = lanes_of(rows, width)
    dz = product(dq_ref[...], w_ref[:, :width], NT)
    dz += product(dk_ref[...], w_ref[:, width : 2 * width], NT)
    dz += product(dv_ref[...], w_ref[:, 2 * width :], NT)
    x = jnp.where(lane < last, x_ref[...].astype(f32), 0.0)
    pulled, gain_rows = norm_back(dz, x, gain_ref[...], lane, last)
    out_ref[...] = (middle_grad_ref[...].astype(f32) + pulled).astype(bf16)

    @pl.when(step == 0)
    def _():
        gains_ref[...] = jnp.zeros_like(gains_ref)

    gains_ref[...] += gain_rows


def stream_gradient(info, parts, w_qkv, stream, gain, middle_grads):
    count, width = middle_grads.shape
    rows = min(BLOCK, count)

    def some(columns):
        return pl.BlockSpec((rows, columns), lambda i, c: (i, 0))

    def whole(shape):
        return pl.BlockSpec(shape, lambda i, c: (0, 0), pipeline_mode=pl.Buffered(1))

    return pl.pallas_call(
        stream_grad_kernel,
        grid_spec=pltpu.PrefetchScalarGridSpec(
            num_scalar_prefetch=1,
            grid=(count // rows,),
            in_specs=[some(width)] * 3
            + [whole(w_qkv.shape), some(width), whole((1, width)), some(width)],
            out_specs=[some(width), whole((8, width))],
        ),
        out_shape=[
            jax.ShapeDtypeStruct((count, width - 1), bf16),
            jax.ShapeDtypeStruct((8, width), f32),
        ],
        compiler_params=pltpu.CompilerParams(vmem_limit_bytes=20 * MIB),
        cost_estimate=pl.CostEstimate(
            flops=6 * count * width * width, bytes_accessed=18 * count * width, transcendentals=0
        ),
        name="stream_grad",
    )(info, *parts, *far(w_qkv, stream), gain, middle_grads)


def body(stream, cotangent, w_qkv, w_out, w_up, w_down, gain_attn, gain_mlp, doc_lengths):
    width = w_out.shape[0]
    roles, group = lax.axis_size("role"), lax.axis_size("dp")
    stages = halving_stages(group)
    routes = [route_of(stage, roles, group) for stage in stages]
    place = lax.axis_index("role") * group + lax.axis_index("dp")
    lengths = lax.dynamic_slice_in_dim(doc_lengths, place, 1, 0)[0]
    ends = jnp.cumsum(lengths)
    info = jnp.concatenate([codes_of(stages), ends]).astype(jnp.int32)
    gain_attn, gain_mlp = gain_attn[None, :], gain_mlp[None, :]

    normed, project, branch_grad, fq, fk, energy_in = enter(info, stream, cotangent, gain_attn, w_qkv)
    attended, lse = attention_forward(project, fq, fk)
    middle, normed_mlp, energy_middle, *wide, half = up_and_grad_down(
        info, 0, attended, w_out, stream, gain_mlp, w_up, branch_grad
    )
    down = RowSum(half, routes)
    normed_mlp = start([down], normed_mlp)
    active, slope, down.keep = up_and_grad_down(
        info, 1, normed_mlp, None, None, None, w_up, branch_grad, wide
    )
    slope, branch_grad = advance([down], slope, branch_grad)
    hidden_grad, half = hidden_grad_and_grad_up(info, 0, branch_grad, w_down, slope, normed_mlp)
    up = RowSum(half, routes)
    branch_grad = start([up], branch_grad)
    hidden_grad, up.keep = hidden_grad_and_grad_up(
        info, 1, branch_grad, w_down, slope, normed_mlp, hidden_grad
    )
    hidden_grad, middle = advance([down, up], hidden_grad, middle)
    middle_grads, attn_grad, attended_grad, gains_mlp = middle_grad(
        info, hidden_grad, w_up, middle, gain_mlp, cotangent, w_out
    )
    parts = None
    pairs = width // PAIR
    plan = [[], [], [down, up], [], [], [down, up]]
    middle_grads, attended_grad = advance([down, up], middle_grads, attended_grad)
    for call in range(pairs):
        parts = attention_backward(
            project, fq, fk, attended, attended_grad, lse, call, 1, parts
        )
        parts, attended_grad = advance(plan[call], parts, attended_grad)
    rights = (*parts, attn_grad)
    half = attn_weight_grad(info, 0, normed, attended, rights)
    attn = RowSum(half, routes)
    normed = start([attn], normed)
    attn.keep = attn_weight_grad(info, 1, normed, attended, rights)
    _, middle_grads = advance([attn], (), middle_grads)
    stream_grad, gains_attn = stream_gradient(info, parts, w_qkv, stream, gain_attn, middle_grads)
    stream_grad, token = advance([down, up], stream_grad, info)
    _, middle = advance([attn], token, middle)
    output, energy_first = leave(info, active, w_down, middle, 0, 2)
    output, token = advance([down, up], output, token)
    _, output = advance([attn], token, output)
    output, energy_second = leave(info, active, w_down, middle, 1, 2, output)

    energies = jnp.stack(
        [energy_in[0, 0], energy_middle[0, 0], energy_first[0, 0] + energy_second[0, 0]]
    )
    small = jnp.concatenate([jnp.sum(gains_attn, 0), jnp.sum(gains_mlp, 0), energies])
    small = jnp.pad(small, (0, -small.shape[0] % 1024)).reshape(-1, PAIR)
    small = SmallSum(small, routes)
    output, token = advance([down], output, token)
    _, token = advance([attn], token, token, [attn, small])
    _, token = advance([up, small], token, token)
    _, token = advance([attn], token, token)
    _, token = advance([down, up, small], token, token)
    _, token = advance([attn], token, token)
    _, token = advance([down, small], token, token)
    _, token = advance([attn], token, token)
    token = drain([down], token)
    (grad_down,) = finish(token, down.pieces, "tall", "down_rows")
    grad_down, token = advance([up, small], grad_down, token)
    _, token = advance([attn], token, token)
    token = drain([up, small], token)
    (grad_up,) = finish(token, up.pieces, "wide", "up_rows")
    grad_up, token = advance([attn], grad_up, token)
    while len(attn.pieces) < 2:
        _, token = advance([attn], token, token)
    attn_rows = finish(token, attn.pieces, "attn", "attn_rows", (0,))
    attn_rows, token = advance([attn], attn_rows, token)
    grad_qkv, grad_out = finish(token, attn.pieces[2:], "attn", "attn_rows", (1,), attn_rows)
    small = small.send[0].reshape(-1)
    live = jnp.sum(doc_lengths).astype(f32)
    return (
        output,
        stream_grad,
        grad_qkv,
        grad_out,
        grad_up,
        grad_down,
        small[:width],
        small[width : 2 * width],
        jnp.sqrt(small[2 * width : 2 * width + 3] / (width * live)),
    )


def solution(mesh):
    rows = P(("role", "dp"), None)
    return jax.shard_map(
        body,
        mesh=mesh,
        in_specs=(rows, rows) + (P(),) * 7,
        out_specs=(rows, rows) + (P(),) * 7,
        check_vma=False,
    )
```

```python
from functools import partial

import jax
import jax.numpy as jnp
from jax import lax
from jax.experimental import pallas as pl
from jax.experimental.pallas import tpu as pltpu
from jax.sharding import PartitionSpec as P

HEAD_DIM = 64
PAIR = 2 * HEAD_DIM
EPS = 1e-05
NEG = -1e30
BLOCK = 256
KINDS = 5
ROWMAX = 4
ENDS = 2
TOTAL = ENDS + ROWMAX - 1
MIB = 2**20
SHORT = pl.CostEstimate(flops=10**6, bytes_accessed=10**5, transcendentals=0)
SQRT_2_PI = 0.7978845608028654
STAGES, ATTN_STAGES = 5, 5
SUB, ATTN_SUB = 8, 8
LOW = 3
AXES = ("role", "dp")
bf16 = jnp.bfloat16
f32 = jnp.float32
NT = (((1,), (1,)), ((), ()))
NN = (((1,), (0,)), ((), ()))
TN = (((0,), (0,)), ((), ()))


def far(*arrays):
    return [pltpu.with_memory_space_constraint(array, pltpu.HBM) for array in arrays]


def product(left, right, dims):
    return lax.dot_general(left, right, dims, preferred_element_type=f32)


def forward_kernel(q_ref, k_ref, v_ref, fq_ref, fk_ref, o_ref, lse_ref):
    count = q_ref.shape[0]
    lane = lax.broadcasted_iota(jnp.int32, (BLOCK, PAIR), 1)
    row = lax.broadcasted_iota(jnp.int32, (BLOCK, BLOCK), 0)
    col = lax.broadcasted_iota(jnp.int32, (BLOCK, BLOCK), 1)
    causal = col <= row

    def scores_of(i):
        here, seen = slice(i * BLOCK, (i + 1) * BLOCK), slice(0, (i + 1) * BLOCK)
        q, feature = q_ref[here, :] * jnp.asarray(0.125, bf16), fq_ref[here, :]
        first = jnp.where(lane < HEAD_DIM, q, jnp.zeros_like(q))
        second = jnp.where(lane < HEAD_DIM, jnp.zeros_like(q), q)
        queries = jnp.concatenate(
            [jnp.concatenate([part, feature], 1) for part in (first, second)], 0
        )
        return product(queries, jnp.concatenate([k_ref[seen, :], fk_ref[seen, :]], 1), NT)

    def attend(i, scores):
        here, seen = slice(i * BLOCK, (i + 1) * BLOCK), slice(0, (i + 1) * BLOCK)
        tops, weights = [], []
        for head in range(2):
            part = scores[head * BLOCK : (head + 1) * BLOCK]
            near = jnp.where(causal, part[:, i * BLOCK :], NEG)
            part = jnp.concatenate([part[:, : i * BLOCK], near], 1) if i else near
            tops.append(jnp.max(part, 1, keepdims=True))
            weights.append(jnp.exp(part - tops[-1]).astype(bf16))
        ones = jnp.ones(((i + 1) * BLOCK, PAIR), bf16)
        values = jnp.concatenate([v_ref[seen, :], ones], 1)
        out = product(jnp.concatenate(weights, 0), values, NN)
        total = out[:, PAIR:]
        out = out[:, :PAIR] / total
        o_ref[here, :] = jnp.where(lane < HEAD_DIM, out[:BLOCK], out[BLOCK:]).astype(bf16)
        sums = [total[:BLOCK, :1], total[BLOCK:, :1]]
        lse_ref[0, here, :] = jnp.concatenate([t + jnp.log(l) for t, l in zip(tops, sums)], 1)

    blocks = list(range(count // BLOCK))[::-1]
    ahead = scores_of(blocks[0])
    for at, i in enumerate(blocks):
        scores = ahead
        if at + 1 < len(blocks):
            ahead = scores_of(blocks[at + 1])
        attend(i, scores)


def attention_forward(project, fq, fk):
    count, width = project.shape[0], project.shape[1] // 3
    pairs = width // PAIR

    def part(at):
        return pl.BlockSpec((count, PAIR), lambda h: (0, h + at))

    same = pl.BlockSpec((count, PAIR), lambda h: (0, 0))
    return pl.pallas_call(
        forward_kernel,
        grid=(pairs,),
        in_specs=[part(0), part(pairs), part(2 * pairs), same, same],
        out_specs=[part(0), pl.BlockSpec((1, count, 2), lambda h: (h, 0, 0))],
        out_shape=[
            jax.ShapeDtypeStruct((count, width), bf16),
            jax.ShapeDtypeStruct((pairs, count, 2), f32),
        ],
        compiler_params=pltpu.CompilerParams(vmem_limit_bytes=24 * MIB),
        name="attention_forward",
    )(project, project, project, fq, fk)


def three_parts(values):
    high = values.astype(bf16)
    rest = values - high.astype(f32)
    middle = rest.astype(bf16)
    return high, middle, (rest - middle.astype(f32)).astype(bf16)


def backward_kernel(
    q_ref, k_ref, v_ref, fq_ref, fk_ref, o_ref, do_ref, lse_ref, _, dq_ref, dk_ref, dv_ref, qa, da, qt, dt, dq
):
    count = q_ref.shape[0]
    lane = lax.broadcasted_iota(jnp.int32, (count, PAIR), 1)
    narrow = lax.broadcasted_iota(jnp.int32, (BLOCK, PAIR), 1)
    row = lax.broadcasted_iota(jnp.int32, (BLOCK, BLOCK), 0)
    col = lax.broadcasted_iota(jnp.int32, (BLOCK, BLOCK), 1)
    causal = col <= row
    q, do, fq = q_ref[...] * jnp.asarray(0.125, bf16), do_ref[...], fq_ref[...]
    both = do.astype(f32) * o_ref[...].astype(f32)
    zero = jnp.zeros_like(q)
    qt[...] = q.T
    dt[...] = do.T
    for head in range(2):
        inside = (lane < HEAD_DIM) if head == 0 else (lane >= HEAD_DIM)
        rows = slice(head * count, (head + 1) * count)
        qa[rows, :PAIR] = jnp.where(inside, q, zero)
        a, b, c = three_parts(-lse_ref[0][:, head : head + 1])
        qa[rows, PAIR:] = jnp.where(
            lane == KINDS, a, jnp.where(lane == KINDS + 1, b, jnp.where(lane == KINDS + 2, c, fq))
        )
        da[rows, :PAIR] = jnp.where(inside, do, zero)
        a, b, c = three_parts(-jnp.sum(jnp.where(inside, both, 0.0), 1, keepdims=True))
        da[rows, PAIR:] = jnp.where(lane == KINDS, a, jnp.where(lane == KINDS + 1, b, zero))
    ones = jnp.where((narrow == KINDS) | (narrow == KINDS + 1), 1.0, 0.0).astype(bf16)
    for j in range(count // BLOCK):
        start = j * BLOCK
        here, rest = slice(start, start + BLOCK), count - start
        k = k_ref[here, :]
        keys = jnp.concatenate([k, fk_ref[here, :]], 1)
        values = jnp.concatenate([v_ref[here, :], ones], 1)
        weights, slopes = [], []
        for head in range(2):
            rows = slice(head * count + start, (head + 1) * count)
            part = jnp.exp(product(qa[rows, :], keys, NT))
            near = jnp.where(causal, part[:BLOCK], 0.0)
            part = jnp.concatenate([near, part[BLOCK:]], 0) if rest > BLOCK else near
            slopes.append((part * product(da[rows, :], values, NT)).astype(bf16))
            weights.append(part.astype(bf16))
        queries = product(jnp.concatenate(slopes, 0), k * jnp.asarray(0.125, bf16), NN)
        queries = jnp.where(lane[:rest] < HEAD_DIM, queries[:rest], queries[rest:])
        if j == 0:
            dq[...] = queries
        else:
            dq[start:, :] += queries
        heads = [slice(0, HEAD_DIM), slice(HEAD_DIM, PAIR)]
        dv = [product(dt[head, start:], part, NN) for head, part in zip(heads, weights)]
        dk = [product(qt[head, start:], part, NN) for head, part in zip(heads, slopes)]
        dv_ref[here, :] = jnp.concatenate(dv, 0).T.astype(bf16)
        dk_ref[here, :] = jnp.concatenate(dk, 0).T.astype(bf16)
    dq_ref[...] = dq[...].astype(bf16)


def attention_backward(info, project, fq, fk, attended, attended_grad, lse, first, pairs, earlier):
    count, width = attended.shape
    total = width // PAIR

    def part(at):
        return pl.BlockSpec((count, PAIR), lambda h: (0, h + at + first))

    same = pl.BlockSpec((count, PAIR), lambda h: (0, 0))
    operands = (project, project, project, fq, fk, attended, attended_grad, lse, info)
    specs = [part(0), part(total), part(2 * total), same, same, part(0), part(0)]
    specs.append(pl.BlockSpec((1, count, 2), lambda h: (h + first, 0, 0)))
    specs.append(pl.BlockSpec(memory_space=pl.ANY))
    kernel, aliases = backward_kernel, {}
    if earlier is not None:
        aliases = {len(operands) + k: k for k in range(3)}
        specs += [pl.BlockSpec(memory_space=pl.ANY)] * 3
        kernel = lambda *refs: backward_kernel(*refs[: len(operands)], *refs[len(operands) + 3 :])
    return pl.pallas_call(
        kernel,
        grid=(pairs,),
        in_specs=specs,
        out_specs=[part(0)] * 3,
        out_shape=[jax.ShapeDtypeStruct((count, width), bf16)] * 3,
        scratch_shapes=[
            pltpu.VMEM((2 * count, 2 * PAIR), bf16),
            pltpu.VMEM((2 * count, 2 * PAIR), bf16),
            pltpu.VMEM((PAIR, count), bf16),
            pltpu.VMEM((PAIR, count), bf16),
            pltpu.VMEM((count, PAIR), f32),
        ],
        input_output_aliases=aliases,
        compiler_params=pltpu.CompilerParams(vmem_limit_bytes=24 * MIB),
        cost_estimate=SHORT,
        name="attention_backward",
    )(*operands, *(earlier or ()))


def halving_stages(group):
    stages = [(("dp", 0), ("dp", 0)), (("role", 0), ("dp", 1)), (("dp", 1), ("role", 0))]
    return stages + [(("dp", bit), ("dp", bit)) for bit in range(2, group.bit_length() - 1)]


def route_of(stage, roles, group):
    pairs = []
    for role in range(roles):
        for place in range(group):
            axis, bit = stage[place & 1]
            other = (role ^ (1 << bit), place) if axis == "role" else (role, place ^ (1 << bit))
            pairs.append((role * group + place, other[0] * group + other[1]))
    return pairs


def codes_of(stages):
    codes = []
    for other in (0, 1):
        place = {"role": lax.axis_index("role"), "dp": lax.axis_index("dp") ^ other}
        odd = place["dp"] & 1
        code = jnp.int32(0)
        for even_way, odd_way in stages[:STAGES]:
            bits = [(place[axis] >> bit) & 1 for axis, bit in (even_way, odd_way)]
            code = code * 2 + jnp.where(odd == 0, bits[0], bits[1])
        codes.append(code)
    return jnp.stack(codes)


def place_rows(acc, low, out_ref, sub=SUB):
    rows = acc.shape[0] // sub
    for j in range(sub):
        at = pl.multiple_of((jnp.int32(j) ^ low) * rows, rows)
        out_ref[pl.ds(at, rows), :] = acc[j * rows : (j + 1) * rows]


def attn_weight_grad_kernel(
    half, info_ref, normed_ref, attended_ref, q_ref, k_ref, v_ref, o_ref, grad_ref, acc_ref
):
    panel = panel_in(half)(pl.program_id(0), info_ref)
    rights = (q_ref, k_ref, v_ref, o_ref)
    for k in range(4):

        @pl.when(panel == k)
        def _():
            left = attended_ref if k == 3 else normed_ref
            acc_ref[...] = product(left[...], rights[k][...], TN).astype(bf16)

    low = (info_ref[1 - half] // (SUB // ATTN_SUB)) & (ATTN_SUB - 1)
    place_rows(acc_ref[...], low, grad_ref, ATTN_SUB)


def attn_weight_grad(info, half, normed, attended, rights):
    count, width = normed.shape
    whole = pl.BlockSpec(memory_space=pltpu.VMEM)
    return pl.pallas_call(
        partial(attn_weight_grad_kernel, half),
        grid_spec=pltpu.PrefetchScalarGridSpec(
            num_scalar_prefetch=1,
            grid=(2,),
            in_specs=[whole] * 6,
            out_specs=pl.BlockSpec((width, width), lambda i, c: (i, 0)),
            scratch_shapes=[pltpu.VMEM((width, width), bf16)],
        ),
        out_shape=jax.ShapeDtypeStruct((2 * width, width), bf16),
        compiler_params=pltpu.CompilerParams(vmem_limit_bytes=22 * MIB),
        cost_estimate=SHORT,
        name="attn_weight_grad",
    )(info, normed, attended, *rights)


def finish_kernel(halves, split, info_ref, *refs):
    pieces = refs[: 2 * len(halves)]
    outs = refs[-2:] if split else refs[-1:]
    step = pl.program_id(0)
    half = halves[0] + step // 2
    code = jnp.where(half == 0, info_ref[0], info_ref[1])
    panel = (step & 1) ^ (code >> LOW)
    sub = ATTN_SUB if split else SUB
    low = (code // (SUB // sub)) & (sub - 1)
    rows = pieces[0].shape[1] // sub

    def fill(out_ref, piece):
        for j in range(sub):
            at = pl.multiple_of((jnp.int32(j) ^ low) * rows, rows)
            out_ref[j * rows : (j + 1) * rows, :] = piece[pl.ds(at, rows), :].astype(f32)

    if split and halves == (1,):

        @pl.when((step == 0) & (code >> LOW + 1 == 0))
        def _():
            outs[1][...] = refs[3][...]

    for k, piece in enumerate(pieces):
        if split:

            @pl.when((step == k) & (panel < 3))
            def _():
                fill(outs[0], piece)

            @pl.when((step == k) & (panel == 3))
            def _():
                fill(outs[1], piece)

        else:

            @pl.when(step == k)
            def _():
                fill(outs[0], piece)


def finish(info, pieces, layout, name, halves=(0, 1), earlier=()):
    width = pieces[0].shape[1]
    block = (width, width)
    split = layout == "attn"

    def panel(i, c):
        return (i & 1) ^ (jnp.where(halves[0] + i // 2 == 0, c[0], c[1]) >> LOW)

    if layout == "tall":
        shapes = [(4 * width, width)]
        places = [lambda i, c: (panel(i, c), 0)]
    elif layout == "wide":
        shapes = [(width, 4 * width)]
        places = [lambda i, c: (0, panel(i, c))]
    else:
        shapes = [(width, 3 * width), (width, width)]
        places = [lambda i, c: (0, jnp.minimum(panel(i, c), 2)), lambda i, c: (0, 0)]
    whole = pl.BlockSpec(block, lambda i, c: (0, 0), pipeline_mode=pl.Buffered(1))
    in_specs = [pl.BlockSpec(memory_space=pltpu.VMEM)] * len(pieces)
    if earlier:
        in_specs += [pl.BlockSpec(memory_space=pl.ANY), whole]
    return pl.pallas_call(
        partial(finish_kernel, halves, split),
        grid_spec=pltpu.PrefetchScalarGridSpec(
            num_scalar_prefetch=1,
            grid=(len(pieces),),
            in_specs=in_specs,
            out_specs=[pl.BlockSpec(block, place) for place in places],
        ),
        out_shape=[jax.ShapeDtypeStruct(shape, f32) for shape in shapes],
        input_output_aliases={3: 0, 4: 1} if earlier else {},
        compiler_params=pltpu.CompilerParams(vmem_limit_bytes=24 * MIB),
        cost_estimate=pl.CostEstimate(
            flops=0, bytes_accessed=6 * len(pieces) * width * width, transcendentals=0
        ),
        name=name,
    )(info, *pieces, *earlier)


def packed(small):
    high = lax.reduce_precision(small, exponent_bits=8, mantissa_bits=7)
    rows = jnp.concatenate([high, small - high], 0).astype(bf16)
    return jnp.pad(rows, ((0, 16 - rows.shape[0]), (0, 0)))


def unpacked(rows, count):
    return rows[:count].astype(f32) + rows[count : 2 * count].astype(f32)


class RowSum:
    def __init__(self, send, routes, stages=STAGES):
        self.send, self.keep, self.got = [send], None, None
        self.pieces, self.small = [], None
        self.steps = [("halve", route) for route in routes[: stages - 1]]
        self.steps += [("last", routes[stages - 1])]
        self.steps += [("whole", route) for route in routes[stages:]]
        self.steps += [("join", route) for route in routes[stages - 1 : 1 : -1]]
        self.steps += [("far", routes[1]), ("core", routes[0])]

    def launch(self):
        self.got = [lax.ppermute(part, AXES, self.steps[0][1]) for part in self.send]

    def with_small(self):
        if self.small is None:
            return [self.keep]
        return [jnp.concatenate([self.keep, packed(self.small)], 0)]

    def add_small(self, rows):
        if self.small is not None:
            self.small = self.small + unpacked(rows, self.small.shape[0])

    def take(self, got):
        kind = self.steps.pop(0)[0]
        if kind == "halve":
            half = self.keep.shape[0] // 2
            self.send = [self.keep[half:] + got[0][half:]]
            self.keep = self.keep[:half] + got[0][:half]
        elif kind in ("last", "whole", "join"):
            count = self.keep.shape[0]
            if kind != "last":
                self.add_small(got[0][count:])
            if kind == "join":
                self.keep = jnp.concatenate([self.keep, got[0][:count]], axis=0)
            else:
                self.keep = self.keep + got[0][:count]
            self.send = self.with_small()
        elif kind == "far":
            self.add_small(got[0][self.keep.shape[0] :])
            self.pieces = [self.keep, got[0]]
            self.send = list(self.pieces)
            if self.small is not None:
                self.send.append(self.small)
        else:
            self.pieces += got[:2]
            if self.small is not None:
                self.small = self.small + got[2]
            self.send = []


def lanes_of(rows, width):
    return lax.broadcasted_iota(jnp.int32, (rows, width), 1)


def live_rows(info_ref, start, rows):
    place = start + lax.broadcasted_iota(jnp.int32, (rows, 1), 0)
    return place, place < info_ref[TOTAL]


def decompressed(values, lane, last):
    return jnp.where(lane == last, -jnp.sum(values, axis=1, keepdims=True), values)


def enter_kernel(
    info_ref,
    x_ref,
    cot_ref,
    gain_ref,
    w_ref,
    inputs_ref,
    normed_ref,
    project_ref,
    bg_ref,
    fq_ref,
    fk_ref,
    energy_ref,
):
    step = pl.program_id(0)
    rows, width = x_ref.shape
    last = width - 1
    lane = lanes_of(rows, width)
    place, live = live_rows(info_ref, step * rows, rows)
    x = jnp.where(lane < last, x_ref[...].astype(f32), 0.0)
    inputs_ref[...] = x.astype(bf16)
    full = decompressed(x, lane, last)
    square = jnp.sum(full * full, axis=1, keepdims=True)
    normed = (full * lax.rsqrt(square * (1.0 / width) + EPS) * gain_ref[...]).astype(bf16)
    normed_ref[...] = normed
    project_ref[...] = product(normed, w_ref[...], NN).astype(bf16)
    cot = jnp.where((lane < last) & live, cot_ref[...].astype(f32), 0.0)
    bg_ref[...] = (cot - jnp.sum(cot, axis=1, keepdims=True) * (1.0 / width)).astype(bf16)
    segment = jnp.zeros_like(place)
    for k in range(ROWMAX):
        segment += (place >= info_ref[ENDS + k]).astype(jnp.int32)
    narrow = lanes_of(rows, PAIR)
    hot = narrow == segment
    fq_ref[...] = jnp.where(hot, 1.0, 0.0).astype(bf16)
    ones = jnp.where(narrow < KINDS + 3, 1.0, 0.0)
    fk_ref[...] = jnp.where(narrow < KINDS, jnp.where(hot, 0.0, NEG), ones).astype(bf16)

    @pl.when(step == 0)
    def _():
        energy_ref[...] = jnp.zeros_like(energy_ref)

    energy_ref[...] += jnp.sum(jnp.where(live, square, 0.0), keepdims=True)


def enter(info, stream, cotangent, gain, w_qkv):
    count, width = stream.shape[0], w_qkv.shape[0]
    rows = min(BLOCK, count)

    def some(columns):
        return pl.BlockSpec((rows, columns), lambda i, c: (i, 0))

    def whole(shape):
        return pl.BlockSpec(shape, lambda i, c: (0, 0), pipeline_mode=pl.Buffered(1))

    return pl.pallas_call(
        enter_kernel,
        grid_spec=pltpu.PrefetchScalarGridSpec(
            num_scalar_prefetch=1,
            grid=(count // rows,),
            in_specs=[some(width), some(width), whole((1, width)), whole(w_qkv.shape)],
            out_specs=[some(width), some(width), some(3 * width), some(width), some(PAIR), some(PAIR)]
            + [pl.BlockSpec((8, PAIR), lambda i, c: (0, 0))],
        ),
        out_shape=[
            jax.ShapeDtypeStruct((count, width), bf16),
            jax.ShapeDtypeStruct((count, width), bf16),
            jax.ShapeDtypeStruct((count, 3 * width), bf16),
            jax.ShapeDtypeStruct((count, width), bf16),
            jax.ShapeDtypeStruct((count, PAIR), bf16),
            jax.ShapeDtypeStruct((count, PAIR), bf16),
            jax.ShapeDtypeStruct((8, PAIR), f32),
        ],
        compiler_params=pltpu.CompilerParams(vmem_limit_bytes=18 * MIB),
        cost_estimate=SHORT,
        name="enter",
    )(info, *far(stream, cotangent), gain, *far(w_qkv))


def middle_rows(info_ref, attended_ref, w_out_ref, x_ref, gain_ref, middle_ref, normed_ref, energy_ref):
    count, width = attended_ref.shape
    last = width - 1
    rows = min(BLOCK, count)
    lane = lanes_of(rows, width)
    energy_ref[...] = jnp.zeros_like(energy_ref)

    @pl.loop(0, count // rows)
    def _(block):
        start = pl.multiple_of(block * rows, rows)
        here = pl.ds(start, rows)
        branch = product(attended_ref[here, :], w_out_ref[...], NN)
        mean = jnp.sum(branch, axis=1, keepdims=True) * (1.0 / width)
        middle = (x_ref[here, :].astype(f32) + branch - mean).astype(bf16)
        middle = jnp.where(lane < last, middle, jnp.zeros_like(middle))
        middle_ref[here, :] = middle
        full = decompressed(middle.astype(f32), lane, last)
        square = jnp.sum(full * full, axis=1, keepdims=True)
        scaled = full * lax.rsqrt(square * (1.0 / width) + EPS) * gain_ref[...]
        normed_ref[here, :] = scaled.astype(bf16)
        _, live = live_rows(info_ref, start, rows)
        energy_ref[...] += jnp.sum(jnp.where(live, square, 0.0), keepdims=True)


def up_rows(normed_ref, w_up_ref, bg_ref, active_ref, slope_ref, grad_ref, low):
    count = normed_ref.shape[0]
    rows = min(BLOCK, count)

    def hidden_of(block):
        return product(normed_ref[block * rows : (block + 1) * rows, :], w_up_ref[...], NN)

    ahead = hidden_of(0)
    for block in range(count // rows):
        here = slice(block * rows, (block + 1) * rows)
        hidden = ahead
        if block + 1 < count // rows:
            ahead = hidden_of(block + 1)
        square = hidden * hidden
        gate = 0.5 + 0.5 * jnp.tanh(hidden * (SQRT_2_PI + (SQRT_2_PI * 0.044715) * square))
        active = hidden * gate
        active_ref[here, :] = active.astype(bf16)
        inner = (1.0 - gate) * (2.0 * SQRT_2_PI + (6.0 * SQRT_2_PI * 0.044715) * square)
        slope_ref[here, :] = (gate + active * inner).astype(bf16)
    place_rows(product(active_ref[...], bg_ref[...], TN).astype(bf16), low, grad_ref)


def first_up_kernel(
    info_ref,
    attended_ref,
    w_out_ref,
    x_ref,
    gain_ref,
    w_up_ref,
    bg_ref,
    middle_ref,
    normed_ref,
    energy_ref,
    active_ref,
    slope_ref,
    grad_ref,
):
    @pl.when(pl.program_id(0) == 0)
    def _():
        middle_rows(
            info_ref, attended_ref, w_out_ref, x_ref, gain_ref, middle_ref, normed_ref, energy_ref
        )

    up_rows(normed_ref, w_up_ref, bg_ref, active_ref, slope_ref, grad_ref, info_ref[1] & (SUB - 1))


def second_up_kernel(
    info_ref, normed_ref, w_up_ref, bg_ref, _, __, active_ref, slope_ref, grad_ref
):
    up_rows(normed_ref, w_up_ref, bg_ref, active_ref, slope_ref, grad_ref, info_ref[0] & (SUB - 1))


def panel_in(half):
    return lambda i, c: i ^ (c[1 - half] >> LOW)


def up_and_grad_down(info, half, attended, w_out, stream, gain, w_up, bg, first=None):
    count, width = bg.shape
    panel = panel_in(half)
    whole = pl.BlockSpec(memory_space=pltpu.VMEM)
    stays = pl.BlockSpec(memory_space=pltpu.VMEM)
    wide = pl.BlockSpec((count, width), lambda i, c: (0, panel(i, c)))
    w_up_spec = pl.BlockSpec((width, width), lambda i, c: (0, panel(i, c)))
    out_specs = [wide, wide, pl.BlockSpec((width, width), lambda i, c: (i, 0))]
    out_shape = [pltpu.HBM((count, 4 * width), bf16)] * 2
    out_shape += [jax.ShapeDtypeStruct((2 * width, width), bf16)]
    if half == 0:
        kernel, aliases = first_up_kernel, {}
        in_specs = [
            whole,
            whole,
            whole,
            pl.BlockSpec((1, width), lambda i, c: (0, 0)),
            w_up_spec,
            whole,
        ]
        operands = (attended, w_out, stream, gain, *far(w_up), bg)
        out_specs = [stays, stays, pl.BlockSpec((8, PAIR), lambda i, c: (0, 0))] + out_specs
        out_shape = [
            jax.ShapeDtypeStruct((count, width), bf16),
            jax.ShapeDtypeStruct((count, width), bf16),
            jax.ShapeDtypeStruct((8, PAIR), f32),
        ] + out_shape
    else:
        kernel, aliases = second_up_kernel, {4: 0, 5: 1}
        in_specs = [whole, w_up_spec, whole] + [pl.BlockSpec(memory_space=pl.ANY)] * 2
        operands = (attended, *far(w_up), bg, *far(*first))
    return pl.pallas_call(
        kernel,
        grid_spec=pltpu.PrefetchScalarGridSpec(
            num_scalar_prefetch=1, grid=(2,), in_specs=in_specs, out_specs=out_specs
        ),
        out_shape=out_shape,
        input_output_aliases=aliases,
        compiler_params=pltpu.CompilerParams(vmem_limit_bytes=34 * MIB),
        cost_estimate=SHORT,
        name="up_and_grad_down",
    )(info, *operands)


def hidden_grad_kernel(half, info_ref, bg_ref, w_down_ref, slope_ref, normed_ref, *refs):
    hg_ref, grad_ref = refs[-2:]
    count = bg_ref.shape[0]
    rows = min(BLOCK, count)
    for block in range(count // rows):
        here = slice(block * rows, (block + 1) * rows)
        grad = product(bg_ref[here, :], w_down_ref[...], NT)
        hg_ref[here, :] = (grad * slope_ref[here, :].astype(f32)).astype(bf16)
    acc = product(normed_ref[...], hg_ref[...], TN).astype(bf16)
    place_rows(acc, info_ref[1 - half] & (SUB - 1), grad_ref)


def hidden_grad_and_grad_up(info, half, bg, w_down, slope, normed, first=None):
    count, width = bg.shape
    panel = panel_in(half)
    whole = pl.BlockSpec(memory_space=pltpu.VMEM)
    wide = pl.BlockSpec((count, width), lambda i, c: (0, panel(i, c)))
    in_specs = [whole, pl.BlockSpec((width, width), lambda i, c: (panel(i, c), 0)), wide, whole]
    operands = [bg, *far(w_down, slope), normed]
    if half:
        in_specs += [pl.BlockSpec(memory_space=pl.ANY)]
        operands += far(first)
    return pl.pallas_call(
        partial(hidden_grad_kernel, half),
        grid_spec=pltpu.PrefetchScalarGridSpec(
            num_scalar_prefetch=1,
            grid=(2,),
            in_specs=in_specs,
            out_specs=[wide, pl.BlockSpec((width, width), lambda i, c: (i, 0))],
        ),
        out_shape=[
            pltpu.HBM((count, 4 * width), bf16),
            jax.ShapeDtypeStruct((2 * width, width), bf16),
        ],
        input_output_aliases={5: 0} if half else {},
        compiler_params=pltpu.CompilerParams(vmem_limit_bytes=24 * MIB),
        cost_estimate=SHORT,
        name="hidden_grad_and_grad_up",
    )(info, *operands)


def norm_back(dz, values, gain, lane, last):
    width = last + 1
    full = decompressed(values, lane, last)
    scale = lax.rsqrt(jnp.sum(full * full, axis=1, keepdims=True) * (1.0 / width) + EPS)
    normal = full * scale
    gain_rows = jnp.sum((dz * normal).reshape(dz.shape[0] // 8, 8, width), axis=0)
    pulled = gain * dz
    inner = jnp.sum(normal * pulled, axis=1, keepdims=True) * (1.0 / width)
    grad = scale * (pulled - normal * inner)
    return grad - jnp.sum(jnp.where(lane == last, grad, 0.0), axis=1, keepdims=True), gain_rows


def middle_grad_kernel(
    info_ref,
    hg_ref,
    w_up_ref,
    middle_ref,
    gain_ref,
    cot_ref,
    w_out_ref,
    grad_ref,
    bag_ref,
    ag_ref,
    gains_ref,
    dz_ref,
):
    step = pl.program_id(0)
    rows, width = middle_ref.shape
    last = width - 1

    @pl.when(step == 0)
    def _():
        dz_ref[...] = product(hg_ref[...], w_up_ref[...], NT)
        gains_ref[...] = jnp.zeros_like(gains_ref)

    @pl.when((step > 0) & (step < 4))
    def _():
        dz_ref[...] += product(hg_ref[...], w_up_ref[...], NT)

    @pl.when(step >= 4)
    def _():
        lane = lanes_of(rows, width)
        start = pl.multiple_of((step - 4) * rows, rows)
        _, live = live_rows(info_ref, start, rows)
        dz = dz_ref[pl.ds(start, rows), :]
        pulled, gain_rows = norm_back(dz, middle_ref[...].astype(f32), gain_ref[...], lane, last)
        cot = jnp.where(live, cot_ref[...].astype(f32), 0.0)
        grad = jnp.where(lane < last, cot + pulled, 0.0).astype(bf16)
        grad_ref[...] = grad
        grad = grad.astype(f32)
        bag = (grad - jnp.sum(grad, axis=1, keepdims=True) * (1.0 / width)).astype(bf16)
        bag_ref[...] = bag
        ag_ref[...] = product(bag, w_out_ref[...], NT).astype(bf16)
        gains_ref[...] += gain_rows


def middle_grad(info, hg, w_up, middle, gain, cotangent, w_out):
    count, width = middle.shape
    rows = min(BLOCK, count)

    def some(columns):
        return pl.BlockSpec((rows, columns), lambda i, c: (jnp.maximum(i - 4, 0), 0))

    def panel(height):
        return pl.BlockSpec((height, width), lambda i, c: (0, jnp.minimum(i, 3)))

    def whole(shape):
        return pl.BlockSpec(shape, lambda i, c: (0, 0), pipeline_mode=pl.Buffered(1))

    return pl.pallas_call(
        middle_grad_kernel,
        grid_spec=pltpu.PrefetchScalarGridSpec(
            num_scalar_prefetch=1,
            grid=(4 + count // rows,),
            in_specs=[
                panel(count),
                panel(width),
                some(width),
                whole((1, width)),
                some(width),
                whole(w_out.shape),
            ],
            out_specs=[some(width)] * 3 + [pl.BlockSpec((8, width), lambda i, c: (0, 0))],
            scratch_shapes=[pltpu.VMEM((count, width), f32)],
        ),
        out_shape=[jax.ShapeDtypeStruct((count, width), bf16)] * 3
        + [jax.ShapeDtypeStruct((8, width), f32)],
        compiler_params=pltpu.CompilerParams(vmem_limit_bytes=24 * MIB),
        cost_estimate=SHORT,
        name="middle_grad",
    )(info, *far(hg, w_up), middle, gain, *far(cotangent), w_out)


def leave_kernel(first, info_ref, active_ref, w_down_ref, middle_ref, *refs):
    out_ref, energy_ref = refs[-2:]
    step = pl.program_id(0)
    rows, width = middle_ref.shape
    last = width - 1
    lane = lanes_of(rows, width)
    _, live = live_rows(info_ref, (first + step) * rows, rows)
    branch = product(active_ref[...], w_down_ref[...], NN)
    mean = jnp.sum(branch, axis=1, keepdims=True) * (1.0 / width)
    out = (middle_ref[...].astype(f32) + branch - mean).astype(bf16)
    out_ref[...] = out
    values = jnp.where(lane < last, out.astype(f32), 0.0)
    full = decompressed(values, lane, last)
    square = jnp.sum(full * full, axis=1, keepdims=True)

    @pl.when(step == 0)
    def _():
        energy_ref[...] = jnp.zeros_like(energy_ref)

    energy_ref[...] += jnp.sum(jnp.where(live, square, 0.0), keepdims=True)


def leave(info, active, w_down, middle, part, parts, earlier=None):
    count, width = middle.shape
    rows = min(BLOCK, count // parts)
    steps = count // parts // rows
    first = part * steps

    def some(columns):
        return pl.BlockSpec((rows, columns), lambda i, c: (i + first, 0))

    def whole(shape):
        return pl.BlockSpec(shape, lambda i, c: (0, 0), pipeline_mode=pl.Buffered(1))

    in_specs = [some(active.shape[1]), whole(w_down.shape), some(width)]
    operands = [*far(active, w_down), middle]
    if part:
        in_specs += [pl.BlockSpec(memory_space=pl.ANY)]
        operands += [earlier]
    return pl.pallas_call(
        partial(leave_kernel, first),
        grid_spec=pltpu.PrefetchScalarGridSpec(
            num_scalar_prefetch=1,
            grid=(steps,),
            in_specs=in_specs,
            out_specs=[some(width), pl.BlockSpec((8, PAIR), lambda i, c: (0, 0))],
        ),
        out_shape=[
            jax.ShapeDtypeStruct((count, width - 1), bf16),
            jax.ShapeDtypeStruct((8, PAIR), f32),
        ],
        input_output_aliases={4: 0} if part else {},
        compiler_params=pltpu.CompilerParams(vmem_limit_bytes=20 * MIB),
        cost_estimate=SHORT,
        name="leave",
    )(info, *operands)


def stream_grad_kernel(
    info_ref, dq_ref, dk_ref, dv_ref, w_ref, x_ref, gain_ref, middle_grad_ref, out_ref, gains_ref
):
    step = pl.program_id(0)
    rows, width = x_ref.shape
    last = width - 1
    lane = lanes_of(rows, width)
    dz = product(dq_ref[...], w_ref[:, :width], NT)
    dz += product(dk_ref[...], w_ref[:, width : 2 * width], NT)
    dz += product(dv_ref[...], w_ref[:, 2 * width :], NT)
    x = jnp.where(lane < last, x_ref[...].astype(f32), 0.0)
    pulled, gain_rows = norm_back(dz, x, gain_ref[...], lane, last)
    out_ref[...] = (middle_grad_ref[...].astype(f32) + pulled).astype(bf16)

    @pl.when(step == 0)
    def _():
        gains_ref[...] = jnp.zeros_like(gains_ref)

    gains_ref[...] += gain_rows


def stream_gradient(info, parts, w_qkv, stream, gain, middle_grads):
    count, width = middle_grads.shape
    rows = min(BLOCK, count)

    def some(columns):
        return pl.BlockSpec((rows, columns), lambda i, c: (i, 0))

    def whole(shape):
        return pl.BlockSpec(shape, lambda i, c: (0, 0), pipeline_mode=pl.Buffered(1))

    return pl.pallas_call(
        stream_grad_kernel,
        grid_spec=pltpu.PrefetchScalarGridSpec(
            num_scalar_prefetch=1,
            grid=(count // rows,),
            in_specs=[some(width)] * 3
            + [whole(w_qkv.shape), some(width), whole((1, width)), some(width)],
            out_specs=[some(width), whole((8, width))],
        ),
        out_shape=[
            jax.ShapeDtypeStruct((count, width - 1), bf16),
            jax.ShapeDtypeStruct((8, width), f32),
        ],
        compiler_params=pltpu.CompilerParams(vmem_limit_bytes=20 * MIB),
        cost_estimate=SHORT,
        name="stream_grad",
    )(info, *parts, *far(w_qkv), stream, gain, middle_grads)


ORDER = (
    "UGDa", "D+", "UGDb", "D-", "HGUa", "D+", "U+", "HGUb", "U-", "U+", "MG", "D-", "D+", "U-", "b", "D-",
    "D+", "U+", "b", "D-", "U-", "D+", "U+", "b", "D-", "U-", "D+", "U+", "GAa", "A+", "GAb", "A-", "A+",
    "stream", "D-", "U-", "A-", "A+", "D+", "U+", "leave0", "A-", "D-", "U-", "A+", "D+", "U+", "leave1", "A-",
    "D-", "A+", "D+", "prep", "A-", "U-", "A+", "U+", "A-", "D-", "U-", "A+", "D+", "U+", "D-", "finD", "A-",
    "A+", "A-", "U-", "A+", "U+", "U-", "finU", "A-", "A+", "finA1", "A-", "small", "finA2",
)


def body(stream, cotangent, w_qkv, w_out, w_up, w_down, gain_attn, gain_mlp, doc_lengths):
    width = w_out.shape[0]
    roles, group = lax.axis_size("role"), lax.axis_size("dp")
    stages = halving_stages(group)
    routes = [route_of(stage, roles, group) for stage in stages]
    place = lax.axis_index("role") * group + lax.axis_index("dp")
    lengths = lax.dynamic_slice_in_dim(doc_lengths, place, 1, 0)[0]
    ends = jnp.cumsum(lengths)
    info = jnp.concatenate([codes_of(stages), ends]).astype(jnp.int32)
    gain_attn, gain_mlp = gain_attn[None, :], gain_mlp[None, :]
    sums, has = {}, {}

    inputs, normed, project, branch_grad, fq, fk, energy_in = enter(
        info, stream, cotangent, gain_attn, w_qkv
    )
    attended, lse = attention_forward(project, fq, fk)

    def up_first(info):
        has["middle"], has["normed"], has["energy"], *has["wide"], half = up_and_grad_down(
            info, 0, attended, w_out, inputs, gain_mlp, w_up, branch_grad
        )
        sums["D"] = RowSum(half, routes)
        return "normed"

    def up_second(info):
        active, has["slope"], sums["D"].keep = up_and_grad_down(
            info, 1, has["normed"], None, None, None, w_up, branch_grad, has["wide"]
        )
        has["active"] = active
        return "slope"

    def hidden_first(info):
        has["hidden"], half = hidden_grad_and_grad_up(
            info, 0, branch_grad, w_down, has["slope"], has["normed"]
        )
        sums["U"] = RowSum(half, routes)
        return "hidden"

    def hidden_second(info):
        has["hidden"], sums["U"].keep = hidden_grad_and_grad_up(
            info, 1, branch_grad, w_down, has["slope"], has["normed"], has["hidden"]
        )
        return "hidden"

    def middle_back(info):
        has["grads"], has["attn_grad"], has["attended_grad"], has["gains"] = middle_grad(
            info, has["hidden"], w_up, has["middle"], gain_mlp, cotangent, w_out
        )
        has["calls"], has["parts"] = 0, None
        return "attended_grad"

    def attention_back(info):
        has["parts"] = attention_backward(
            info,
            project,
            fq,
            fk,
            attended,
            has["attended_grad"],
            lse,
            has["calls"],
            2,
            has["parts"],
        )
        has["calls"] += 2
        return "parts"

    def attn_first(info):
        rights = (*has["parts"], has["attn_grad"])
        half = attn_weight_grad(info, 0, normed, attended, rights)
        sums["A"] = RowSum(half, routes, ATTN_STAGES)
        has["half"] = half
        return "half"

    def attn_second(info):
        rights = (*has["parts"], has["attn_grad"])
        has["half"] = sums["A"].keep = attn_weight_grad(info, 1, normed, attended, rights)
        return "half"

    def stream_back(info):
        has["stream_grad"], has["gains_attn"] = stream_gradient(
            info, has["parts"], w_qkv, inputs, gain_attn, has["grads"]
        )
        return "stream_grad"

    def leave_part(part):
        def call(info):
            has["output"], has["energy", part] = leave(
                info, has["active"], w_down, has["middle"], part, 2, has.get("output")
            )
            return "output"

        return call

    def small_sums(info):
        energies = [energy_in, has["energy"], has["energy", 0] + has["energy", 1]]
        energies = jnp.concatenate([each[:1] for each in energies], 1)
        energies = jnp.pad(energies, ((0, 0), (0, width - 3 * PAIR)))
        gains = [jnp.sum(each, 0, keepdims=True) for each in (has["gains_attn"], has["gains"])]
        has["small"] = sums["A"].small = jnp.concatenate([*gains, energies], 0)
        return "small"

    def vectors(info):
        small = sums["A"].small
        live = jnp.sum(doc_lengths).astype(f32)
        has["vectors"] = (small[0], small[1], jnp.sqrt(small[2, : 3 * PAIR : PAIR] / (width * live)))
        return "vectors"

    def rows_of(name, layout):
        def call(info):
            (has[name],) = finish(info, sums[name].pieces, layout, "weight_rows")
            return name

        return call

    def attn_rows_first(info):
        has["rows"] = finish(info, sums["A"].pieces[:2], "attn", "weight_rows", (0,))
        return "rows"

    def attn_rows_second(info):
        has["rows"] = finish(info, sums["A"].pieces[2:], "attn", "weight_rows", (1,), has["rows"])
        return "rows"

    kernels = {
        "UGDa": up_first,
        "UGDb": up_second,
        "HGUa": hidden_first,
        "HGUb": hidden_second,
        "MG": middle_back,
        "b": attention_back,
        "GAa": attn_first,
        "GAb": attn_second,
        "stream": stream_back,
        "leave0": leave_part(0),
        "leave1": leave_part(1),
        "prep": small_sums,
        "small": vectors,
        "finD": rows_of("D", "tall"),
        "finU": rows_of("U", "wide"),
        "finA1": attn_rows_first,
        "finA2": attn_rows_second,
    }
    complete = {"finD": "D", "finU": "U", "finA2": "A", "small": "A"}
    token = info

    def exchange(name, launch, token):
        each = sums[name]
        if launch and each.got is None and each.steps:
            each.send, token = lax.optimization_barrier((each.send, token))
            with jax.named_scope("exchange_%s_%d" % (name, len(each.steps))):
                each.launch()
        elif not launch and each.got is not None:
            got, token = lax.optimization_barrier((each.got, token))
            each.got = None
            each.take(got)
        return token

    def finished(name, token):
        while sums[name].steps:
            token = exchange(name, True, token)
            token = exchange(name, False, token)
        return token

    for event in ORDER:
        if event[-1] in "+-":
            token = exchange(event[:-1], event[-1] == "+", token)
            continue
        if event in complete:
            token = finished(complete[event], token)
        if event == "finA1":
            while not sums["A"].pieces:
                token = exchange("A", True, token)
                token = exchange("A", False, token)
            token = exchange("A", True, token)
        key = kernels[event](token)
        has[key], token = lax.optimization_barrier((has[key], token))
        if event == "prep":
            sums["A"].small = has["small"]
    return (has["output"], has["stream_grad"], *has["rows"], has["U"], has["D"], *has["vectors"])


def solution(mesh):
    rows = P(("role", "dp"), None)
    return jax.shard_map(
        body,
        mesh=mesh,
        in_specs=(rows, rows) + (P(),) * 7,
        out_specs=(rows, rows) + (P(),) * 7,
        check_vma=False,
    )
```

```python
from functools import partial

import jax
import jax.numpy as jnp
from jax import lax
from jax.experimental import pallas as pl
from jax.experimental.pallas import tpu as pltpu
from jax.sharding import PartitionSpec as P

HEAD_DIM = 64
PAIR = 2 * HEAD_DIM
EPS = 1e-05
NEG = -1e30
BLOCK = 256
KINDS = 5
ROWMAX = 4
ENDS = 2
TOTAL = ENDS + ROWMAX - 1
MIB = 2**20
SHORT = pl.CostEstimate(flops=10**6, bytes_accessed=10**5, transcendentals=0)
SQRT_2_PI = 0.7978845608028654
STAGES = 5
SUB = 8
LOW = 3
AXES = ("role", "dp")
bf16 = jnp.bfloat16
f32 = jnp.float32
NT = (((1,), (1,)), ((), ()))
NN = (((1,), (0,)), ((), ()))
TN = (((0,), (0,)), ((), ()))


def far(*arrays):
    return [pltpu.with_memory_space_constraint(array, pltpu.HBM) for array in arrays]


def product(left, right, dims):
    return lax.dot_general(left, right, dims, preferred_element_type=f32)


def forward_kernel(q_ref, k_ref, v_ref, fq_ref, fk_ref, o_ref, lse_ref):
    count = q_ref.shape[0]
    lane = lax.broadcasted_iota(jnp.int32, (BLOCK, PAIR), 1)
    row = lax.broadcasted_iota(jnp.int32, (BLOCK, BLOCK), 0)
    col = lax.broadcasted_iota(jnp.int32, (BLOCK, BLOCK), 1)
    causal = col <= row

    def scores_of(i):
        here, seen = slice(i * BLOCK, (i + 1) * BLOCK), slice(0, (i + 1) * BLOCK)
        q, feature = q_ref[here, :] * jnp.asarray(0.125, bf16), fq_ref[here, :]
        first = jnp.where(lane < HEAD_DIM, q, jnp.zeros_like(q))
        second = jnp.where(lane < HEAD_DIM, jnp.zeros_like(q), q)
        queries = jnp.concatenate(
            [jnp.concatenate([part, feature], 1) for part in (first, second)], 0
        )
        return product(queries, jnp.concatenate([k_ref[seen, :], fk_ref[seen, :]], 1), NT)

    def attend(i, scores):
        here, seen = slice(i * BLOCK, (i + 1) * BLOCK), slice(0, (i + 1) * BLOCK)
        tops, weights = [], []
        for head in range(2):
            part = scores[head * BLOCK : (head + 1) * BLOCK]
            near = jnp.where(causal, part[:, i * BLOCK :], NEG)
            part = jnp.concatenate([part[:, : i * BLOCK], near], 1) if i else near
            tops.append(jnp.max(part, 1, keepdims=True))
            weights.append(jnp.exp(part - tops[-1]).astype(bf16))
        ones = jnp.ones(((i + 1) * BLOCK, PAIR), bf16)
        values = jnp.concatenate([v_ref[seen, :], ones], 1)
        out = product(jnp.concatenate(weights, 0), values, NN)
        total = out[:, PAIR:]
        out = out[:, :PAIR] / total
        o_ref[here, :] = jnp.where(lane < HEAD_DIM, out[:BLOCK], out[BLOCK:]).astype(bf16)
        sums = [total[:BLOCK, :1], total[BLOCK:, :1]]
        lse_ref[0, here, :] = jnp.concatenate([t + jnp.log(l) for t, l in zip(tops, sums)], 1)

    blocks = list(range(count // BLOCK))[::-1]
    ahead = scores_of(blocks[0])
    for at, i in enumerate(blocks):
        scores = ahead
        if at + 1 < len(blocks):
            ahead = scores_of(blocks[at + 1])
        attend(i, scores)


def attention_forward(project, fq, fk):
    count, width = project.shape[0], project.shape[1] // 3
    pairs = width // PAIR

    def part(at):
        return pl.BlockSpec((count, PAIR), lambda h: (0, h + at))

    same = pl.BlockSpec((count, PAIR), lambda h: (0, 0))
    return pl.pallas_call(
        forward_kernel,
        grid=(pairs,),
        in_specs=[part(0), part(pairs), part(2 * pairs), same, same],
        out_specs=[part(0), pl.BlockSpec((1, count, 2), lambda h: (h, 0, 0))],
        out_shape=[
            jax.ShapeDtypeStruct((count, width), bf16),
            jax.ShapeDtypeStruct((pairs, count, 2), f32),
        ],
        compiler_params=pltpu.CompilerParams(vmem_limit_bytes=24 * MIB),
        name="attention_forward",
    )(project, project, project, fq, fk)


def three_parts(values):
    high = values.astype(bf16)
    rest = values - high.astype(f32)
    middle = rest.astype(bf16)
    return high, middle, (rest - middle.astype(f32)).astype(bf16)


def backward_kernel(
    q_ref, k_ref, v_ref, fq_ref, fk_ref, o_ref, do_ref, lse_ref, _, dq_ref, dk_ref, dv_ref, qa, da, qt, dt, dq
):
    count = q_ref.shape[0]
    lane = lax.broadcasted_iota(jnp.int32, (count, PAIR), 1)
    narrow = lax.broadcasted_iota(jnp.int32, (BLOCK, PAIR), 1)
    row = lax.broadcasted_iota(jnp.int32, (BLOCK, BLOCK), 0)
    col = lax.broadcasted_iota(jnp.int32, (BLOCK, BLOCK), 1)
    causal = col <= row
    q, do, fq = q_ref[...] * jnp.asarray(0.125, bf16), do_ref[...], fq_ref[...]
    both = do.astype(f32) * o_ref[...].astype(f32)
    zero = jnp.zeros_like(q)
    qt[...] = q.T
    dt[...] = do.T
    for head in range(2):
        inside = (lane < HEAD_DIM) if head == 0 else (lane >= HEAD_DIM)
        rows = slice(head * count, (head + 1) * count)
        qa[rows, :PAIR] = jnp.where(inside, q, zero)
        a, b, c = three_parts(-lse_ref[0][:, head : head + 1])
        qa[rows, PAIR:] = jnp.where(
            lane == KINDS, a, jnp.where(lane == KINDS + 1, b, jnp.where(lane == KINDS + 2, c, fq))
        )
        da[rows, :PAIR] = jnp.where(inside, do, zero)
        a, b, c = three_parts(-jnp.sum(jnp.where(inside, both, 0.0), 1, keepdims=True))
        da[rows, PAIR:] = jnp.where(lane == KINDS, a, jnp.where(lane == KINDS + 1, b, zero))
    ones = jnp.where((narrow == KINDS) | (narrow == KINDS + 1), 1.0, 0.0).astype(bf16)
    for j in range(count // BLOCK):
        start = j * BLOCK
        here, rest = slice(start, start + BLOCK), count - start
        k = k_ref[here, :]
        keys = jnp.concatenate([k, fk_ref[here, :]], 1)
        values = jnp.concatenate([v_ref[here, :], ones], 1)
        weights, slopes = [], []
        for head in range(2):
            rows = slice(head * count + start, (head + 1) * count)
            part = jnp.exp(product(qa[rows, :], keys, NT))
            near = jnp.where(causal, part[:BLOCK], 0.0)
            part = jnp.concatenate([near, part[BLOCK:]], 0) if rest > BLOCK else near
            slopes.append((part * product(da[rows, :], values, NT)).astype(bf16))
            weights.append(part.astype(bf16))
        queries = product(jnp.concatenate(slopes, 0), k * jnp.asarray(0.125, bf16), NN)
        queries = jnp.where(lane[:rest] < HEAD_DIM, queries[:rest], queries[rest:])
        if j == 0:
            dq[...] = queries
        else:
            dq[start:, :] += queries
        heads = [slice(0, HEAD_DIM), slice(HEAD_DIM, PAIR)]
        dv = [product(dt[head, start:], part, NN) for head, part in zip(heads, weights)]
        dk = [product(qt[head, start:], part, NN) for head, part in zip(heads, slopes)]
        dv_ref[here, :] = jnp.concatenate(dv, 0).T.astype(bf16)
        dk_ref[here, :] = jnp.concatenate(dk, 0).T.astype(bf16)
    dq_ref[...] = dq[...].astype(bf16)


def attention_backward(info, project, fq, fk, attended, attended_grad, lse, first, pairs, earlier):
    count, width = attended.shape
    total = width // PAIR

    def part(at):
        return pl.BlockSpec((count, PAIR), lambda h: (0, h + at + first))

    same = pl.BlockSpec((count, PAIR), lambda h: (0, 0))
    operands = (project, project, project, fq, fk, attended, attended_grad, lse, info)
    specs = [part(0), part(total), part(2 * total), same, same, part(0), part(0)]
    specs.append(pl.BlockSpec((1, count, 2), lambda h: (h + first, 0, 0)))
    specs.append(pl.BlockSpec(memory_space=pl.ANY))
    kernel, aliases = backward_kernel, {}
    if earlier is not None:
        aliases = {len(operands) + k: k for k in range(3)}
        specs += [pl.BlockSpec(memory_space=pl.ANY)] * 3
        kernel = lambda *refs: backward_kernel(*refs[: len(operands)], *refs[len(operands) + 3 :])
    return pl.pallas_call(
        kernel,
        grid=(pairs,),
        in_specs=specs,
        out_specs=[part(0)] * 3,
        out_shape=[jax.ShapeDtypeStruct((count, width), bf16)] * 3,
        scratch_shapes=[
            pltpu.VMEM((2 * count, 2 * PAIR), bf16),
            pltpu.VMEM((2 * count, 2 * PAIR), bf16),
            pltpu.VMEM((PAIR, count), bf16),
            pltpu.VMEM((PAIR, count), bf16),
            pltpu.VMEM((count, PAIR), f32),
        ],
        input_output_aliases=aliases,
        compiler_params=pltpu.CompilerParams(vmem_limit_bytes=24 * MIB),
        cost_estimate=SHORT,
        name="attention_backward",
    )(*operands, *(earlier or ()))


def halving_stages(group):
    stages = [(("dp", 0), ("dp", 0)), (("role", 0), ("dp", 1)), (("dp", 1), ("role", 0))]
    return stages + [(("dp", bit), ("dp", bit)) for bit in range(2, group.bit_length() - 1)]


def route_of(stage, roles, group):
    pairs = []
    for role in range(roles):
        for place in range(group):
            axis, bit = stage[place & 1]
            other = (role ^ (1 << bit), place) if axis == "role" else (role, place ^ (1 << bit))
            pairs.append((role * group + place, other[0] * group + other[1]))
    return pairs


def codes_of(stages):
    codes = []
    for other in (0, 1):
        place = {"role": lax.axis_index("role"), "dp": lax.axis_index("dp") ^ other}
        odd = place["dp"] & 1
        code = jnp.int32(0)
        for even_way, odd_way in stages[:STAGES]:
            bits = [(place[axis] >> bit) & 1 for axis, bit in (even_way, odd_way)]
            code = code * 2 + jnp.where(odd == 0, bits[0], bits[1])
        codes.append(code)
    return jnp.stack(codes)


def place_rows(acc, low, out_ref):
    rows = acc.shape[0] // SUB
    for j in range(SUB):
        at = pl.multiple_of((jnp.int32(j) ^ low) * rows, rows)
        out_ref[pl.ds(at, rows), :] = acc[j * rows : (j + 1) * rows]


def attn_weight_grad_kernel(
    half, info_ref, normed_ref, attended_ref, q_ref, k_ref, v_ref, o_ref, grad_ref, acc_ref
):
    panel = panel_in(half)(pl.program_id(0), info_ref)
    rights = (q_ref, k_ref, v_ref, o_ref)
    for k in range(4):

        @pl.when(panel == k)
        def _():
            left = attended_ref if k == 3 else normed_ref
            acc_ref[...] = product(left[...], rights[k][...], TN).astype(bf16)

    place_rows(acc_ref[...], info_ref[1 - half] & (SUB - 1), grad_ref)


def attn_weight_grad(info, half, normed, attended, rights):
    count, width = normed.shape
    whole = pl.BlockSpec(memory_space=pltpu.VMEM)
    return pl.pallas_call(
        partial(attn_weight_grad_kernel, half),
        grid_spec=pltpu.PrefetchScalarGridSpec(
            num_scalar_prefetch=1,
            grid=(2,),
            in_specs=[whole] * 6,
            out_specs=pl.BlockSpec((width, width), lambda i, c: (i, 0)),
            scratch_shapes=[pltpu.VMEM((width, width), bf16)],
        ),
        out_shape=jax.ShapeDtypeStruct((2 * width, width), bf16),
        compiler_params=pltpu.CompilerParams(vmem_limit_bytes=22 * MIB),
        cost_estimate=SHORT,
        name="attn_weight_grad",
    )(info, normed, attended, *rights)


def finish_kernel(halves, split, info_ref, *refs):
    pieces = refs[: 2 * len(halves)]
    step = pl.program_id(0)
    half = halves[0] + step // 2
    code = jnp.where(half == 0, info_ref[0], info_ref[1])
    low = code & (SUB - 1)
    rows = pieces[0].shape[1] // SUB

    def fill(out_ref, piece):
        for j in range(SUB):
            at = pl.multiple_of((jnp.int32(j) ^ low) * rows, rows)
            out_ref[j * rows : (j + 1) * rows, :] = piece[pl.ds(at, rows), :].astype(f32)

    if not split:
        for k, piece in enumerate(pieces):

            @pl.when(step == k)
            def _():
                fill(refs[-1], piece)

        return
    out_ref, far_ref, held_ref, sem = refs[-4:]
    source = (1 - step) ^ ((code >> LOW) & 1)
    last_half = code >> LOW + 1 == 1
    copy = pltpu.make_async_copy(held_ref, far_ref, sem)
    for k, piece in enumerate(pieces):

        @pl.when((source == k) & (last_half & (step == 0)))
        def _():
            fill(held_ref, piece)
            copy.start()

        @pl.when((source == k) & jnp.logical_not(last_half & (step == 0)))
        def _():
            fill(out_ref, piece)

    @pl.when(last_half & (step == 1))
    def _():
        copy.wait()


def finish(info, pieces, layout, name, halves=(0, 1), earlier=()):
    width = pieces[0].shape[1]
    block = (width, width)
    split = layout == "attn"

    def panel(i, c):
        code = jnp.where(halves[0] + i // 2 == 0, c[0], c[1])
        if split:
            return 2 * (code >> LOW + 1) + 1 - i
        return (i & 1) ^ (code >> LOW)

    out_specs, scratch = [], []
    if layout == "tall":
        shapes = [(4 * width, width)]
        out_specs = [pl.BlockSpec(block, lambda i, c: (panel(i, c), 0))]
    elif layout == "wide":
        shapes = [(width, 4 * width)]
        out_specs = [pl.BlockSpec(block, lambda i, c: (0, panel(i, c)))]
    else:
        shapes = [(width, 3 * width), (width, width)]
        out_specs = [pl.BlockSpec(block, lambda i, c: (0, jnp.minimum(panel(i, c), 2)))]
        out_specs += [pl.BlockSpec(memory_space=pl.ANY)]
        scratch = [pltpu.VMEM(block, f32), pltpu.SemaphoreType.DMA]
    in_specs = [pl.BlockSpec(memory_space=pltpu.VMEM)] * len(pieces)
    in_specs += [pl.BlockSpec(memory_space=pl.ANY)] * len(earlier)
    return pl.pallas_call(
        partial(finish_kernel, halves, split),
        grid_spec=pltpu.PrefetchScalarGridSpec(
            num_scalar_prefetch=1,
            grid=(len(pieces),),
            in_specs=in_specs,
            out_specs=out_specs,
            scratch_shapes=scratch,
        ),
        out_shape=[jax.ShapeDtypeStruct(shape, f32) for shape in shapes],
        input_output_aliases={3: 0, 4: 1} if earlier else {},
        compiler_params=pltpu.CompilerParams(vmem_limit_bytes=24 * MIB),
        cost_estimate=SHORT,
        name=name,
    )(info, *pieces, *earlier)


def packed(small):
    high = lax.reduce_precision(small, exponent_bits=8, mantissa_bits=7)
    rows = jnp.concatenate([high, small - high], 0).astype(bf16)
    return jnp.pad(rows, ((0, 16 - rows.shape[0]), (0, 0)))


def unpacked(rows, count):
    return rows[:count].astype(f32) + rows[count : 2 * count].astype(f32)


class RowSum:
    def __init__(self, send, routes, stages=STAGES):
        self.send, self.keep, self.got = [send], None, None
        self.pieces, self.small = [], None
        self.steps = [("halve", route) for route in routes[: stages - 1]]
        self.steps += [("last", routes[stages - 1])]
        self.steps += [("whole", route) for route in routes[stages:]]
        self.steps += [("join", route) for route in routes[stages - 1 : 1 : -1]]
        self.steps += [("far", routes[1]), ("core", routes[0])]

    def launch(self):
        self.got = [lax.ppermute(part, AXES, self.steps[0][1]) for part in self.send]

    def with_small(self):
        if self.small is None:
            return [self.keep]
        return [jnp.concatenate([self.keep, packed(self.small)], 0)]

    def add_small(self, rows):
        if self.small is not None:
            self.small = self.small + unpacked(rows, self.small.shape[0])

    def take(self, got):
        kind = self.steps.pop(0)[0]
        if kind == "halve":
            half = self.keep.shape[0] // 2
            self.send = [self.keep[half:] + got[0][half:]]
            self.keep = self.keep[:half] + got[0][:half]
        elif kind in ("last", "whole", "join"):
            count = self.keep.shape[0]
            if kind != "last":
                self.add_small(got[0][count:])
            if kind == "join":
                self.keep = jnp.concatenate([self.keep, got[0][:count]], axis=0)
            else:
                self.keep = self.keep + got[0][:count]
            self.send = self.with_small()
        elif kind == "far":
            self.add_small(got[0][self.keep.shape[0] :])
            self.pieces = [self.keep, got[0]]
            self.send = list(self.pieces)
            if self.small is not None:
                self.send.append(self.small)
        else:
            self.pieces += got[:2]
            if self.small is not None:
                self.small = self.small + got[2]
            self.send = []


def lanes_of(rows, width):
    return lax.broadcasted_iota(jnp.int32, (rows, width), 1)


def live_rows(info_ref, start, rows):
    place = start + lax.broadcasted_iota(jnp.int32, (rows, 1), 0)
    return place, place < info_ref[TOTAL]


def decompressed(values, lane, last):
    return jnp.where(lane == last, -jnp.sum(values, axis=1, keepdims=True), values)


def enter_kernel(
    info_ref,
    x_ref,
    cot_ref,
    gain_ref,
    w_ref,
    inputs_ref,
    normed_ref,
    project_ref,
    bg_ref,
    fq_ref,
    fk_ref,
    energy_ref,
):
    step = pl.program_id(0)
    rows, width = x_ref.shape
    last = width - 1
    lane = lanes_of(rows, width)
    place, live = live_rows(info_ref, step * rows, rows)
    x = jnp.where(lane < last, x_ref[...].astype(f32), 0.0)
    inputs_ref[...] = x.astype(bf16)
    full = decompressed(x, lane, last)
    square = jnp.sum(full * full, axis=1, keepdims=True)
    normed = (full * lax.rsqrt(square * (1.0 / width) + EPS) * gain_ref[:1, :]).astype(bf16)
    normed_ref[...] = normed
    project_ref[...] = product(normed, w_ref[...], NN).astype(bf16)
    cot = jnp.where((lane < last) & live, cot_ref[...].astype(f32), 0.0)
    bg_ref[...] = (cot - jnp.sum(cot, axis=1, keepdims=True) * (1.0 / width)).astype(bf16)
    segment = jnp.zeros_like(place)
    for k in range(ROWMAX):
        segment += (place >= info_ref[ENDS + k]).astype(jnp.int32)
    narrow = lanes_of(rows, PAIR)
    hot = narrow == segment
    fq_ref[...] = jnp.where(hot, 1.0, 0.0).astype(bf16)
    ones = jnp.where(narrow < KINDS + 3, 1.0, 0.0)
    fk_ref[...] = jnp.where(narrow < KINDS, jnp.where(hot, 0.0, NEG), ones).astype(bf16)

    @pl.when(step == 0)
    def _():
        energy_ref[...] = jnp.zeros_like(energy_ref)

    energy_ref[...] += jnp.sum(jnp.where(live, square, 0.0), keepdims=True)


def enter(info, stream, cotangent, gain, w_qkv):
    count, width = stream.shape[0], w_qkv.shape[0]
    rows = min(BLOCK, count)

    def some(columns):
        return pl.BlockSpec((rows, columns), lambda i, c: (i, 0))

    def whole(shape):
        return pl.BlockSpec(shape, lambda i, c: (0, 0), pipeline_mode=pl.Buffered(1))

    return pl.pallas_call(
        enter_kernel,
        grid_spec=pltpu.PrefetchScalarGridSpec(
            num_scalar_prefetch=1,
            grid=(count // rows,),
            in_specs=[some(width), some(width), whole((2, width)), whole(w_qkv.shape)],
            out_specs=[some(width), some(width), some(3 * width), some(width), some(PAIR), some(PAIR)]
            + [pl.BlockSpec((8, PAIR), lambda i, c: (0, 0))],
        ),
        out_shape=[
            jax.ShapeDtypeStruct((count, width), bf16),
            jax.ShapeDtypeStruct((count, width), bf16),
            jax.ShapeDtypeStruct((count, 3 * width), bf16),
            jax.ShapeDtypeStruct((count, width), bf16),
            jax.ShapeDtypeStruct((count, PAIR), bf16),
            jax.ShapeDtypeStruct((count, PAIR), bf16),
            jax.ShapeDtypeStruct((8, PAIR), f32),
        ],
        compiler_params=pltpu.CompilerParams(vmem_limit_bytes=18 * MIB),
        cost_estimate=SHORT,
        name="enter",
    )(info, *far(stream, cotangent), gain, *far(w_qkv))


def middle_rows(info_ref, attended_ref, w_out_ref, x_ref, gain_ref, middle_ref, normed_ref, energy_ref):
    count, width = attended_ref.shape
    last = width - 1
    rows = min(BLOCK, count)
    lane = lanes_of(rows, width)
    energy_ref[...] = jnp.zeros_like(energy_ref)

    @pl.loop(0, count // rows)
    def _(block):
        start = pl.multiple_of(block * rows, rows)
        here = pl.ds(start, rows)
        branch = product(attended_ref[here, :], w_out_ref[...], NN)
        mean = jnp.sum(branch, axis=1, keepdims=True) * (1.0 / width)
        middle = (x_ref[here, :].astype(f32) + branch - mean).astype(bf16)
        middle = jnp.where(lane < last, middle, jnp.zeros_like(middle))
        middle_ref[here, :] = middle
        full = decompressed(middle.astype(f32), lane, last)
        square = jnp.sum(full * full, axis=1, keepdims=True)
        scaled = full * lax.rsqrt(square * (1.0 / width) + EPS) * gain_ref[1:, :]
        normed_ref[here, :] = scaled.astype(bf16)
        _, live = live_rows(info_ref, start, rows)
        energy_ref[...] += jnp.sum(jnp.where(live, square, 0.0), keepdims=True)


def up_rows(normed_ref, w_up_ref, bg_ref, active_ref, slope_ref, grad_ref, low):
    count = normed_ref.shape[0]
    rows = min(BLOCK, count)

    def hidden_of(block):
        return product(normed_ref[block * rows : (block + 1) * rows, :], w_up_ref[...], NN)

    ahead = hidden_of(0)
    for block in range(count // rows):
        here = slice(block * rows, (block + 1) * rows)
        hidden = ahead
        if block + 1 < count // rows:
            ahead = hidden_of(block + 1)
        square = hidden * hidden
        gate = 0.5 + 0.5 * jnp.tanh(hidden * (SQRT_2_PI + (SQRT_2_PI * 0.044715) * square))
        active = hidden * gate
        active_ref[here, :] = active.astype(bf16)
        inner = (1.0 - gate) * (2.0 * SQRT_2_PI + (6.0 * SQRT_2_PI * 0.044715) * square)
        slope_ref[here, :] = (gate + active * inner).astype(bf16)
    place_rows(product(active_ref[...], bg_ref[...], TN).astype(bf16), low, grad_ref)


def first_up_kernel(
    info_ref,
    attended_ref,
    w_out_ref,
    x_ref,
    gain_ref,
    w_up_ref,
    bg_ref,
    middle_ref,
    normed_ref,
    energy_ref,
    active_ref,
    slope_ref,
    grad_ref,
):
    @pl.when(pl.program_id(0) == 0)
    def _():
        middle_rows(
            info_ref, attended_ref, w_out_ref, x_ref, gain_ref, middle_ref, normed_ref, energy_ref
        )

    up_rows(normed_ref, w_up_ref, bg_ref, active_ref, slope_ref, grad_ref, info_ref[1] & (SUB - 1))


def second_up_kernel(
    info_ref, normed_ref, w_up_ref, bg_ref, _, __, active_ref, slope_ref, grad_ref
):
    up_rows(normed_ref, w_up_ref, bg_ref, active_ref, slope_ref, grad_ref, info_ref[0] & (SUB - 1))


def panel_in(half):
    return lambda i, c: i ^ (c[1 - half] >> LOW)


def up_and_grad_down(info, half, attended, w_out, stream, gain, w_up, bg, first=None):
    count, width = bg.shape
    panel = panel_in(half)
    whole = pl.BlockSpec(memory_space=pltpu.VMEM)
    stays = pl.BlockSpec(memory_space=pltpu.VMEM)
    wide = pl.BlockSpec((count, width), lambda i, c: (0, panel(i, c)))
    w_up_spec = pl.BlockSpec((width, width), lambda i, c: (0, panel(i, c)))
    out_specs = [wide, wide, pl.BlockSpec((width, width), lambda i, c: (i, 0))]
    out_shape = [pltpu.HBM((count, 4 * width), bf16)] * 2
    out_shape += [jax.ShapeDtypeStruct((2 * width, width), bf16)]
    if half == 0:
        kernel, aliases = first_up_kernel, {}
        in_specs = [
            whole,
            whole,
            whole,
            pl.BlockSpec((2, width), lambda i, c: (0, 0)),
            w_up_spec,
            whole,
        ]
        operands = (attended, w_out, stream, gain, *far(w_up), bg)
        out_specs = [stays, stays, pl.BlockSpec((8, PAIR), lambda i, c: (0, 0))] + out_specs
        out_shape = [
            jax.ShapeDtypeStruct((count, width), bf16),
            jax.ShapeDtypeStruct((count, width), bf16),
            jax.ShapeDtypeStruct((8, PAIR), f32),
        ] + out_shape
    else:
        kernel, aliases = second_up_kernel, {4: 0, 5: 1}
        in_specs = [whole, w_up_spec, whole] + [pl.BlockSpec(memory_space=pl.ANY)] * 2
        operands = (attended, *far(w_up), bg, *far(*first))
    return pl.pallas_call(
        kernel,
        grid_spec=pltpu.PrefetchScalarGridSpec(
            num_scalar_prefetch=1, grid=(2,), in_specs=in_specs, out_specs=out_specs
        ),
        out_shape=out_shape,
        input_output_aliases=aliases,
        compiler_params=pltpu.CompilerParams(vmem_limit_bytes=34 * MIB),
        cost_estimate=SHORT,
        name="up_and_grad_down",
    )(info, *operands)


def hidden_grad_kernel(half, info_ref, bg_ref, w_down_ref, slope_ref, normed_ref, *refs):
    hg_ref, grad_ref = refs[-2:]
    count = bg_ref.shape[0]
    rows = min(BLOCK, count)
    for block in range(count // rows):
        here = slice(block * rows, (block + 1) * rows)
        grad = product(bg_ref[here, :], w_down_ref[...], NT)
        hg_ref[here, :] = (grad * slope_ref[here, :].astype(f32)).astype(bf16)
    acc = product(normed_ref[...], hg_ref[...], TN).astype(bf16)
    place_rows(acc, info_ref[1 - half] & (SUB - 1), grad_ref)


def hidden_grad_and_grad_up(info, half, bg, w_down, slope, normed, first=None):
    count, width = bg.shape
    panel = panel_in(half)
    whole = pl.BlockSpec(memory_space=pltpu.VMEM)
    wide = pl.BlockSpec((count, width), lambda i, c: (0, panel(i, c)))
    in_specs = [whole, pl.BlockSpec((width, width), lambda i, c: (panel(i, c), 0)), wide, whole]
    operands = [bg, *far(w_down, slope), normed]
    if half:
        in_specs += [pl.BlockSpec(memory_space=pl.ANY)]
        operands += far(first)
    return pl.pallas_call(
        partial(hidden_grad_kernel, half),
        grid_spec=pltpu.PrefetchScalarGridSpec(
            num_scalar_prefetch=1,
            grid=(2,),
            in_specs=in_specs,
            out_specs=[wide, pl.BlockSpec((width, width), lambda i, c: (i, 0))],
        ),
        out_shape=[
            pltpu.HBM((count, 4 * width), bf16),
            jax.ShapeDtypeStruct((2 * width, width), bf16),
        ],
        input_output_aliases={5: 0} if half else {},
        compiler_params=pltpu.CompilerParams(vmem_limit_bytes=24 * MIB),
        cost_estimate=SHORT,
        name="hidden_grad_and_grad_up",
    )(info, *operands)


def norm_back(dz, values, gain, lane, last):
    width = last + 1
    full = decompressed(values, lane, last)
    scale = lax.rsqrt(jnp.sum(full * full, axis=1, keepdims=True) * (1.0 / width) + EPS)
    normal = full * scale
    gain_rows = jnp.sum((dz * normal).reshape(dz.shape[0] // 8, 8, width), axis=0)
    pulled = gain * dz
    inner = jnp.sum(normal * pulled, axis=1, keepdims=True) * (1.0 / width)
    grad = scale * (pulled - normal * inner)
    return grad - jnp.sum(jnp.where(lane == last, grad, 0.0), axis=1, keepdims=True), gain_rows


def middle_grad_kernel(
    info_ref,
    hg_ref,
    w_up_ref,
    middle_ref,
    gain_ref,
    cot_ref,
    w_out_ref,
    grad_ref,
    bag_ref,
    ag_ref,
    gains_ref,
    dz_ref,
):
    step = pl.program_id(0)
    rows, width = middle_ref.shape
    last = width - 1

    @pl.when(step == 0)
    def _():
        dz_ref[...] = product(hg_ref[...], w_up_ref[...], NT)
        gains_ref[...] = jnp.zeros_like(gains_ref)

    @pl.when((step > 0) & (step < 4))
    def _():
        dz_ref[...] += product(hg_ref[...], w_up_ref[...], NT)

    @pl.when(step >= 4)
    def _():
        lane = lanes_of(rows, width)
        start = pl.multiple_of((step - 4) * rows, rows)
        _, live = live_rows(info_ref, start, rows)
        dz = dz_ref[pl.ds(start, rows), :]
        pulled, gain_rows = norm_back(dz, middle_ref[...].astype(f32), gain_ref[1:, :], lane, last)
        cot = jnp.where(live, cot_ref[...].astype(f32), 0.0)
        grad = jnp.where(lane < last, cot + pulled, 0.0).astype(bf16)
        grad_ref[...] = grad
        grad = grad.astype(f32)
        bag = (grad - jnp.sum(grad, axis=1, keepdims=True) * (1.0 / width)).astype(bf16)
        bag_ref[...] = bag
        ag_ref[...] = product(bag, w_out_ref[...], NT).astype(bf16)
        gains_ref[...] += gain_rows


def middle_grad(info, hg, w_up, middle, gain, cotangent, w_out):
    count, width = middle.shape
    rows = min(BLOCK, count)

    def some(columns):
        return pl.BlockSpec((rows, columns), lambda i, c: (jnp.maximum(i - 4, 0), 0))

    def panel(height):
        return pl.BlockSpec((height, width), lambda i, c: (0, jnp.minimum(i, 3)))

    def whole(shape):
        return pl.BlockSpec(shape, lambda i, c: (0, 0), pipeline_mode=pl.Buffered(1))

    return pl.pallas_call(
        middle_grad_kernel,
        grid_spec=pltpu.PrefetchScalarGridSpec(
            num_scalar_prefetch=1,
            grid=(4 + count // rows,),
            in_specs=[
                panel(count),
                panel(width),
                some(width),
                whole((2, width)),
                some(width),
                whole(w_out.shape),
            ],
            out_specs=[some(width)] * 3 + [pl.BlockSpec((8, width), lambda i, c: (0, 0))],
            scratch_shapes=[pltpu.VMEM((count, width), f32)],
        ),
        out_shape=[jax.ShapeDtypeStruct((count, width), bf16)] * 3
        + [jax.ShapeDtypeStruct((8, width), f32)],
        compiler_params=pltpu.CompilerParams(vmem_limit_bytes=24 * MIB),
        cost_estimate=SHORT,
        name="middle_grad",
    )(info, *far(hg, w_up), middle, gain, *far(cotangent), w_out)


def leave_kernel(first, info_ref, active_ref, w_down_ref, middle_ref, *refs):
    out_ref, energy_ref = refs[-2:]
    step = pl.program_id(0)
    rows, width = middle_ref.shape
    last = width - 1
    lane = lanes_of(rows, width)
    _, live = live_rows(info_ref, (first + step) * rows, rows)
    branch = product(active_ref[...], w_down_ref[...], NN)
    mean = jnp.sum(branch, axis=1, keepdims=True) * (1.0 / width)
    out = (middle_ref[...].astype(f32) + branch - mean).astype(bf16)
    out_ref[...] = out
    values = jnp.where(lane < last, out.astype(f32), 0.0)
    full = decompressed(values, lane, last)
    square = jnp.sum(full * full, axis=1, keepdims=True)

    @pl.when(step == 0)
    def _():
        energy_ref[...] = jnp.zeros_like(energy_ref)

    energy_ref[...] += jnp.sum(jnp.where(live, square, 0.0), keepdims=True)


def leave(info, active, w_down, middle, part, parts, earlier=None):
    count, width = middle.shape
    rows = min(BLOCK, count // parts)
    steps = count // parts // rows
    first = part * steps

    def some(columns):
        return pl.BlockSpec((rows, columns), lambda i, c: (i + first, 0))

    def whole(shape):
        return pl.BlockSpec(shape, lambda i, c: (0, 0), pipeline_mode=pl.Buffered(1))

    in_specs = [some(active.shape[1]), whole(w_down.shape), some(width)]
    operands = [*far(active, w_down), middle]
    if part:
        in_specs += [pl.BlockSpec(memory_space=pl.ANY)]
        operands += [earlier]
    return pl.pallas_call(
        partial(leave_kernel, first),
        grid_spec=pltpu.PrefetchScalarGridSpec(
            num_scalar_prefetch=1,
            grid=(steps,),
            in_specs=in_specs,
            out_specs=[some(width), pl.BlockSpec((8, PAIR), lambda i, c: (0, 0))],
        ),
        out_shape=[
            jax.ShapeDtypeStruct((count, width - 1), bf16),
            jax.ShapeDtypeStruct((8, PAIR), f32),
        ],
        input_output_aliases={4: 0} if part else {},
        compiler_params=pltpu.CompilerParams(vmem_limit_bytes=20 * MIB),
        cost_estimate=SHORT,
        name="leave",
    )(info, *operands)


def stream_grad_kernel(
    info_ref, dq_ref, dk_ref, dv_ref, w_ref, x_ref, gain_ref, middle_grad_ref, out_ref, gains_ref
):
    step = pl.program_id(0)
    rows, width = x_ref.shape
    last = width - 1
    lane = lanes_of(rows, width)
    dz = product(dq_ref[...], w_ref[:, :width], NT)
    dz += product(dk_ref[...], w_ref[:, width : 2 * width], NT)
    dz += product(dv_ref[...], w_ref[:, 2 * width :], NT)
    x = jnp.where(lane < last, x_ref[...].astype(f32), 0.0)
    pulled, gain_rows = norm_back(dz, x, gain_ref[:1, :], lane, last)
    out_ref[...] = (middle_grad_ref[...].astype(f32) + pulled).astype(bf16)

    @pl.when(step == 0)
    def _():
        gains_ref[...] = jnp.zeros_like(gains_ref)

    gains_ref[...] += gain_rows


def stream_gradient(info, parts, w_qkv, stream, gain, middle_grads):
    count, width = middle_grads.shape
    rows = min(BLOCK, count)

    def some(columns):
        return pl.BlockSpec((rows, columns), lambda i, c: (i, 0))

    def whole(shape):
        return pl.BlockSpec(shape, lambda i, c: (0, 0), pipeline_mode=pl.Buffered(1))

    return pl.pallas_call(
        stream_grad_kernel,
        grid_spec=pltpu.PrefetchScalarGridSpec(
            num_scalar_prefetch=1,
            grid=(count // rows,),
            in_specs=[some(width)] * 3
            + [whole(w_qkv.shape), some(width), whole((2, width)), some(width)],
            out_specs=[some(width), whole((8, width))],
        ),
        out_shape=[
            jax.ShapeDtypeStruct((count, width - 1), bf16),
            jax.ShapeDtypeStruct((8, width), f32),
        ],
        compiler_params=pltpu.CompilerParams(vmem_limit_bytes=20 * MIB),
        cost_estimate=SHORT,
        name="stream_grad",
    )(info, *parts, *far(w_qkv), stream, gain, middle_grads)


D, U, A = range(3)
(
    UP_1,
    UP_2,
    HIDDEN_1,
    HIDDEN_2,
    MIDDLE,
    BACK,
    GRADS_1,
    GRADS_2,
    STREAM,
    LEAVE_1,
    LEAVE_2,
    PREP,
    VECTORS,
    DOWN_ROWS,
    UP_ROWS,
    ATTN_ROWS_1,
    ATTN_ROWS_2,
) = range(17)
D_GO, D_IN, U_GO, U_IN, A_GO, A_IN = range(17, 23)
EXCHANGES = {
    D_GO: (D, True),
    D_IN: (D, False),
    U_GO: (U, True),
    U_IN: (U, False),
    A_GO: (A, True),
    A_IN: (A, False),
}
ORDER = (
    UP_1, D_GO, UP_2, D_IN, HIDDEN_1, D_GO, U_GO, HIDDEN_2, U_IN, U_GO, MIDDLE, D_IN, D_GO, BACK, D_IN,
    U_IN, D_GO, U_GO, BACK, D_IN, U_IN, D_GO, U_GO, BACK, D_IN, U_IN, D_GO, U_GO, GRADS_1, A_GO, GRADS_2,
    A_IN, A_GO, STREAM, D_IN, U_IN, A_IN, A_GO, D_GO, U_GO, LEAVE_1, A_IN, D_IN, U_IN, A_GO, D_GO, U_GO,
    LEAVE_2, A_IN, D_IN, A_GO, D_GO, PREP, A_IN, U_IN, A_GO, U_GO, A_IN, D_IN, U_IN, A_GO, D_GO, U_GO,
    D_IN, DOWN_ROWS, A_IN, A_GO, A_IN, U_IN, A_GO, U_GO, U_IN, UP_ROWS, A_IN, A_GO, ATTN_ROWS_1, A_IN,
    VECTORS, ATTN_ROWS_2,
)


class Held:
    pass


def body(stream, cotangent, w_qkv, w_out, w_up, w_down, gain_attn, gain_mlp, doc_lengths):
    width = w_out.shape[0]
    roles, group = lax.axis_size("role"), lax.axis_size("dp")
    stages = halving_stages(group)
    routes = [route_of(stage, roles, group) for stage in stages]
    place = lax.axis_index("role") * group + lax.axis_index("dp")
    lengths = lax.dynamic_slice_in_dim(doc_lengths, place, 1, 0)[0]
    ends = jnp.cumsum(lengths)
    info = jnp.concatenate([codes_of(stages), ends]).astype(jnp.int32)
    gains = jnp.stack([gain_attn, gain_mlp])
    sums, has = [None] * 3, Held()
    has.output, has.leaving = None, {}

    inputs, normed, project, branch_grad, fq, fk, energy_in = enter(
        info, stream, cotangent, gains, w_qkv
    )
    attended, lse = attention_forward(project, fq, fk)

    def up_first(info):
        has.middle, has.normed, has.energy, *has.wide, half = up_and_grad_down(
            info, 0, attended, w_out, inputs, gains, w_up, branch_grad
        )
        sums[D] = RowSum(half, routes)
        return "normed"

    def up_second(info):
        active, has.slope, sums[D].keep = up_and_grad_down(
            info, 1, has.normed, None, None, None, w_up, branch_grad, has.wide
        )
        has.active = active
        return "slope"

    def hidden_first(info):
        has.hidden, half = hidden_grad_and_grad_up(
            info, 0, branch_grad, w_down, has.slope, has.normed
        )
        sums[U] = RowSum(half, routes)
        return "hidden"

    def hidden_second(info):
        has.hidden, sums[U].keep = hidden_grad_and_grad_up(
            info, 1, branch_grad, w_down, has.slope, has.normed, has.hidden
        )
        return "hidden"

    def middle_back(info):
        has.grads, has.attn_grad, has.attended_grad, has.gains = middle_grad(
            info, has.hidden, w_up, has.middle, gains, cotangent, w_out
        )
        has.calls, has.parts = 0, None
        return "attended_grad"

    def attention_back(info):
        has.parts = attention_backward(
            info,
            project,
            fq,
            fk,
            attended,
            has.attended_grad,
            lse,
            has.calls,
            2,
            has.parts,
        )
        has.calls += 2
        return "parts"

    def attn_first(info):
        rights = (*has.parts, has.attn_grad)
        half = attn_weight_grad(info, 0, normed, attended, rights)
        sums[A] = RowSum(half, routes)
        has.half = half
        return "half"

    def attn_second(info):
        rights = (*has.parts, has.attn_grad)
        has.half = sums[A].keep = attn_weight_grad(info, 1, normed, attended, rights)
        return "half"

    def stream_back(info):
        has.stream_grad, has.gains_attn = stream_gradient(
            info, has.parts, w_qkv, inputs, gains, has.grads
        )
        return "stream_grad"

    def leave_part(part):
        def call(info):
            has.output, has.leaving[part] = leave(
                info, has.active, w_down, has.middle, part, 2, has.output
            )
            return "output"

        return call

    def small_sums(info):
        energies = [energy_in, has.energy, has.leaving[0] + has.leaving[1]]
        energies = jnp.concatenate([each[:1] for each in energies], 1)
        energies = jnp.pad(energies, ((0, 0), (0, width - 3 * PAIR)))
        rows = [jnp.sum(each, 0, keepdims=True) for each in (has.gains_attn, has.gains)]
        has.small = sums[A].small = jnp.concatenate([*rows, energies], 0)
        return "small"

    def vectors(info):
        small = sums[A].small
        live = jnp.sum(doc_lengths).astype(f32)
        has.vectors = (small[0], small[1], jnp.sqrt(small[2, : 3 * PAIR : PAIR] / (width * live)))
        return "vectors"

    def rows_of(name, tall):
        def call(info):
            pieces = sums[name].pieces
            (rows,) = finish(info, pieces, "tall" if tall else "wide", "weight_rows")
            setattr(has, "down" if tall else "up", rows)
            return "down" if tall else "up"

        return call

    def attn_rows_first(info):
        has.rows = finish(info, sums[A].pieces[:2], "attn", "weight_rows", (0,))
        return "rows"

    def attn_rows_second(info):
        has.rows = finish(info, sums[A].pieces[2:], "attn", "weight_rows", (1,), has.rows)
        return "rows"

    kernels = {
        UP_1: up_first,
        UP_2: up_second,
        HIDDEN_1: hidden_first,
        HIDDEN_2: hidden_second,
        MIDDLE: middle_back,
        BACK: attention_back,
        GRADS_1: attn_first,
        GRADS_2: attn_second,
        STREAM: stream_back,
        LEAVE_1: leave_part(0),
        LEAVE_2: leave_part(1),
        PREP: small_sums,
        VECTORS: vectors,
        DOWN_ROWS: rows_of(D, True),
        UP_ROWS: rows_of(U, False),
        ATTN_ROWS_1: attn_rows_first,
        ATTN_ROWS_2: attn_rows_second,
    }
    complete = {DOWN_ROWS: D, UP_ROWS: U, ATTN_ROWS_2: A, VECTORS: A}
    token = info

    def exchange(name, launch, token):
        each = sums[name]
        if launch and each.got is None and each.steps:
            each.send, token = lax.optimization_barrier((each.send, token))
            with jax.named_scope("exchange_%s_%d" % ("DUA"[name], len(each.steps))):
                each.launch()
        elif not launch and each.got is not None:
            got, token = lax.optimization_barrier((each.got, token))
            each.got = None
            each.take(got)
        return token

    def finished(name, token):
        while sums[name].steps:
            token = exchange(name, True, token)
            token = exchange(name, False, token)
        return token

    for event in ORDER:
        if event in EXCHANGES:
            token = exchange(*EXCHANGES[event], token)
            continue
        if event in complete:
            token = finished(complete[event], token)
        if event == ATTN_ROWS_1:
            while not sums[A].pieces:
                token = exchange(A, True, token)
                token = exchange(A, False, token)
            token = exchange(A, True, token)
        key = kernels[event](token)
        held, token = lax.optimization_barrier((getattr(has, key), token))
        setattr(has, key, held)
        if event == PREP:
            sums[A].small = has.small
    return (has.output, has.stream_grad, *has.rows, has.up, has.down, *has.vectors)


def solution(mesh):
    rows = P(("role", "dp"), None)
    return jax.shard_map(
        body,
        mesh=mesh,
        in_specs=(rows, rows) + (P(),) * 7,
        out_specs=(rows, rows) + (P(),) * 7,
        check_vma=False,
    )
```

```python
from functools import partial

import jax
import jax.numpy as jnp
from jax import lax
from jax.experimental import pallas as pl
from jax.experimental.pallas import tpu as pltpu
from jax.sharding import PartitionSpec as P

HEAD_DIM = 64
PAIR = 2 * HEAD_DIM
EPS = 1e-05
NEG = -1e30
BLOCK = 256
KINDS = 5
ROWMAX = 4
ENDS = 2
TOTAL = ENDS + ROWMAX - 1
MIB = 2**20
SHORT = pl.CostEstimate(flops=10**6, bytes_accessed=10**5, transcendentals=0)
SQRT_2_PI = 0.7978845608028654
STAGES = 5
SUB = 8
LOW = 3
AXES = ("role", "dp")
bf16 = jnp.bfloat16
f32 = jnp.float32
NT = (((1,), (1,)), ((), ()))
NN = (((1,), (0,)), ((), ()))
TN = (((0,), (0,)), ((), ()))


def far(*arrays):
    return [pltpu.with_memory_space_constraint(array, pltpu.HBM) for array in arrays]


def product(left, right, dims):
    return lax.dot_general(left, right, dims, preferred_element_type=f32)


def forward_kernel(q_ref, k_ref, v_ref, fq_ref, fk_ref, o_ref, lse_ref):
    count = q_ref.shape[0]
    lane = lax.broadcasted_iota(jnp.int32, (BLOCK, PAIR), 1)
    row = lax.broadcasted_iota(jnp.int32, (BLOCK, BLOCK), 0)
    col = lax.broadcasted_iota(jnp.int32, (BLOCK, BLOCK), 1)
    causal = col <= row

    def scores_of(i):
        here, seen = slice(i * BLOCK, (i + 1) * BLOCK), slice(0, (i + 1) * BLOCK)
        q, feature = q_ref[here, :] * jnp.asarray(0.125, bf16), fq_ref[here, :]
        first = jnp.where(lane < HEAD_DIM, q, jnp.zeros_like(q))
        second = jnp.where(lane < HEAD_DIM, jnp.zeros_like(q), q)
        queries = jnp.concatenate(
            [jnp.concatenate([part, feature], 1) for part in (first, second)], 0
        )
        return product(queries, jnp.concatenate([k_ref[seen, :], fk_ref[seen, :]], 1), NT)

    def attend(i, scores):
        here, seen = slice(i * BLOCK, (i + 1) * BLOCK), slice(0, (i + 1) * BLOCK)
        tops, weights = [], []
        for head in range(2):
            part = scores[head * BLOCK : (head + 1) * BLOCK]
            near = jnp.where(causal, part[:, i * BLOCK :], NEG)
            part = jnp.concatenate([part[:, : i * BLOCK], near], 1) if i else near
            tops.append(jnp.max(part, 1, keepdims=True))
            weights.append(jnp.exp(part - tops[-1]).astype(bf16))
        ones = jnp.ones(((i + 1) * BLOCK, PAIR), bf16)
        values = jnp.concatenate([v_ref[seen, :], ones], 1)
        out = product(jnp.concatenate(weights, 0), values, NN)
        total = out[:, PAIR:]
        out = out[:, :PAIR] / total
        o_ref[here, :] = jnp.where(lane < HEAD_DIM, out[:BLOCK], out[BLOCK:]).astype(bf16)
        sums = [total[:BLOCK, :1], total[BLOCK:, :1]]
        lse_ref[0, here, :] = jnp.concatenate([t + jnp.log(l) for t, l in zip(tops, sums)], 1)

    blocks = list(range(count // BLOCK))[::-1]
    ahead = scores_of(blocks[0])
    for at, i in enumerate(blocks):
        scores = ahead
        if at + 1 < len(blocks):
            ahead = scores_of(blocks[at + 1])
        attend(i, scores)


def attention_forward(project, fq, fk):
    count, width = project.shape[0], project.shape[1] // 3
    pairs = width // PAIR

    def part(at):
        return pl.BlockSpec((count, PAIR), lambda h: (0, h + at))

    same = pl.BlockSpec((count, PAIR), lambda h: (0, 0))
    return pl.pallas_call(
        forward_kernel,
        grid=(pairs,),
        in_specs=[part(0), part(pairs), part(2 * pairs), same, same],
        out_specs=[part(0), pl.BlockSpec((1, count, 2), lambda h: (h, 0, 0))],
        out_shape=[
            jax.ShapeDtypeStruct((count, width), bf16),
            jax.ShapeDtypeStruct((pairs, count, 2), f32),
        ],
        compiler_params=pltpu.CompilerParams(vmem_limit_bytes=24 * MIB),
        name="attention_forward",
    )(project, project, project, fq, fk)


def three_parts(values):
    high = values.astype(bf16)
    rest = values - high.astype(f32)
    middle = rest.astype(bf16)
    return high, middle, (rest - middle.astype(f32)).astype(bf16)


def backward_kernel(
    q_ref, k_ref, v_ref, fq_ref, fk_ref, o_ref, do_ref, lse_ref, _, dq_ref, dk_ref, dv_ref, qa, da, qt, dt, dq
):
    count = q_ref.shape[0]
    lane = lax.broadcasted_iota(jnp.int32, (count, PAIR), 1)
    narrow = lax.broadcasted_iota(jnp.int32, (BLOCK, PAIR), 1)
    row = lax.broadcasted_iota(jnp.int32, (BLOCK, BLOCK), 0)
    col = lax.broadcasted_iota(jnp.int32, (BLOCK, BLOCK), 1)
    causal = col <= row
    q, do, fq = q_ref[...] * jnp.asarray(0.125, bf16), do_ref[...], fq_ref[...]
    both = do.astype(f32) * o_ref[...].astype(f32)
    zero = jnp.zeros_like(q)
    qt[...] = q.T
    dt[...] = do.T
    for head in range(2):
        inside = (lane < HEAD_DIM) if head == 0 else (lane >= HEAD_DIM)
        rows = slice(head * count, (head + 1) * count)
        qa[rows, :PAIR] = jnp.where(inside, q, zero)
        a, b, c = three_parts(-lse_ref[0][:, head : head + 1])
        qa[rows, PAIR:] = jnp.where(
            lane == KINDS, a, jnp.where(lane == KINDS + 1, b, jnp.where(lane == KINDS + 2, c, fq))
        )
        da[rows, :PAIR] = jnp.where(inside, do, zero)
        a, b, c = three_parts(-jnp.sum(jnp.where(inside, both, 0.0), 1, keepdims=True))
        da[rows, PAIR:] = jnp.where(lane == KINDS, a, jnp.where(lane == KINDS + 1, b, zero))
    ones = jnp.where((narrow == KINDS) | (narrow == KINDS + 1), 1.0, 0.0).astype(bf16)
    for j in range(count // BLOCK):
        start = j * BLOCK
        here, rest = slice(start, start + BLOCK), count - start
        k = k_ref[here, :]
        keys = jnp.concatenate([k, fk_ref[here, :]], 1)
        values = jnp.concatenate([v_ref[here, :], ones], 1)
        weights, slopes = [], []
        for head in range(2):
            rows = slice(head * count + start, (head + 1) * count)
            part = jnp.exp(product(qa[rows, :], keys, NT))
            near = jnp.where(causal, part[:BLOCK], 0.0)
            part = jnp.concatenate([near, part[BLOCK:]], 0) if rest > BLOCK else near
            slopes.append((part * product(da[rows, :], values, NT)).astype(bf16))
            weights.append(part.astype(bf16))
        queries = product(jnp.concatenate(slopes, 0), k * jnp.asarray(0.125, bf16), NN)
        queries = jnp.where(lane[:rest] < HEAD_DIM, queries[:rest], queries[rest:])
        if j == 0:
            dq[...] = queries
        else:
            dq[start:, :] += queries
        heads = [slice(0, HEAD_DIM), slice(HEAD_DIM, PAIR)]
        dv = [product(dt[head, start:], part, NN) for head, part in zip(heads, weights)]
        dk = [product(qt[head, start:], part, NN) for head, part in zip(heads, slopes)]
        dv_ref[here, :] = jnp.concatenate(dv, 0).T.astype(bf16)
        dk_ref[here, :] = jnp.concatenate(dk, 0).T.astype(bf16)
    dq_ref[...] = dq[...].astype(bf16)


def attention_backward(info, project, fq, fk, attended, attended_grad, lse, first, pairs, earlier):
    count, width = attended.shape
    total = width // PAIR

    def part(at):
        return pl.BlockSpec((count, PAIR), lambda h: (0, h + at + first))

    same = pl.BlockSpec((count, PAIR), lambda h: (0, 0))
    operands = (project, project, project, fq, fk, attended, attended_grad, lse, info)
    specs = [part(0), part(total), part(2 * total), same, same, part(0), part(0)]
    specs.append(pl.BlockSpec((1, count, 2), lambda h: (h + first, 0, 0)))
    specs.append(pl.BlockSpec(memory_space=pl.ANY))
    kernel, aliases = backward_kernel, {}
    if earlier is not None:
        aliases = {len(operands) + k: k for k in range(3)}
        specs += [pl.BlockSpec(memory_space=pl.ANY)] * 3
        kernel = lambda *refs: backward_kernel(*refs[: len(operands)], *refs[len(operands) + 3 :])
    return pl.pallas_call(
        kernel,
        grid=(pairs,),
        in_specs=specs,
        out_specs=[part(0)] * 3,
        out_shape=[jax.ShapeDtypeStruct((count, width), bf16)] * 3,
        scratch_shapes=[
            pltpu.VMEM((2 * count, 2 * PAIR), bf16),
            pltpu.VMEM((2 * count, 2 * PAIR), bf16),
            pltpu.VMEM((PAIR, count), bf16),
            pltpu.VMEM((PAIR, count), bf16),
            pltpu.VMEM((count, PAIR), f32),
        ],
        input_output_aliases=aliases,
        compiler_params=pltpu.CompilerParams(vmem_limit_bytes=24 * MIB),
        cost_estimate=SHORT,
        name="attention_backward",
    )(*operands, *(earlier or ()))


def halving_stages(group):
    stages = [(("dp", 0), ("dp", 0)), (("role", 0), ("dp", 1)), (("dp", 1), ("role", 0))]
    return stages + [(("dp", bit), ("dp", bit)) for bit in range(2, group.bit_length() - 1)]


def route_of(stage, roles, group):
    pairs = []
    for role in range(roles):
        for place in range(group):
            axis, bit = stage[place & 1]
            other = (role ^ (1 << bit), place) if axis == "role" else (role, place ^ (1 << bit))
            pairs.append((role * group + place, other[0] * group + other[1]))
    return pairs


def codes_of(stages):
    codes = []
    for other in (0, 1):
        place = {"role": lax.axis_index("role"), "dp": lax.axis_index("dp") ^ other}
        odd = place["dp"] & 1
        code = jnp.int32(0)
        for even_way, odd_way in stages[:STAGES]:
            bits = [(place[axis] >> bit) & 1 for axis, bit in (even_way, odd_way)]
            code = code * 2 + jnp.where(odd == 0, bits[0], bits[1])
        codes.append(code)
    return jnp.stack(codes)


def place_rows(acc, low, out_ref):
    rows = acc.shape[0] // SUB
    for j in range(SUB):
        at = pl.multiple_of((jnp.int32(j) ^ low) * rows, rows)
        out_ref[pl.ds(at, rows), :] = acc[j * rows : (j + 1) * rows]


def attn_weight_grad_kernel(
    half, info_ref, normed_ref, attended_ref, q_ref, k_ref, v_ref, o_ref, grad_ref, acc_ref
):
    panel = panel_in(half)(pl.program_id(0), info_ref)
    rights = (q_ref, k_ref, v_ref, o_ref)
    for k in range(4):

        @pl.when(panel == k)
        def _():
            left = attended_ref if k == 3 else normed_ref
            acc_ref[...] = product(left[...], rights[k][...], TN).astype(bf16)

    place_rows(acc_ref[...], info_ref[1 - half] & (SUB - 1), grad_ref)


def attn_weight_grad(info, half, normed, attended, rights):
    count, width = normed.shape
    whole = pl.BlockSpec(memory_space=pltpu.VMEM)
    return pl.pallas_call(
        partial(attn_weight_grad_kernel, half),
        grid_spec=pltpu.PrefetchScalarGridSpec(
            num_scalar_prefetch=1,
            grid=(2,),
            in_specs=[whole] * 6,
            out_specs=pl.BlockSpec((width, width), lambda i, c: (i, 0)),
            scratch_shapes=[pltpu.VMEM((width, width), bf16)],
        ),
        out_shape=jax.ShapeDtypeStruct((2 * width, width), bf16),
        compiler_params=pltpu.CompilerParams(vmem_limit_bytes=22 * MIB),
        cost_estimate=SHORT,
        name="attn_weight_grad",
    )(info, normed, attended, *rights)


def finish_kernel(halves, split, info_ref, *refs):
    pieces = refs[: 2 * len(halves)]
    step = pl.program_id(0)
    half = halves[0] + step // 2
    code = jnp.where(half == 0, info_ref[0], info_ref[1])
    low = code & (SUB - 1)
    rows = pieces[0].shape[1] // SUB

    def fill(out_ref, piece):
        for j in range(SUB):
            at = pl.multiple_of((jnp.int32(j) ^ low) * rows, rows)
            out_ref[j * rows : (j + 1) * rows, :] = piece[pl.ds(at, rows), :].astype(f32)

    if not split:
        for k, piece in enumerate(pieces):

            @pl.when(step == k)
            def _():
                fill(refs[-1], piece)

        return
    out_ref, far_ref, held_ref, sem = refs[-4:]
    source = (1 - step) ^ ((code >> LOW) & 1)
    last_half = code >> LOW + 1 == 1
    copy = pltpu.make_async_copy(held_ref, far_ref, sem)
    for k, piece in enumerate(pieces):

        @pl.when((source == k) & (last_half & (step == 0)))
        def _():
            fill(held_ref, piece)
            copy.start()

        @pl.when((source == k) & jnp.logical_not(last_half & (step == 0)))
        def _():
            fill(out_ref, piece)

    @pl.when(last_half & (step == 1))
    def _():
        copy.wait()


def finish(info, pieces, layout, name, halves=(0, 1), earlier=()):
    width = pieces[0].shape[1]
    block = (width, width)
    split = layout == "attn"

    def panel(i, c):
        code = jnp.where(halves[0] + i // 2 == 0, c[0], c[1])
        if split:
            return 2 * (code >> LOW + 1) + 1 - i
        return (i & 1) ^ (code >> LOW)

    out_specs, scratch = [], []
    if layout == "tall":
        shapes = [(4 * width, width)]
        out_specs = [pl.BlockSpec(block, lambda i, c: (panel(i, c), 0))]
    elif layout == "wide":
        shapes = [(width, 4 * width)]
        out_specs = [pl.BlockSpec(block, lambda i, c: (0, panel(i, c)))]
    else:
        shapes = [(width, 3 * width), (width, width)]
        out_specs = [pl.BlockSpec(block, lambda i, c: (0, jnp.minimum(panel(i, c), 2)))]
        out_specs += [pl.BlockSpec(memory_space=pl.ANY)]
        scratch = [pltpu.VMEM(block, f32), pltpu.SemaphoreType.DMA]
    in_specs = [pl.BlockSpec(memory_space=pltpu.VMEM)] * len(pieces)
    in_specs += [pl.BlockSpec(memory_space=pl.ANY)] * len(earlier)
    return pl.pallas_call(
        partial(finish_kernel, halves, split),
        grid_spec=pltpu.PrefetchScalarGridSpec(
            num_scalar_prefetch=1,
            grid=(len(pieces),),
            in_specs=in_specs,
            out_specs=out_specs,
            scratch_shapes=scratch,
        ),
        out_shape=[jax.ShapeDtypeStruct(shape, f32) for shape in shapes],
        input_output_aliases={3: 0, 4: 1} if earlier else {},
        compiler_params=pltpu.CompilerParams(vmem_limit_bytes=24 * MIB),
        cost_estimate=SHORT,
        name=name,
    )(info, *pieces, *earlier)


def packed(small):
    high = lax.reduce_precision(small, exponent_bits=8, mantissa_bits=7)
    rows = jnp.concatenate([high, small - high], 0).astype(bf16)
    return jnp.pad(rows, ((0, 16 - rows.shape[0]), (0, 0)))


def unpacked(rows, count):
    return rows[:count].astype(f32) + rows[count : 2 * count].astype(f32)


class RowSum:
    def __init__(self, send, routes, stages=STAGES):
        self.send, self.keep, self.got = [send], None, None
        self.pieces, self.small = [], None
        self.steps = [("halve", route) for route in routes[: stages - 1]]
        self.steps += [("last", routes[stages - 1])]
        self.steps += [("whole", route) for route in routes[stages:]]
        self.steps += [("join", route) for route in routes[stages - 1 : 1 : -1]]
        self.steps += [("far", routes[1]), ("core", routes[0])]

    def launch(self):
        self.got = [lax.ppermute(part, AXES, self.steps[0][1]) for part in self.send]

    def with_small(self):
        if self.small is None:
            return [self.keep]
        return [jnp.concatenate([self.keep, packed(self.small)], 0)]

    def add_small(self, rows):
        if self.small is not None:
            self.small = self.small + unpacked(rows, self.small.shape[0])

    def take(self, got):
        kind = self.steps.pop(0)[0]
        if kind == "halve":
            half = self.keep.shape[0] // 2
            self.send = [self.keep[half:] + got[0][half:]]
            self.keep = self.keep[:half] + got[0][:half]
        elif kind in ("last", "whole", "join"):
            count = self.keep.shape[0]
            if kind != "last":
                self.add_small(got[0][count:])
            if kind == "join":
                self.keep = jnp.concatenate([self.keep, got[0][:count]], axis=0)
            else:
                self.keep = self.keep + got[0][:count]
            self.send = self.with_small()
        elif kind == "far":
            self.add_small(got[0][self.keep.shape[0] :])
            self.pieces = [self.keep, got[0]]
            self.send = list(self.pieces)
            if self.small is not None:
                self.send.append(self.small)
        else:
            self.pieces += got[:2]
            self.send = []


def lanes_of(rows, width):
    return lax.broadcasted_iota(jnp.int32, (rows, width), 1)


def live_rows(info_ref, start, rows):
    place = start + lax.broadcasted_iota(jnp.int32, (rows, 1), 0)
    return place, place < info_ref[TOTAL]


def decompressed(values, lane, last):
    return jnp.where(lane == last, -jnp.sum(values, axis=1, keepdims=True), values)


def enter_kernel(
    info_ref,
    x_ref,
    cot_ref,
    gain_ref,
    w_ref,
    inputs_ref,
    normed_ref,
    project_ref,
    bg_ref,
    fq_ref,
    fk_ref,
    energy_ref,
):
    step = pl.program_id(0)
    rows, width = x_ref.shape
    last = width - 1
    lane = lanes_of(rows, width)
    place, live = live_rows(info_ref, step * rows, rows)
    x = jnp.where(lane < last, x_ref[...].astype(f32), 0.0)
    inputs_ref[...] = x.astype(bf16)
    full = decompressed(x, lane, last)
    square = jnp.sum(full * full, axis=1, keepdims=True)
    normed = (full * lax.rsqrt(square * (1.0 / width) + EPS) * gain_ref[:1, :]).astype(bf16)
    normed_ref[...] = normed
    project_ref[...] = product(normed, w_ref[...], NN).astype(bf16)
    cot = jnp.where((lane < last) & live, cot_ref[...].astype(f32), 0.0)
    bg_ref[...] = (cot - jnp.sum(cot, axis=1, keepdims=True) * (1.0 / width)).astype(bf16)
    segment = jnp.zeros_like(place)
    for k in range(ROWMAX):
        segment += (place >= info_ref[ENDS + k]).astype(jnp.int32)
    narrow = lanes_of(rows, PAIR)
    hot = narrow == segment
    fq_ref[...] = jnp.where(hot, 1.0, 0.0).astype(bf16)
    ones = jnp.where(narrow < KINDS + 3, 1.0, 0.0)
    fk_ref[...] = jnp.where(narrow < KINDS, jnp.where(hot, 0.0, NEG), ones).astype(bf16)

    @pl.when(step == 0)
    def _():
        energy_ref[...] = jnp.zeros_like(energy_ref)

    energy_ref[...] += jnp.sum(jnp.where(live, square, 0.0), keepdims=True)


def enter(info, stream, cotangent, gain, w_qkv):
    count, width = stream.shape[0], w_qkv.shape[0]
    rows = min(BLOCK, count)

    def some(columns):
        return pl.BlockSpec((rows, columns), lambda i, c: (i, 0))

    def whole(shape):
        return pl.BlockSpec(shape, lambda i, c: (0, 0), pipeline_mode=pl.Buffered(1))

    return pl.pallas_call(
        enter_kernel,
        grid_spec=pltpu.PrefetchScalarGridSpec(
            num_scalar_prefetch=1,
            grid=(count // rows,),
            in_specs=[some(width), some(width), whole((2, width)), whole(w_qkv.shape)],
            out_specs=[some(width), some(width), some(3 * width), some(width), some(PAIR), some(PAIR)]
            + [pl.BlockSpec((8, PAIR), lambda i, c: (0, 0))],
        ),
        out_shape=[
            jax.ShapeDtypeStruct((count, width), bf16),
            jax.ShapeDtypeStruct((count, width), bf16),
            jax.ShapeDtypeStruct((count, 3 * width), bf16),
            jax.ShapeDtypeStruct((count, width), bf16),
            jax.ShapeDtypeStruct((count, PAIR), bf16),
            jax.ShapeDtypeStruct((count, PAIR), bf16),
            jax.ShapeDtypeStruct((8, PAIR), f32),
        ],
        compiler_params=pltpu.CompilerParams(vmem_limit_bytes=18 * MIB),
        cost_estimate=SHORT,
        name="enter",
    )(info, *far(stream, cotangent), gain, *far(w_qkv))


def middle_rows(info_ref, attended_ref, w_out_ref, x_ref, gain_ref, middle_ref, normed_ref, energy_ref):
    count, width = attended_ref.shape
    last = width - 1
    rows = min(BLOCK, count)
    lane = lanes_of(rows, width)
    energy_ref[...] = jnp.zeros_like(energy_ref)

    @pl.loop(0, count // rows)
    def _(block):
        start = pl.multiple_of(block * rows, rows)
        here = pl.ds(start, rows)
        branch = product(attended_ref[here, :], w_out_ref[...], NN)
        mean = jnp.sum(branch, axis=1, keepdims=True) * (1.0 / width)
        middle = (x_ref[here, :].astype(f32) + branch - mean).astype(bf16)
        middle = jnp.where(lane < last, middle, jnp.zeros_like(middle))
        middle_ref[here, :] = middle
        full = decompressed(middle.astype(f32), lane, last)
        square = jnp.sum(full * full, axis=1, keepdims=True)
        scaled = full * lax.rsqrt(square * (1.0 / width) + EPS) * gain_ref[1:, :]
        normed_ref[here, :] = scaled.astype(bf16)
        _, live = live_rows(info_ref, start, rows)
        energy_ref[...] += jnp.sum(jnp.where(live, square, 0.0), keepdims=True)


def up_rows(normed_ref, w_up_ref, bg_ref, active_ref, slope_ref, grad_ref, low):
    count = normed_ref.shape[0]
    rows = min(BLOCK, count)

    def hidden_of(block):
        return product(normed_ref[block * rows : (block + 1) * rows, :], w_up_ref[...], NN)

    ahead = hidden_of(0)
    for block in range(count // rows):
        here = slice(block * rows, (block + 1) * rows)
        hidden = ahead
        if block + 1 < count // rows:
            ahead = hidden_of(block + 1)
        square = hidden * hidden
        gate = 0.5 + 0.5 * jnp.tanh(hidden * (SQRT_2_PI + (SQRT_2_PI * 0.044715) * square))
        active = hidden * gate
        active_ref[here, :] = active.astype(bf16)
        inner = (1.0 - gate) * (2.0 * SQRT_2_PI + (6.0 * SQRT_2_PI * 0.044715) * square)
        slope_ref[here, :] = (gate + active * inner).astype(bf16)
    place_rows(product(active_ref[...], bg_ref[...], TN).astype(bf16), low, grad_ref)


def first_up_kernel(
    info_ref,
    attended_ref,
    w_out_ref,
    x_ref,
    gain_ref,
    w_up_ref,
    bg_ref,
    middle_ref,
    normed_ref,
    energy_ref,
    active_ref,
    slope_ref,
    grad_ref,
):
    @pl.when(pl.program_id(0) == 0)
    def _():
        middle_rows(
            info_ref, attended_ref, w_out_ref, x_ref, gain_ref, middle_ref, normed_ref, energy_ref
        )

    up_rows(normed_ref, w_up_ref, bg_ref, active_ref, slope_ref, grad_ref, info_ref[1] & (SUB - 1))


def second_up_kernel(
    info_ref, normed_ref, w_up_ref, bg_ref, _, __, active_ref, slope_ref, grad_ref
):
    up_rows(normed_ref, w_up_ref, bg_ref, active_ref, slope_ref, grad_ref, info_ref[0] & (SUB - 1))


def panel_in(half):
    return lambda i, c: i ^ (c[1 - half] >> LOW)


def up_and_grad_down(info, half, attended, w_out, stream, gain, w_up, bg, first=None):
    count, width = bg.shape
    panel = panel_in(half)
    whole = pl.BlockSpec(memory_space=pltpu.VMEM)
    stays = pl.BlockSpec(memory_space=pltpu.VMEM)
    wide = pl.BlockSpec((count, width), lambda i, c: (0, panel(i, c)))
    w_up_spec = pl.BlockSpec((width, width), lambda i, c: (0, panel(i, c)))
    out_specs = [wide, wide, pl.BlockSpec((width, width), lambda i, c: (i, 0))]
    out_shape = [pltpu.HBM((count, 4 * width), bf16)] * 2
    out_shape += [jax.ShapeDtypeStruct((2 * width, width), bf16)]
    if half == 0:
        kernel, aliases = first_up_kernel, {}
        in_specs = [
            whole,
            whole,
            whole,
            pl.BlockSpec((2, width), lambda i, c: (0, 0)),
            w_up_spec,
            whole,
        ]
        operands = (attended, w_out, stream, gain, *far(w_up), bg)
        out_specs = [stays, stays, pl.BlockSpec((8, PAIR), lambda i, c: (0, 0))] + out_specs
        out_shape = [
            jax.ShapeDtypeStruct((count, width), bf16),
            jax.ShapeDtypeStruct((count, width), bf16),
            jax.ShapeDtypeStruct((8, PAIR), f32),
        ] + out_shape
    else:
        kernel, aliases = second_up_kernel, {4: 0, 5: 1}
        in_specs = [whole, w_up_spec, whole] + [pl.BlockSpec(memory_space=pl.ANY)] * 2
        operands = (attended, *far(w_up), bg, *far(*first))
    return pl.pallas_call(
        kernel,
        grid_spec=pltpu.PrefetchScalarGridSpec(
            num_scalar_prefetch=1, grid=(2,), in_specs=in_specs, out_specs=out_specs
        ),
        out_shape=out_shape,
        input_output_aliases=aliases,
        compiler_params=pltpu.CompilerParams(vmem_limit_bytes=34 * MIB),
        cost_estimate=SHORT,
        name="up_and_grad_down",
    )(info, *operands)


def hidden_grad_kernel(half, info_ref, bg_ref, w_down_ref, slope_ref, normed_ref, *refs):
    hg_ref, grad_ref = refs[-2:]
    count = bg_ref.shape[0]
    rows = min(BLOCK, count)
    for block in range(count // rows):
        here = slice(block * rows, (block + 1) * rows)
        grad = product(bg_ref[here, :], w_down_ref[...], NT)
        hg_ref[here, :] = (grad * slope_ref[here, :].astype(f32)).astype(bf16)
    acc = product(normed_ref[...], hg_ref[...], TN).astype(bf16)
    place_rows(acc, info_ref[1 - half] & (SUB - 1), grad_ref)


def hidden_grad_and_grad_up(info, half, bg, w_down, slope, normed, first=None):
    count, width = bg.shape
    panel = panel_in(half)
    whole = pl.BlockSpec(memory_space=pltpu.VMEM)
    wide = pl.BlockSpec((count, width), lambda i, c: (0, panel(i, c)))
    in_specs = [whole, pl.BlockSpec((width, width), lambda i, c: (panel(i, c), 0)), wide, whole]
    operands = [bg, *far(w_down, slope), normed]
    if half:
        in_specs += [pl.BlockSpec(memory_space=pl.ANY)]
        operands += far(first)
    return pl.pallas_call(
        partial(hidden_grad_kernel, half),
        grid_spec=pltpu.PrefetchScalarGridSpec(
            num_scalar_prefetch=1,
            grid=(2,),
            in_specs=in_specs,
            out_specs=[wide, pl.BlockSpec((width, width), lambda i, c: (i, 0))],
        ),
        out_shape=[
            pltpu.HBM((count, 4 * width), bf16),
            jax.ShapeDtypeStruct((2 * width, width), bf16),
        ],
        input_output_aliases={5: 0} if half else {},
        compiler_params=pltpu.CompilerParams(vmem_limit_bytes=24 * MIB),
        cost_estimate=SHORT,
        name="hidden_grad_and_grad_up",
    )(info, *operands)


def norm_back(dz, values, gain, lane, last):
    width = last + 1
    full = decompressed(values, lane, last)
    scale = lax.rsqrt(jnp.sum(full * full, axis=1, keepdims=True) * (1.0 / width) + EPS)
    normal = full * scale
    gain_rows = jnp.sum((dz * normal).reshape(dz.shape[0] // 8, 8, width), axis=0)
    pulled = gain * dz
    inner = jnp.sum(normal * pulled, axis=1, keepdims=True) * (1.0 / width)
    grad = scale * (pulled - normal * inner)
    return grad - jnp.sum(jnp.where(lane == last, grad, 0.0), axis=1, keepdims=True), gain_rows


def middle_grad_kernel(
    info_ref,
    hg_ref,
    w_up_ref,
    middle_ref,
    gain_ref,
    cot_ref,
    w_out_ref,
    grad_ref,
    bag_ref,
    ag_ref,
    gains_ref,
    dz_ref,
):
    step = pl.program_id(0)
    rows, width = middle_ref.shape
    last = width - 1

    @pl.when(step == 0)
    def _():
        dz_ref[...] = product(hg_ref[...], w_up_ref[...], NT)
        gains_ref[...] = jnp.zeros_like(gains_ref)

    @pl.when((step > 0) & (step < 4))
    def _():
        dz_ref[...] += product(hg_ref[...], w_up_ref[...], NT)

    @pl.when(step >= 4)
    def _():
        lane = lanes_of(rows, width)
        start = pl.multiple_of((step - 4) * rows, rows)
        _, live = live_rows(info_ref, start, rows)
        dz = dz_ref[pl.ds(start, rows), :]
        pulled, gain_rows = norm_back(dz, middle_ref[...].astype(f32), gain_ref[1:, :], lane, last)
        cot = jnp.where(live, cot_ref[...].astype(f32), 0.0)
        grad = jnp.where(lane < last, cot + pulled, 0.0).astype(bf16)
        grad_ref[...] = grad
        grad = grad.astype(f32)
        bag = (grad - jnp.sum(grad, axis=1, keepdims=True) * (1.0 / width)).astype(bf16)
        bag_ref[...] = bag
        ag_ref[...] = product(bag, w_out_ref[...], NT).astype(bf16)
        gains_ref[...] += gain_rows


def middle_grad(info, hg, w_up, middle, gain, cotangent, w_out):
    count, width = middle.shape
    rows = min(BLOCK, count)

    def some(columns):
        return pl.BlockSpec((rows, columns), lambda i, c: (jnp.maximum(i - 4, 0), 0))

    def panel(height):
        return pl.BlockSpec((height, width), lambda i, c: (0, jnp.minimum(i, 3)))

    def whole(shape):
        return pl.BlockSpec(shape, lambda i, c: (0, 0), pipeline_mode=pl.Buffered(1))

    return pl.pallas_call(
        middle_grad_kernel,
        grid_spec=pltpu.PrefetchScalarGridSpec(
            num_scalar_prefetch=1,
            grid=(4 + count // rows,),
            in_specs=[
                panel(count),
                panel(width),
                some(width),
                whole((2, width)),
                some(width),
                whole(w_out.shape),
            ],
            out_specs=[some(width)] * 3 + [pl.BlockSpec((8, width), lambda i, c: (0, 0))],
            scratch_shapes=[pltpu.VMEM((count, width), f32)],
        ),
        out_shape=[jax.ShapeDtypeStruct((count, width), bf16)] * 3
        + [jax.ShapeDtypeStruct((8, width), f32)],
        compiler_params=pltpu.CompilerParams(vmem_limit_bytes=24 * MIB),
        cost_estimate=SHORT,
        name="middle_grad",
    )(info, *far(hg, w_up), middle, gain, *far(cotangent), w_out)


def leave_kernel(first, info_ref, active_ref, w_down_ref, middle_ref, *refs):
    out_ref, energy_ref = refs[-2:]
    step = pl.program_id(0)
    rows, width = middle_ref.shape
    last = width - 1
    lane = lanes_of(rows, width)
    _, live = live_rows(info_ref, (first + step) * rows, rows)
    branch = product(active_ref[...], w_down_ref[...], NN)
    mean = jnp.sum(branch, axis=1, keepdims=True) * (1.0 / width)
    out = (middle_ref[...].astype(f32) + branch - mean).astype(bf16)
    out_ref[...] = out
    values = jnp.where(lane < last, out.astype(f32), 0.0)
    full = decompressed(values, lane, last)
    square = jnp.sum(full * full, axis=1, keepdims=True)

    @pl.when(step == 0)
    def _():
        energy_ref[...] = jnp.zeros_like(energy_ref)

    energy_ref[...] += jnp.sum(jnp.where(live, square, 0.0), keepdims=True)


def leave(info, active, w_down, middle, part, parts, earlier=None):
    count, width = middle.shape
    rows = min(BLOCK, count // parts)
    steps = count // parts // rows
    first = part * steps

    def some(columns):
        return pl.BlockSpec((rows, columns), lambda i, c: (i + first, 0))

    def whole(shape):
        return pl.BlockSpec(shape, lambda i, c: (0, 0), pipeline_mode=pl.Buffered(1))

    in_specs = [some(active.shape[1]), whole(w_down.shape), some(width)]
    operands = [*far(active, w_down), middle]
    if part:
        in_specs += [pl.BlockSpec(memory_space=pl.ANY)]
        operands += [earlier]
    return pl.pallas_call(
        partial(leave_kernel, first),
        grid_spec=pltpu.PrefetchScalarGridSpec(
            num_scalar_prefetch=1,
            grid=(steps,),
            in_specs=in_specs,
            out_specs=[some(width), pl.BlockSpec((8, PAIR), lambda i, c: (0, 0))],
        ),
        out_shape=[
            jax.ShapeDtypeStruct((count, width - 1), bf16),
            jax.ShapeDtypeStruct((8, PAIR), f32),
        ],
        input_output_aliases={4: 0} if part else {},
        compiler_params=pltpu.CompilerParams(vmem_limit_bytes=20 * MIB),
        cost_estimate=SHORT,
        name="leave",
    )(info, *operands)


def stream_grad_kernel(
    info_ref, dq_ref, dk_ref, dv_ref, w_ref, x_ref, gain_ref, middle_grad_ref, out_ref, gains_ref
):
    step = pl.program_id(0)
    rows, width = x_ref.shape
    last = width - 1
    lane = lanes_of(rows, width)
    dz = product(dq_ref[...], w_ref[:, :width], NT)
    dz += product(dk_ref[...], w_ref[:, width : 2 * width], NT)
    dz += product(dv_ref[...], w_ref[:, 2 * width :], NT)
    x = jnp.where(lane < last, x_ref[...].astype(f32), 0.0)
    pulled, gain_rows = norm_back(dz, x, gain_ref[:1, :], lane, last)
    out_ref[...] = (middle_grad_ref[...].astype(f32) + pulled).astype(bf16)

    @pl.when(step == 0)
    def _():
        gains_ref[...] = jnp.zeros_like(gains_ref)

    gains_ref[...] += gain_rows


def stream_gradient(info, parts, w_qkv, stream, gain, middle_grads):
    count, width = middle_grads.shape
    rows = min(BLOCK, count)

    def some(columns):
        return pl.BlockSpec((rows, columns), lambda i, c: (i, 0))

    def whole(shape):
        return pl.BlockSpec(shape, lambda i, c: (0, 0), pipeline_mode=pl.Buffered(1))

    return pl.pallas_call(
        stream_grad_kernel,
        grid_spec=pltpu.PrefetchScalarGridSpec(
            num_scalar_prefetch=1,
            grid=(count // rows,),
            in_specs=[some(width)] * 3
            + [whole(w_qkv.shape), some(width), whole((2, width)), some(width)],
            out_specs=[some(width), whole((8, width))],
        ),
        out_shape=[
            jax.ShapeDtypeStruct((count, width - 1), bf16),
            jax.ShapeDtypeStruct((8, width), f32),
        ],
        compiler_params=pltpu.CompilerParams(vmem_limit_bytes=20 * MIB),
        cost_estimate=SHORT,
        name="stream_grad",
    )(info, *parts, *far(w_qkv), stream, gain, middle_grads)


D, U, A = range(3)
(
    UP_1,
    UP_2,
    HIDDEN_1,
    HIDDEN_2,
    MIDDLE,
    BACK,
    GRADS_1,
    GRADS_2,
    STREAM,
    LEAVE_1,
    LEAVE_2,
    PREP,
    VECTORS,
    DOWN_ROWS,
    UP_ROWS,
    ATTN_ROWS_1,
    ATTN_ROWS_2,
) = range(17)
D_GO, D_IN, U_GO, U_IN, A_GO, A_IN = range(17, 23)
EXCHANGES = {
    D_GO: (D, True),
    D_IN: (D, False),
    U_GO: (U, True),
    U_IN: (U, False),
    A_GO: (A, True),
    A_IN: (A, False),
}
ORDER = (
    UP_1, D_GO, UP_2, D_IN, HIDDEN_1, D_GO, U_GO, HIDDEN_2, U_IN, U_GO, MIDDLE, D_IN, D_GO, BACK, D_IN,
    U_IN, D_GO, U_GO, BACK, D_IN, U_IN, D_GO, U_GO, BACK, D_IN, U_IN, D_GO, U_GO, GRADS_1, A_GO, GRADS_2,
    A_IN, A_GO, STREAM, D_IN, U_IN, A_IN, A_GO, D_GO, U_GO, LEAVE_1, A_IN, D_IN, U_IN, A_GO, D_GO, U_GO,
    LEAVE_2, A_IN, D_IN, A_GO, D_GO, PREP, A_IN, U_IN, A_GO, U_GO, A_IN, D_IN, U_IN, A_GO, D_GO, U_GO,
    D_IN, DOWN_ROWS, A_IN, A_GO, A_IN, U_IN, A_GO, U_GO, U_IN, UP_ROWS, A_IN, A_GO, ATTN_ROWS_1, VECTORS,
    A_IN, ATTN_ROWS_2,
)


class Held:
    pass


def body(stream, cotangent, w_qkv, w_out, w_up, w_down, gain_attn, gain_mlp, doc_lengths):
    width = w_out.shape[0]
    roles, group = lax.axis_size("role"), lax.axis_size("dp")
    stages = halving_stages(group)
    routes = [route_of(stage, roles, group) for stage in stages]
    place = lax.axis_index("role") * group + lax.axis_index("dp")
    lengths = lax.dynamic_slice_in_dim(doc_lengths, place, 1, 0)[0]
    ends = jnp.cumsum(lengths)
    info = jnp.concatenate([codes_of(stages), ends]).astype(jnp.int32)
    gains = jnp.stack([gain_attn, gain_mlp])
    sums, has = [None] * 3, Held()
    has.output, has.leaving = None, {}

    inputs, normed, project, branch_grad, fq, fk, energy_in = enter(
        info, stream, cotangent, gains, w_qkv
    )
    attended, lse = attention_forward(project, fq, fk)

    def up_first(info):
        has.middle, has.normed, has.energy, *has.wide, half = up_and_grad_down(
            info, 0, attended, w_out, inputs, gains, w_up, branch_grad
        )
        sums[D] = RowSum(half, routes)
        return "normed"

    def up_second(info):
        active, has.slope, sums[D].keep = up_and_grad_down(
            info, 1, has.normed, None, None, None, w_up, branch_grad, has.wide
        )
        has.active = active
        return "slope"

    def hidden_first(info):
        has.hidden, half = hidden_grad_and_grad_up(
            info, 0, branch_grad, w_down, has.slope, has.normed
        )
        sums[U] = RowSum(half, routes)
        return "hidden"

    def hidden_second(info):
        has.hidden, sums[U].keep = hidden_grad_and_grad_up(
            info, 1, branch_grad, w_down, has.slope, has.normed, has.hidden
        )
        return "hidden"

    def middle_back(info):
        has.grads, has.attn_grad, has.attended_grad, has.gains = middle_grad(
            info, has.hidden, w_up, has.middle, gains, cotangent, w_out
        )
        has.calls, has.parts = 0, None
        return "attended_grad"

    def attention_back(info):
        has.parts = attention_backward(
            info,
            project,
            fq,
            fk,
            attended,
            has.attended_grad,
            lse,
            has.calls,
            2,
            has.parts,
        )
        has.calls += 2
        return "parts"

    def attn_first(info):
        rights = (*has.parts, has.attn_grad)
        half = attn_weight_grad(info, 0, normed, attended, rights)
        sums[A] = RowSum(half, routes)
        has.half = half
        return "half"

    def attn_second(info):
        rights = (*has.parts, has.attn_grad)
        has.half = sums[A].keep = attn_weight_grad(info, 1, normed, attended, rights)
        return "half"

    def stream_back(info):
        has.stream_grad, has.gains_attn = stream_gradient(
            info, has.parts, w_qkv, inputs, gains, has.grads
        )
        return "stream_grad"

    def leave_part(part):
        def call(info):
            has.output, has.leaving[part] = leave(
                info, has.active, w_down, has.middle, part, 2, has.output
            )
            return "output"

        return call

    def small_sums(info):
        energies = [energy_in, has.energy, has.leaving[0] + has.leaving[1]]
        energies = jnp.concatenate([each[:1] for each in energies], 1)
        energies = jnp.pad(energies, ((0, 0), (0, width - 3 * PAIR)))
        rows = [jnp.sum(each, 0, keepdims=True) for each in (has.gains_attn, has.gains)]
        small = jnp.concatenate([*rows, energies], 0)
        has.small, has.live = lax.optimization_barrier((small, jnp.sum(doc_lengths).astype(f32)))
        return "small"

    def vectors(info):
        small = sums[A].small + sums[A].got[2]
        has.vectors = (small[0], small[1], jnp.sqrt(small[2, : 3 * PAIR : PAIR] / (width * has.live)))
        return "vectors"

    def rows_of(name, tall):
        def call(info):
            pieces = sums[name].pieces
            (rows,) = finish(info, pieces, "tall" if tall else "wide", "weight_rows")
            setattr(has, "down" if tall else "up", rows)
            return "down" if tall else "up"

        return call

    def attn_rows_first(info):
        has.rows = finish(info, sums[A].pieces[:2], "attn", "weight_rows", (0,))
        return "rows"

    def attn_rows_second(info):
        has.rows = finish(info, sums[A].pieces[2:], "attn", "weight_rows", (1,), has.rows)
        return "rows"

    kernels = {
        UP_1: up_first,
        UP_2: up_second,
        HIDDEN_1: hidden_first,
        HIDDEN_2: hidden_second,
        MIDDLE: middle_back,
        BACK: attention_back,
        GRADS_1: attn_first,
        GRADS_2: attn_second,
        STREAM: stream_back,
        LEAVE_1: leave_part(0),
        LEAVE_2: leave_part(1),
        PREP: small_sums,
        VECTORS: vectors,
        DOWN_ROWS: rows_of(D, True),
        UP_ROWS: rows_of(U, False),
        ATTN_ROWS_1: attn_rows_first,
        ATTN_ROWS_2: attn_rows_second,
    }
    complete = {DOWN_ROWS: D, UP_ROWS: U, ATTN_ROWS_2: A}
    token = info

    def exchange(name, launch, token):
        each = sums[name]
        if launch and each.got is None and each.steps:
            each.send, token = lax.optimization_barrier((each.send, token))
            with jax.named_scope("exchange_%s_%d" % ("DUA"[name], len(each.steps))):
                each.launch()
        elif not launch and each.got is not None:
            got, token = lax.optimization_barrier((each.got, token))
            each.got = None
            each.take(got)
        return token

    def finished(name, token):
        while sums[name].steps:
            token = exchange(name, True, token)
            token = exchange(name, False, token)
        return token

    for event in ORDER:
        if event in EXCHANGES:
            token = exchange(*EXCHANGES[event], token)
            continue
        if event in complete:
            token = finished(complete[event], token)
        if event == ATTN_ROWS_1:
            while not sums[A].pieces:
                token = exchange(A, True, token)
                token = exchange(A, False, token)
            token = exchange(A, True, token)
        key = kernels[event](token)
        held, token = lax.optimization_barrier((getattr(has, key), token))
        setattr(has, key, held)
        if event == PREP:
            sums[A].small = has.small
    return (has.output, has.stream_grad, *has.rows, has.up, has.down, *has.vectors)


def solution(mesh):
    rows = P(("role", "dp"), None)
    return jax.shard_map(
        body,
        mesh=mesh,
        in_specs=(rows, rows) + (P(),) * 7,
        out_specs=(rows, rows) + (P(),) * 7,
        check_vma=False,
    )
```
